32 devices in a mesh: dp: 8 (over z, y), seq: 4 (over x, core).
Axes of the slice: x: 2, y: 2, z: 4, core: 2. Of those that a mesh axis runs over, the one named last changes fastest.
Arguments:
- inputs: bfloat16 [8, 1024, 768], P('dp', 'seq'), may hold values from -6 to 6
- attn_gain: float32 [768], P('dp'), may hold values from 0.5 to 1.5
- qkv_weight: float32 [768, 12, 3, 64], P('dp'), may hold values from -0.21875 to 0.21875
- out_weight: float32 [768, 768], P('dp'), may hold values from -3.5 to 3.5
- ffn_gain: float32 [768], P('dp'), may hold values from 0.5 to 1.5
- router_weight: float32 [768, 3], P('dp'), may hold values from -0.15625 to 0.15625
- expert_in: float32 [3, 768, 4096], P(None, 'dp'), may hold values from -0.21875 to 0.21875
- expert_out: float32 [3, 2048, 768], P(None, 'dp'), may hold values from -0.5 to 0.5
- shared_in: float32 [768, 4096], P('dp'), may hold values from -0.21875 to 0.21875
- shared_out: float32 [2048, 768], P('dp'), may hold values from -0.25 to 0.25
- routes: int32 [8, 1024, 2], P('dp', 'seq'), may hold values from 0 to 2, as said below
- slot_index: int32 [8, 1024, 2], P('dp', 'seq'), may hold values from 0 to 191, as said below
- cotangent: bfloat16 [8, 1024, 768], P('dp', 'seq'), may hold values from -6 to 6
Outputs:
- output: bfloat16 [8, 1024, 768], P('dp', 'seq')
- input_grad: float32 [8, 1024, 768], P('dp', 'seq')
- attn_gain_grad: float32 [768], P('dp')
- qkv_weight_grad: float32 [768, 12, 3, 64], P('dp')
- out_weight_grad: float32 [768, 768], P('dp')
- ffn_gain_grad: float32 [768], P('dp')
- router_weight_grad: float32 [768, 3], P('dp')
- expert_in_grad: float32 [3, 768, 4096], P(None, 'dp')
- expert_out_grad: float32 [3, 2048, 768], P(None, 'dp')
- shared_in_grad: float32 [768, 4096], P('dp')
- shared_out_grad: float32 [2048, 768], P('dp')
The draws below stay inside these ranges and needn't reach their ends.
Inputs may be any that keep to these rules, and one draw needn't show every extreme that they name: `routes`: A token's 2 experts differ. Within the tokens of one device (aligned blocks of 256 tokens of a sequence), no expert is named more than 192 times, one expert exactly 192 times, and every expert at least once. `slot_index`: within the tokens of one device, the slots of an expert named n times are 0 to n - 1, each once.
All inputs are finite; a program needn't handle non-finite values.
Results may differ from the reference program's by a relative error of at most 0.02.
The reference program's roundings to bfloat16 on the way count: a program that leaves them out, or rounds other values in their place, can miss the bound.
Values may be sent and summed in bfloat16 or wider, within the bound.
A program may use at most 160 MiB of HBM per device.

```python
import jax
import jax.numpy as jnp
from jax import lax

D = 768
HEADS = 12
HEAD_DIM = 64
FF = 2048
EXPERTS = 3
TOP = 2
ATT_BLOCK = 256
TOK_DEV = 256
SEQS = 8
LEN = 1024
CAP = 192
N_SEQ = 4


def route_block(block_key, block_rows, capacity, expert_count):
    load_key, order_key, flip_key, row_key = jax.random.split(block_key, 4)
    load_keys = jax.random.split(load_key, expert_count)
    load_list = [jnp.asarray(capacity, jnp.int32)]
    remaining = jnp.asarray(TOP * block_rows - capacity, jnp.int32)
    for number in range(1, expert_count - 1):
        others = expert_count - number - 1
        lowest = jnp.maximum(1, remaining - others * capacity)
        highest = jnp.minimum(capacity, remaining - others)
        chosen = jax.random.randint(load_keys[number], (), lowest, highest + 1, dtype=jnp.int32)
        load_list.append(chosen)
        remaining = remaining - chosen
    load_list.append(remaining)
    load_array = jnp.stack(load_list).astype(jnp.int32)
    run_ends = jnp.cumsum(load_array)
    run_starts = run_ends - load_array
    positions = jnp.arange(TOP * block_rows, dtype=jnp.int32)
    run_label = jnp.sum((positions[:, None] >= run_ends[None, :]).astype(jnp.int32), axis=1)
    slot_of = positions - run_starts[run_label]
    expert_order = jax.random.permutation(order_key, expert_count).astype(jnp.int32)
    expert_of = expert_order[run_label]
    pair_expert = expert_of.reshape(TOP, block_rows).T
    pair_slot = slot_of.reshape(TOP, block_rows).T
    column_shift = jax.random.randint(flip_key, (block_rows,), 0, TOP, dtype=jnp.int32)
    columns = (jnp.arange(TOP, dtype=jnp.int32)[None, :] + column_shift[:, None]) % TOP
    pair_expert = jnp.take_along_axis(pair_expert, columns, axis=1)
    pair_slot = jnp.take_along_axis(pair_slot, columns, axis=1)
    shuffle = jax.random.permutation(row_key, block_rows)
    return (pair_expert[shuffle], pair_slot[shuffle])


def draw_both(key):
    base_key = jax.random.fold_in(key, 1234)
    block_count = SEQS * LEN // TOK_DEV
    block_keys = jax.random.split(base_key, block_count)
    experts_drawn, slots_drawn = jax.vmap(lambda block_key: route_block(block_key, TOK_DEV, CAP, EXPERTS))(block_keys)
    return (experts_drawn.reshape(SEQS, LEN, TOP).astype(jnp.int32), slots_drawn.reshape(SEQS, LEN, TOP).astype(jnp.int32))


def draw_routes(key, part):
    return draw_both(key)[0]


def draw_slot_index(key, part):
    return draw_both(key)[1]


def spiked(values, stream_key, source, target, parts, factor):
    def block_of(axis_at):
        return (jnp.arange(values.shape[axis_at]) // (values.shape[axis_at] // parts)).reshape((-1,) + (1,) * (values.ndim - 1 - axis_at))

    first = jax.random.permutation(stream_key, parts)[block_of(target)]
    other_side = (block_of(target) + parts // 2) % parts
    return jnp.where((block_of(source) == first) | (block_of(source) == other_side), factor * values, values)


def block_scale(own_key, dims, cuts, low, top_value):
    def one(dim, blocks):
        steps = jax.random.uniform(jax.random.fold_in(jax.random.fold_in(own_key, 6), dim), (blocks,), jnp.float32, low / len(cuts), top_value / len(cuts))
        return jnp.repeat(jnp.exp(steps), dims[dim] // blocks).reshape((-1,) + (1,) * (len(dims) - dim - 1))

    loudness = one(*cuts[0])
    for cut in cuts[1:]:
        loudness = loudness * one(*cut)
    return loudness


def noise(own_key, dims, width, reach, pieces=(), kind=jnp.bfloat16):
    factor_of = block_scale(own_key, dims, pieces, -0.22, 0.18) if pieces else 1.0
    array = jax.random.normal(own_key, dims, jnp.float32) * width * factor_of
    return jnp.minimum(jnp.maximum(array, -reach), reach).astype(kind)


def noise_with(key, dims, spread, reach, cuts, heavy, kind=jnp.bfloat16):
    array = spread * jax.random.normal(key, dims, jnp.float32)
    if cuts:
        array = array * block_scale(key, dims, cuts, -0.22, 0.18)
    return jnp.clip(spiked(array, jax.random.fold_in(key, 3), *heavy), -reach, reach).astype(kind)


def setup_inputs(seed: int = 0) -> dict:
    seeds = jax.random.split(jax.random.key(seed), 14)
    inputs = noise_with(seeds[0], (SEQS, LEN, D), 1.0, 6.0, ((0, 8), (1, 4)), (0, 2, 8, 2.0))
    attn_gain = jnp.clip(1.0 + 0.1 * jax.random.normal(seeds[1], (D,), jnp.float32), 0.5, 1.5)
    qkv_weight = noise(seeds[2], (D, HEADS, 3, HEAD_DIM), D ** -0.5, 0.21875, ((0, 8),), jnp.float32)
    out_weight = noise(seeds[3], (D, D), (max(D // 256, 1)) ** -0.5, 3.5, ((0, 8),), jnp.float32)
    ffn_gain = jnp.clip(1.0 + 0.1 * jax.random.normal(seeds[4], (D,), jnp.float32), 0.5, 1.5)
    router_weight = noise(seeds[5], (D, EXPERTS), (2 * D) ** -0.5, 0.15625, ((0, 8),), jnp.float32)
    expert_in = noise(seeds[6], (EXPERTS, D, 2 * FF), D ** -0.5, 0.21875, ((1, 8),), jnp.float32)
    expert_out = noise(seeds[7], (EXPERTS, FF, D), (FF // 16) ** -0.5, 0.5, ((1, 8),), jnp.float32)
    shared_in = noise(seeds[8], (D, 2 * FF), D ** -0.5, 0.21875, ((0, 8),), jnp.float32)
    shared_out = noise(seeds[9], (FF, D), (FF // 4) ** -0.5, 0.25, ((0, 8),), jnp.float32)
    routes = draw_routes(jax.random.fold_in(seeds[13], 71), 0)
    slot_index = draw_slot_index(jax.random.fold_in(seeds[13], 71), 0)
    cotangent = noise(seeds[12], (SEQS, LEN, D), 1.0, 6.0, ((0, 8), (1, 4)))
    return {"inputs": inputs, "attn_gain": attn_gain, "qkv_weight": qkv_weight, "out_weight": out_weight, "ffn_gain": ffn_gain, "router_weight": router_weight, "expert_in": expert_in, "expert_out": expert_out, "shared_in": shared_in, "shared_out": shared_out, "routes": routes, "slot_index": slot_index, "cotangent": cotangent}


EPSILON = 1e-05
BEST_PRECISION = lax.Precision.HIGHEST

@jax.custom_vjp
def low(v):
    return lax.optimization_barrier(v.astype(jnp.bfloat16)).astype(jnp.float32)

@jax.custom_vjp
def low_back(v):
    return v

def low_keep(v):
    return (low(v), None)

def low_pass(kept, grad):
    return (grad,)

def back_keep(v):
    return (v, None)

def back_low(kept, grad):
    return (low(grad),)
low.defvjp(low_keep, low_pass)
low_back.defvjp(back_keep, back_low)

def rotary_tables(positions):
    half_dim = HEAD_DIM // 2
    frequency = 10000.0 ** (-jnp.arange(half_dim, dtype=jnp.float32) / half_dim)
    angles = positions.astype(jnp.float32)[:, None] * frequency[None, :]
    return (jnp.cos(angles), jnp.sin(angles))

def rotate(values, cos_table, sine_table):
    half_dim = values.shape[-1] // 2
    first_half = values[..., :half_dim]
    second_half = values[..., half_dim:]
    cos_heads = cos_table[:, None, :]
    sine_heads = sine_table[:, None, :]
    return jnp.concatenate([first_half * cos_heads - second_half * sine_heads, second_half * cos_heads + first_half * sine_heads], axis=-1)

def attend_sequence(queries, keys_all, values_all):
    length = queries.shape[0]
    block_rows = min(512, length)
    block_count = length // block_rows
    key_block = jnp.arange(length) // ATT_BLOCK
    score_scale = HEAD_DIM ** (-0.5)

    @jax.checkpoint
    def one_block(query_rows, row_start):
        scores = jnp.einsum('qhe,khe->hqk', query_rows, keys_all, precision=BEST_PRECISION) * score_scale
        scores = low_back(scores)
        query_block = (row_start + jnp.arange(block_rows)) // ATT_BLOCK
        allowed = key_block[None, :] <= query_block[:, None]
        scores = jnp.where(allowed[None], scores, -1e+30)
        attn_probs = jax.nn.softmax(scores, axis=-1)
        return jnp.einsum('hqk,khe->qhe', low(attn_probs), values_all, precision=BEST_PRECISION)
    starts = jnp.arange(block_count) * block_rows
    blocked = queries.reshape(block_count, block_rows, HEADS, HEAD_DIM)
    results = lax.map(lambda element: one_block(element[0], element[1]), (blocked, starts))
    return results.reshape(length, HEADS, HEAD_DIM)

def layer(stream, attn_gain, qkv_weight, out_weight, ffn_gain, router_weight, expert_in, expert_out, shared_in, shared_out, route_rows, slot_rows):
    length = stream.shape[0]
    cos_table, sine_table = rotary_tables(jnp.arange(length))
    normed = stream * lax.rsqrt(lax.optimization_barrier(jnp.mean(stream * stream, axis=-1, keepdims=True)) + EPSILON) * low(attn_gain)
    projected = jnp.einsum('td,dhce->thce', low(normed), low(qkv_weight), precision=BEST_PRECISION)
    projected = low_back(projected)
    rotated = jnp.stack([rotate(projected[:, :, 0], cos_table, sine_table), rotate(projected[:, :, 1], cos_table, sine_table), projected[:, :, 2]], axis=2)
    rotated = low(low_back(rotated))
    attended = attend_sequence(rotated[:, :, 0], rotated[:, :, 1], rotated[:, :, 2])
    attended = low(low_back(attended)).reshape(length, D)
    branch = low_back(jnp.dot(attended, low(out_weight), precision=BEST_PRECISION))
    middle = stream + branch
    normed_two = middle * lax.rsqrt(lax.optimization_barrier(jnp.mean(middle * middle, axis=-1, keepdims=True)) + EPSILON) * low(ffn_gain)
    hidden_in = low(normed_two)
    logits = low_back(jnp.dot(hidden_in, low(router_weight), precision=BEST_PRECISION))
    router_probs = jax.nn.softmax(logits, axis=-1)
    gate_values = jnp.take_along_axis(router_probs, route_rows, axis=1)
    owner = (jnp.arange(length) // TOK_DEV).astype(jnp.int32)[:, None]
    flat_slot = ((owner * EXPERTS + route_rows) * CAP + slot_rows).astype(jnp.int32).reshape(-1)
    buffer = jnp.zeros((N_SEQ * EXPERTS * CAP, D), jnp.float32).at[flat_slot].set(jnp.repeat(hidden_in, TOP, axis=0))
    buffer = buffer.reshape(N_SEQ, EXPERTS, CAP, D)
    gate_up = low_back(jnp.einsum('secd,edf->secf', buffer, low(expert_in), precision=BEST_PRECISION))
    activated = low(jax.nn.silu(gate_up[..., :FF]) * gate_up[..., FF:])
    expert_rows = low_back(jnp.einsum('secf,efd->secd', activated, low(expert_out), precision=BEST_PRECISION)).reshape(-1, D)
    picked = expert_rows[flat_slot].reshape(length, TOP, D)
    mixture = lax.optimization_barrier(jnp.sum(gate_values[:, :, None] * picked, axis=1))
    shared_gu = low_back(jnp.dot(hidden_in, low(shared_in), precision=BEST_PRECISION))
    shared_act = low(jax.nn.silu(shared_gu[:, :FF]) * shared_gu[:, FF:])
    shared_rows = low_back(jnp.dot(shared_act, low(shared_out), precision=BEST_PRECISION))
    return middle + mixture + shared_rows

def reference(inputs, attn_gain, qkv_weight, out_weight, ffn_gain, router_weight, expert_in, expert_out, shared_in, shared_out, routes, slot_index, cotangent):
    weights = (attn_gain, qkv_weight, out_weight, ffn_gain, router_weight, expert_in, expert_out, shared_in, shared_out)

    def per_sequence(running, element):
        stream, route_rows, slot_rows, upstream = element

        def forward(stream_in, *params):
            return layer(stream_in, *params, route_rows, slot_rows)
        result, pullback = jax.vjp(forward, stream.astype(jnp.float32), *weights)
        gradients = pullback(upstream.astype(jnp.float32))
        running = tuple((summed + gradient for summed, gradient in zip(running, gradients[1:])))
        return (running, (result.astype(jnp.bfloat16), gradients[0]))
    initial = tuple((jnp.zeros_like(weight_arr) for weight_arr in weights))
    totals, (outputs, input_grads) = lax.scan(per_sequence, initial, (inputs, routes, slot_index, cotangent))
    return (outputs, input_grads, totals[0], totals[1], totals[2], totals[3], totals[4], totals[5], totals[6], totals[7], totals[8])
```

```python
import functools
import types

import jax
import jax.numpy as jnp
import numpy as np
from jax import lax
from jax.experimental import pallas as pl
from jax.experimental.pallas import tpu as pltpu
from jax.sharding import PartitionSpec as P

D = 768
HEADS = 12
HEAD_DIM = 64
FF = 2048
EXPERTS = 3
TOP = 2
ATT_BLOCK = 256
CAP = 192


EPSILON = 1e-05
VMEM_LIMIT = 66_000_000


def rotary_tables(positions):
    half_dim = HEAD_DIM // 2
    frequency = 10000.0 ** (-jnp.arange(half_dim, dtype=jnp.float32) / half_dim)
    angles = positions.astype(jnp.float32)[:, None] * frequency[None, :]
    return (jnp.cos(angles), jnp.sin(angles))


def rotate(values, cos_table, sine_table):
    half_dim = values.shape[-1] // 2
    first_half = values[..., :half_dim]
    second_half = values[..., half_dim:]
    cos_heads = cos_table[:, None, :]
    sine_heads = sine_table[:, None, :]
    return jnp.concatenate(
        [
            first_half * cos_heads - second_half * sine_heads,
            second_half * cos_heads + first_half * sine_heads,
        ],
        axis=-1,
    )


def unrotate(values, cos_table, sine_table):
    half_dim = values.shape[-1] // 2
    first_half = values[..., :half_dim]
    second_half = values[..., half_dim:]
    cos_heads = cos_table[:, None, :]
    sine_heads = sine_table[:, None, :]
    return jnp.concatenate(
        [
            first_half * cos_heads + second_half * sine_heads,
            second_half * cos_heads - first_half * sine_heads,
        ],
        axis=-1,
    )


def silu_grads(gate_in, up_in, upstream):
    sigmoid = jax.nn.sigmoid(gate_in)
    swish = gate_in * sigmoid
    slope = sigmoid * (1.0 + gate_in * (1.0 - sigmoid))
    return jnp.concatenate([upstream * up_in * slope, upstream * swish], axis=-1)


def block_mask(row_start, block_rows, length):
    query_block = (row_start + jnp.arange(block_rows, dtype=jnp.int32)) // ATT_BLOCK
    key_block = jnp.arange(length, dtype=jnp.int32) // ATT_BLOCK
    return key_block[None, :] <= query_block[:, None]


def attend_heads(received):
    packed = received[:, 0]
    length = packed.shape[0]
    heads_here = packed.shape[1]
    queries = packed[..., :HEAD_DIM]
    keys_all = packed[..., HEAD_DIM : 2 * HEAD_DIM]
    values_all = packed[..., 2 * HEAD_DIM :]
    block_rows = min(512, length)
    block_count = length // block_rows
    score_scale = HEAD_DIM ** (-0.5)

    def one_block(element):
        query_rows, row_start = element
        scores = (
            jnp.einsum("qhe,khe->hqk", query_rows, keys_all, preferred_element_type=jnp.float32)
            * score_scale
        )
        scores = jnp.where(block_mask(row_start, block_rows, length)[None], scores, -1e30)
        largest = jnp.max(scores, axis=-1, keepdims=True)
        weights_exp = jnp.exp(scores - largest)
        totals = jnp.sum(weights_exp, axis=-1, keepdims=True)
        attn_probs = (weights_exp / totals).astype(jnp.bfloat16)
        mixed_rows = jnp.einsum(
            "hqk,khe->qhe", attn_probs, values_all, preferred_element_type=jnp.float32
        )
        log_total = (largest + jnp.log(totals))[..., 0]
        return (mixed_rows.astype(jnp.bfloat16), jnp.transpose(log_total))

    blocked = queries.reshape(block_count, block_rows, heads_here, HEAD_DIM)
    starts = jnp.arange(block_count, dtype=jnp.int32) * block_rows
    mixed_rows, log_total = lax.map(one_block, (blocked, starts))
    return (
        mixed_rows.reshape(length, 1, heads_here, HEAD_DIM),
        log_total.reshape(length, 1, heads_here),
        received,
    )


def attend_back(received, log_sum, grad_in):
    packed = received[:, 0]
    length = packed.shape[0]
    heads_here = packed.shape[1]
    queries = packed[..., :HEAD_DIM]
    keys_all = packed[..., HEAD_DIM : 2 * HEAD_DIM]
    values_all = packed[..., 2 * HEAD_DIM :]
    block_rows = min(512, length)
    block_count = length // block_rows
    score_scale = HEAD_DIM ** (-0.5)

    def one_block(running, element):
        key_acc, value_acc = running
        query_rows, grad_rows, log_rows, row_start = element
        scores = (
            jnp.einsum("qhe,khe->hqk", query_rows, keys_all, preferred_element_type=jnp.float32)
            * score_scale
        )
        scores = jnp.where(block_mask(row_start, block_rows, length)[None], scores, -1e30)
        attn_probs = jnp.exp(scores - jnp.transpose(log_rows)[:, :, None])
        value_acc = value_acc + jnp.einsum(
            "hqk,qhe->khe",
            attn_probs.astype(jnp.bfloat16),
            grad_rows,
            preferred_element_type=jnp.float32,
        )
        grad_probs = jnp.einsum(
            "qhe,khe->hqk", grad_rows, values_all, preferred_element_type=jnp.float32
        )
        centre = jnp.sum(attn_probs * grad_probs, axis=-1, keepdims=True)
        grad_scores = (attn_probs * (grad_probs - centre)).astype(jnp.bfloat16)
        query_grad = (
            jnp.einsum("hqk,khe->qhe", grad_scores, keys_all, preferred_element_type=jnp.float32)
            * score_scale
        )
        key_acc = key_acc + jnp.einsum(
            "hqk,qhe->khe", grad_scores, query_rows, preferred_element_type=jnp.float32
        )
        return ((key_acc, value_acc), query_grad)

    empty_acc = jnp.zeros((length, heads_here, HEAD_DIM), jnp.float32)
    blocked_query = queries.reshape(block_count, block_rows, heads_here, HEAD_DIM)
    blocked_grad = grad_in[:, 0].reshape(block_count, block_rows, heads_here, HEAD_DIM)
    blocked_log = log_sum[:, 0].reshape(block_count, block_rows, heads_here)
    starts = jnp.arange(block_count, dtype=jnp.int32) * block_rows
    (key_acc, value_acc), query_grads = lax.scan(
        one_block, (empty_acc, empty_acc), (blocked_query, blocked_grad, blocked_log, starts)
    )
    stacked = jnp.stack(
        [query_grads.reshape(length, heads_here, HEAD_DIM), key_acc * score_scale, value_acc],
        axis=2,
    )
    return stacked.astype(jnp.bfloat16).reshape(length, 1, heads_here, 3 * HEAD_DIM)


def norm_back(values, scale_rows, gain_row, upstream):
    scaled = upstream * gain_row
    gain_term = jnp.sum(upstream * values * scale_rows, axis=0)
    value_grad = scale_rows * scaled - values * scale_rows**3 * jnp.mean(
        scaled * values, axis=-1, keepdims=True
    )
    return (gain_term, value_grad)


def on_device(
    inputs,
    attn_gain,
    qkv_weight,
    out_weight,
    ffn_gain,
    router_weight,
    expert_in,
    expert_out,
    shared_in,
    shared_out,
    routes,
    slot_index,
    cotangent,
):
    tok_rows = inputs.shape[1]
    group_count = lax.axis_size("seq")
    heads_group = HEADS // group_count
    stream = inputs[0].astype(jnp.float32)
    attn_local = (
        attn_gain.astype(jnp.bfloat16),
        qkv_weight.astype(jnp.bfloat16),
        out_weight.astype(jnp.bfloat16),
    )
    attn_full = (
        lax.all_gather(attn_local[0], "dp", axis=0, tiled=True),
        lax.all_gather(attn_local[1], "dp", axis=0, tiled=True),
        lax.all_gather(attn_local[2], "dp", axis=0, tiled=True),
    )
    gain_first, qkv_full, out_full = attn_full
    positions = lax.axis_index("seq") * tok_rows + jnp.arange(tok_rows, dtype=jnp.int32)
    cos_table, sine_table = rotary_tables(positions)
    scale_one = lax.rsqrt(jnp.mean(stream * stream, axis=-1, keepdims=True) + EPSILON)
    gain_one_f = gain_first.astype(jnp.float32)
    normed = (stream * scale_one * gain_one_f).astype(jnp.bfloat16)
    projected = jnp.einsum("td,dhce->thce", normed, qkv_full, preferred_element_type=jnp.float32)
    rotated = jnp.stack(
        [
            rotate(projected[:, :, 0], cos_table, sine_table),
            rotate(projected[:, :, 1], cos_table, sine_table),
            projected[:, :, 2],
        ],
        axis=2,
    ).astype(jnp.bfloat16)
    outgoing = rotated.reshape(tok_rows, group_count, heads_group, 3 * HEAD_DIM)
    head_out, log_sum, head_qkv = attend_heads(
        lax.all_to_all(outgoing, "seq", split_axis=1, concat_axis=0, tiled=True)
    )
    attended = lax.all_to_all(head_out, "seq", split_axis=0, concat_axis=1, tiled=True).reshape(
        tok_rows, D
    )
    middle = stream + jnp.dot(attended, out_full, preferred_element_type=jnp.float32)
    ffn_local = (
        ffn_gain.astype(jnp.bfloat16),
        router_weight.astype(jnp.bfloat16),
        expert_in.astype(jnp.bfloat16),
        expert_out.astype(jnp.bfloat16),
        shared_in.astype(jnp.bfloat16),
        shared_out.astype(jnp.bfloat16),
    )
    ffn_full = (
        lax.all_gather(ffn_local[0], "dp", axis=0, tiled=True),
        lax.all_gather(ffn_local[1], "dp", axis=0, tiled=True),
        lax.all_gather(ffn_local[2], "dp", axis=1, tiled=True),
        lax.all_gather(ffn_local[3], "dp", axis=1, tiled=True),
        lax.all_gather(ffn_local[4], "dp", axis=0, tiled=True),
        lax.all_gather(ffn_local[5], "dp", axis=0, tiled=True),
    )
    gain_second, router_full, exp_in_full, exp_out_full, sh_in_full, sh_out_full = ffn_full
    scale_two = lax.rsqrt(jnp.mean(middle * middle, axis=-1, keepdims=True) + EPSILON)
    gain_two_f = gain_second.astype(jnp.float32)
    normed_two = (middle * scale_two * gain_two_f).astype(jnp.bfloat16)
    logits = jnp.dot(normed_two, router_full, preferred_element_type=jnp.float32)
    router_probs = jax.nn.softmax(logits, axis=-1)
    route_rows = routes[0]
    choice_hot = (
        route_rows[:, :, None] == jnp.arange(EXPERTS, dtype=jnp.int32)[None, None, :]
    ).astype(jnp.float32)
    gate_values = jnp.sum(choice_hot * router_probs[:, None, :], axis=-1)
    flat_slot = (route_rows * CAP + slot_index[0]).reshape(-1)
    buffer = (
        jnp.zeros((EXPERTS * CAP, D), jnp.bfloat16)
        .at[flat_slot]
        .set(jnp.repeat(normed_two, TOP, axis=0))
        .reshape(EXPERTS, CAP, D)
    )
    gate_up = jnp.einsum("ecd,edf->ecf", buffer, exp_in_full, preferred_element_type=jnp.float32)
    activated = (jax.nn.silu(gate_up[..., :FF]) * gate_up[..., FF:]).astype(jnp.bfloat16)
    expert_rows = jnp.einsum(
        "ecf,efd->ecd", activated, exp_out_full, preferred_element_type=jnp.float32
    ).reshape(EXPERTS * CAP, D)
    picked = expert_rows[flat_slot].reshape(tok_rows, TOP, D)
    mixture = jnp.sum(gate_values[:, :, None] * picked, axis=1)
    shared_gu = jnp.dot(normed_two, sh_in_full, preferred_element_type=jnp.float32)
    shared_act = (jax.nn.silu(shared_gu[:, :FF]) * shared_gu[:, FF:]).astype(jnp.bfloat16)
    result = middle + mixture + jnp.dot(shared_act, sh_out_full, preferred_element_type=jnp.float32)
    output = result.astype(jnp.bfloat16)[None]
    ffn_back = (
        lax.all_gather(ffn_local[0], "dp", axis=0, tiled=True),
        lax.all_gather(ffn_local[1], "dp", axis=0, tiled=True),
        lax.all_gather(ffn_local[2], "dp", axis=1, tiled=True),
        lax.all_gather(ffn_local[3], "dp", axis=1, tiled=True),
        lax.all_gather(ffn_local[4], "dp", axis=0, tiled=True),
        lax.all_gather(ffn_local[5], "dp", axis=0, tiled=True),
    )
    router_back, exp_in_back, exp_out_back, sh_in_back, sh_out_back = (
        ffn_back[1],
        ffn_back[2],
        ffn_back[3],
        ffn_back[4],
        ffn_back[5],
    )
    upstream = cotangent[0].astype(jnp.float32)
    grad_low = upstream.astype(jnp.bfloat16)
    shared_out_grad = jnp.einsum(
        "tf,td->fd", shared_act, grad_low, preferred_element_type=jnp.float32
    )
    shared_act_grad = jnp.einsum(
        "td,fd->tf", grad_low, sh_out_back, preferred_element_type=jnp.float32
    )
    shared_gu_grad = silu_grads(shared_gu[:, :FF], shared_gu[:, FF:], shared_act_grad).astype(
        jnp.bfloat16
    )
    shared_in_grad = jnp.einsum(
        "td,tf->df", normed_two, shared_gu_grad, preferred_element_type=jnp.float32
    )
    norm_grad_two = jnp.einsum(
        "tf,df->td", shared_gu_grad, sh_in_back, preferred_element_type=jnp.float32
    )
    slot_terms = (gate_values[:, :, None] * upstream[:, None, :]).reshape(tok_rows * TOP, D)
    slot_grad = (
        jnp.zeros((EXPERTS * CAP, D), jnp.float32)
        .at[flat_slot]
        .set(slot_terms)
        .astype(jnp.bfloat16)
        .reshape(EXPERTS, CAP, D)
    )
    expert_out_grad = jnp.einsum(
        "ecf,ecd->efd", activated, slot_grad, preferred_element_type=jnp.float32
    )
    activated_grad = jnp.einsum(
        "ecd,efd->ecf", slot_grad, exp_out_back, preferred_element_type=jnp.float32
    )
    gate_up_grad = silu_grads(gate_up[..., :FF], gate_up[..., FF:], activated_grad).astype(
        jnp.bfloat16
    )
    expert_in_grad = jnp.einsum(
        "ecd,ecf->edf", buffer, gate_up_grad, preferred_element_type=jnp.float32
    )
    buffer_grad = jnp.einsum(
        "ecf,edf->ecd", gate_up_grad, exp_in_back, preferred_element_type=jnp.float32
    ).reshape(EXPERTS * CAP, D)
    norm_grad_two = norm_grad_two + jnp.sum(
        buffer_grad[flat_slot].reshape(tok_rows, TOP, D), axis=1
    )
    gate_grad = jnp.sum(upstream[:, None, :] * picked, axis=-1)
    prob_grad = jnp.sum(choice_hot * gate_grad[:, :, None], axis=1)
    logit_grad = (
        router_probs * (prob_grad - jnp.sum(router_probs * prob_grad, axis=-1, keepdims=True))
    ).astype(jnp.bfloat16)
    router_weight_grad = jnp.einsum(
        "td,te->de", normed_two, logit_grad, preferred_element_type=jnp.float32
    )
    norm_grad_two = norm_grad_two + jnp.einsum(
        "te,de->td", logit_grad, router_back, preferred_element_type=jnp.float32
    )
    ffn_gain_term, middle_part = norm_back(middle, scale_two, gain_two_f, norm_grad_two)
    middle_grad = upstream + middle_part
    attn_back = (
        lax.all_gather(attn_local[0], "dp", axis=0, tiled=True),
        lax.all_gather(attn_local[1], "dp", axis=0, tiled=True),
        lax.all_gather(attn_local[2], "dp", axis=0, tiled=True),
    )
    qkv_back, out_back = (attn_back[1], attn_back[2])
    middle_low = middle_grad.astype(jnp.bfloat16)
    out_weight_grad = jnp.einsum(
        "tf,td->fd", attended, middle_low, preferred_element_type=jnp.float32
    )
    attended_grad = jnp.einsum(
        "td,fd->tf", middle_low, out_back, preferred_element_type=jnp.float32
    ).astype(jnp.bfloat16)
    head_grad = lax.all_to_all(
        attended_grad.reshape(tok_rows, group_count, heads_group, HEAD_DIM),
        "seq",
        split_axis=1,
        concat_axis=0,
        tiled=True,
    )
    stacked = attend_back(head_qkv, log_sum, head_grad)
    returned = (
        lax.all_to_all(stacked, "seq", split_axis=0, concat_axis=1, tiled=True)
        .reshape(tok_rows, HEADS, 3, HEAD_DIM)
        .astype(jnp.float32)
    )
    projected_grad = jnp.stack(
        [
            unrotate(returned[:, :, 0], cos_table, sine_table),
            unrotate(returned[:, :, 1], cos_table, sine_table),
            returned[:, :, 2],
        ],
        axis=2,
    ).astype(jnp.bfloat16)
    qkv_weight_grad = jnp.einsum(
        "td,thce->dhce", normed, projected_grad, preferred_element_type=jnp.float32
    )
    norm_grad = jnp.einsum(
        "thce,dhce->td", projected_grad, qkv_back, preferred_element_type=jnp.float32
    )
    attn_gain_term, input_part = norm_back(stream, scale_one, gain_one_f, norm_grad)
    input_grad = (middle_grad + input_part)[None]
    parts = (
        lax.psum_scatter(
            qkv_weight_grad.astype(jnp.bfloat16), "seq", scatter_dimension=1, tiled=True
        ).astype(jnp.float32),
        lax.psum_scatter(
            out_weight_grad.astype(jnp.bfloat16), "seq", scatter_dimension=1, tiled=True
        ).astype(jnp.float32),
        lax.psum_scatter(
            expert_in_grad.astype(jnp.bfloat16), "seq", scatter_dimension=2, tiled=True
        ).astype(jnp.float32),
        lax.psum_scatter(
            expert_out_grad.astype(jnp.bfloat16), "seq", scatter_dimension=2, tiled=True
        ).astype(jnp.float32),
        lax.psum_scatter(
            shared_in_grad.astype(jnp.bfloat16), "seq", scatter_dimension=1, tiled=True
        ).astype(jnp.float32),
        lax.psum_scatter(
            shared_out_grad.astype(jnp.bfloat16), "seq", scatter_dimension=1, tiled=True
        ).astype(jnp.float32),
    )
    owned = (
        lax.psum_scatter(attn_gain_term, "dp", scatter_dimension=0, tiled=True),
        lax.psum_scatter(ffn_gain_term, "dp", scatter_dimension=0, tiled=True),
        lax.psum_scatter(router_weight_grad, "dp", scatter_dimension=0, tiled=True),
        lax.psum_scatter(parts[0], "dp", scatter_dimension=0, tiled=True),
        lax.psum_scatter(parts[1], "dp", scatter_dimension=0, tiled=True),
        lax.psum_scatter(parts[2], "dp", scatter_dimension=1, tiled=True),
        lax.psum_scatter(parts[3], "dp", scatter_dimension=1, tiled=True),
        lax.psum_scatter(parts[4], "dp", scatter_dimension=0, tiled=True),
        lax.psum_scatter(parts[5], "dp", scatter_dimension=0, tiled=True),
    )
    small = lax.psum((owned[0], owned[1], owned[2]), "seq")
    joined = (
        lax.all_gather(owned[3].astype(jnp.bfloat16), "seq", axis=1, tiled=True).astype(
            jnp.float32
        ),
        lax.all_gather(owned[4].astype(jnp.bfloat16), "seq", axis=1, tiled=True).astype(
            jnp.float32
        ),
        lax.all_gather(owned[5].astype(jnp.bfloat16), "seq", axis=2, tiled=True).astype(
            jnp.float32
        ),
        lax.all_gather(owned[6].astype(jnp.bfloat16), "seq", axis=2, tiled=True).astype(
            jnp.float32
        ),
        lax.all_gather(owned[7].astype(jnp.bfloat16), "seq", axis=1, tiled=True).astype(
            jnp.float32
        ),
        lax.all_gather(owned[8].astype(jnp.bfloat16), "seq", axis=1, tiled=True).astype(
            jnp.float32
        ),
    )
    return (
        output,
        input_grad,
        small[0],
        joined[0],
        joined[1],
        small[1],
        small[2],
        joined[2],
        joined[3],
        joined[4],
        joined[5],
    )


MESH = pl.DeviceIdType.MESH
BF = jnp.bfloat16
F32 = jnp.float32
TOK = ATT_BLOCK
QKV_PAD = 640


def nn(a, b):
    return lax.dot_general(a, b, (((1,), (0,)), ((), ())), preferred_element_type=F32)


def nt(a, b):
    return lax.dot_general(a, b, (((1,), (1,)), ((), ())), preferred_element_type=F32)


def tn(a, b):
    return lax.dot_general(a, b, (((0,), (0,)), ((), ())), preferred_element_type=F32)


def swap_halves(v):
    lane = lax.broadcasted_iota(jnp.int32, v.shape, 1)
    return jnp.where(lax.rem(lane, 64) < 32, pltpu.roll(v, 96, 1), pltpu.roll(v, 32, 1))


def layer_kernel(names, *refs):
    r = types.SimpleNamespace(**dict(zip(names, refs)))
    b = lax.axis_index("dp")
    s = lax.axis_index("seq")
    z = lax.div(b, 2)
    y = lax.rem(b, 2)
    z1 = lax.div(b, 4)
    z0 = lax.rem(z, 2)
    x = lax.div(s, 2)
    c = lax.rem(s, 2)
    zf = z + 1 - 2 * z0
    zg = z + 2 - 4 * z1
    zh = zf + 2 - 4 * z1
    core = (b, s + 1 - 2 * c)
    xp = (b, s + 2 - 4 * x)
    diag = (b, 3 - s)
    yp = (b + 1 - 2 * y, s)
    z0p = (b + 2 - 4 * z0, s)
    z1p = (b + 4 - 8 * z1, s)
    p1 = (b + c * (2 - 4 * z0), s + (1 - c) * (2 - 4 * x))
    p2 = (b + (1 - c) * (2 - 4 * z0), s + c * (2 - 4 * x))
    jme = z0 * 2 + x
    jx = z0 * 2 + 1 - x
    jz = (1 - z0) * 2 + x
    jd = (1 - z0) * 2 + 1 - x
    jp1 = jx + c * (jz - jx)
    jp2 = jz + c * (jx - jz)
    oc = 1 - c
    oy = 1 - y

    def send(src, dst, ss, rs, dev):
        pltpu.make_async_remote_copy(
            src_ref=src, dst_ref=dst, send_sem=ss, recv_sem=rs, device_id=dev, device_id_type=MESH
        ).start()

    def sent(src, ss):
        pltpu.make_async_remote_copy(
            src_ref=src, dst_ref=src, send_sem=ss, recv_sem=ss, device_id=core, device_id_type=MESH
        ).wait_send()

    def got(dst, rs):
        pltpu.make_async_remote_copy(
            src_ref=dst, dst_ref=dst, send_sem=rs, recv_sem=rs, device_id=core, device_id_type=MESH
        ).wait_recv()

    def ag_first(src, slot, ss, rs):
        send(src, slot(z, y), ss(0), rs(b), z0p)

    def ag_own(slot, ss, rs):
        send(slot(z, y), slot(z, y), ss(1), rs(b), z1p)
        send(slot(z, y), slot(z, y), ss(2), rs(b), yp)

    def ag_z0(slot, ss, rs):
        k = 2 * zf + y
        got(slot(zf, y), rs(k))
        send(slot(zf, y), slot(zf, y), ss(3), rs(k), z1p)
        send(slot(zf, y), slot(zf, y), ss(4), rs(k), yp)

    def ag_z1(slot, ss, rs):
        for zz, n in ((zg, 5), (zh, 6)):
            k = 2 * zz + y
            got(slot(zz, y), rs(k))
            send(slot(zz, y), slot(zz, y), ss(n), rs(k), yp)

    def ag_fin(slot, rs):
        for zz in range(4):
            got(slot(zz, oy), rs(2 * zz + oy))

    def ag_sent(src, slot, ss):
        sent(src, ss(0))
        for n in range(1, 7):
            sent(slot(z, y), ss(n))

    def tok_own(buf, n):
        own = buf.at[jme, c]
        send(own, own, r.tok_s.at[n, 1], r.tok_r.at[n, 1], p1)
        send(own, own, r.tok_s.at[n, 2], r.tok_r.at[n, 2], p2)
        send(own, own, r.tok_s.at[n, 0], r.tok_r.at[n, 0], core)

    def tok_relay(buf, n):
        v = buf.at[jp1, c]
        got(v, r.tok_r.at[n, 1])
        send(v, v, r.tok_s.at[n, 3], r.tok_r.at[n, 3], p2)
        send(v, v, r.tok_s.at[n, 4], r.tok_r.at[n, 4], core)
        v = buf.at[jp2, c]
        got(v, r.tok_r.at[n, 2])
        send(v, v, r.tok_s.at[n, 5], r.tok_r.at[n, 5], core)
        v = buf.at[jd, c]
        got(v, r.tok_r.at[n, 3])
        send(v, v, r.tok_s.at[n, 6], r.tok_r.at[n, 6], core)

    def tok_fin(buf, n):
        got(buf.at[jme, oc], r.tok_r.at[n, 0])
        got(buf.at[jp2, oc], r.tok_r.at[n, 4])
        got(buf.at[jp1, oc], r.tok_r.at[n, 5])
        got(buf.at[jd, oc], r.tok_r.at[n, 6])
        for k in range(7):
            sent(buf.at[jme, c], r.tok_s.at[n, k])

    def sum_first(buf, rc, n):
        send(buf.at[:, oc], rc, r.sum_s.at[n, 0], r.sum_r.at[n, 0], core)

    def sum_core(buf, rc, rp, n):
        got(rc, r.sum_r.at[n, 0])
        for j in range(4):
            buf[j, c] = (buf[j, c].astype(F32) + rc[j].astype(F32)).astype(BF)
        send(buf.at[jd, c], rp.at[0], r.sum_s.at[n, 1], r.sum_r.at[n, 1], p2)
        send(buf.at[jp2, c], rp.at[1], r.sum_s.at[n, 2], r.sum_r.at[n, 2], p2)

    def sum_relay(buf, rp, n):
        got(rp.at[0], r.sum_r.at[n, 1])
        buf[jp1, c] = (buf[jp1, c].astype(F32) + rp[0].astype(F32)).astype(BF)
        send(buf.at[jp1, c], rp.at[2], r.sum_s.at[n, 3], r.sum_r.at[n, 3], p1)

    def sum_fin(buf, rc, rp, n):
        got(rp.at[1], r.sum_r.at[n, 2])
        got(rp.at[2], r.sum_r.at[n, 3])
        total = buf[jme, c].astype(F32) + rp[1].astype(F32) + rp[2].astype(F32)
        sent(rc, r.sum_s.at[n, 0])
        for k in range(1, 4):
            sent(rp.at[0], r.sum_s.at[n, k])
        return total

    barrier = pltpu.get_barrier_semaphore()
    peers = (core, xp, diag, yp, z0p, z1p)
    for dev in peers:
        pl.semaphore_signal(barrier, inc=1, device_id=dev, device_id_type=MESH)

    def stage_copies():
        out = []
        for m in range(4):
            for zz in range(2):
                for h in range(2):
                    for k in range(2):
                        zt = z0 + zz * (1 - 2 * z0)
                        col = pl.multiple_of(
                            h * 2048 + 1024 * k + 512 * zt + 256 * c + 128 * x, 128
                        )
                        if m < 3:
                            src = r.e_in.at[m, :, pl.ds(col, 128)]
                        else:
                            src = r.s_in.at[:, pl.ds(col, 128)]
                        at = (h * 2 + k) * 128
                        q = 2 * m + zz
                        dst = r.acc.at[q // 2, q % 2, pl.ds(0, 96), pl.ds(at, 128)]
                        out.append((src, dst, r.stage_sem.at[m, zz * 4 + h * 2 + k]))
            row = pl.multiple_of(128 * x, 128)
            if m < 3:
                src = r.e_out.at[m, pl.ds(row, 128), :]
            else:
                src = r.s_out.at[pl.ds(row, 128), :]
            dst = r.acc.at[m // 2, m % 2, pl.ds(96, 128), pl.ds(0, D)]
            out.append((src, dst, r.stage_sem.at[m, 8]))
        return [pltpu.make_async_copy(*one) for one in out]

    staged = stage_copies()
    for one in staged:
        one.start()

    q_slot = lambda zz, yy: r.wq.at[zz, yy]
    q_ss = lambda n: r.att_s.at[0, n]
    q_rs = lambda n: r.att_r.at[0, n]
    o_slot = lambda zz, yy: r.ow.at[zz, yy, c]
    o_ss = lambda n: r.att_s.at[1, n]
    o_rs = lambda n: r.att_r.at[1, n]
    m_slot = lambda zz, yy: r.misc.at[zz, yy]
    m_ss = lambda n: r.att_s.at[2, n]
    m_rs = lambda n: r.att_r.at[2, n]

    def w_slot(m):
        return lambda zz, yy: r.win.at[m, zz, yy]

    def w_ss(m):
        return lambda n: r.w_s.at[m, n]

    def w_rs(m):
        return lambda n: r.w_r.at[m, n]

    r.wq[z, y] = r.wq_in[...]
    r.misc[z, y] = r.misc_in[...]
    r.ow[z, y, c] = r.ow_in[...]
    r.nall[s] = r.x_in[...]
    r.cota[jme, c] = r.cot_in[...]

    pl.semaphore_wait(barrier, len(peers))

    send(r.x_in, r.nall.at[s], r.x_s.at[0], r.x_r.at[0], core)
    send(r.x_in, r.nall.at[s], r.x_s.at[1], r.x_r.at[1], xp)
    att_sets = (
        (r.misc_in, m_slot, m_ss, m_rs),
        (r.wq_in, q_slot, q_ss, q_rs),
        (r.ow_in, o_slot, o_ss, o_rs),
    )
    for src, slot, ss, rs in att_sets:
        ag_first(src, slot, ss, rs)
        ag_own(slot, ss, rs)

    for one in staged:
        one.wait()
    for m in range(4):
        q = 2 * m
        r.win[m, z, y] = r.acc[q // 2, q % 2, 0:96, 0:512].astype(BF)
        q = 2 * m + 1
        r.dg[m, 0:96, :] = r.acc[q // 2, q % 2, 0:96, 0:512].astype(BF)
        ag_first(r.dg.at[m, pl.ds(0, 96)], w_slot(m), w_ss(m), w_rs(m))

    @pl.when(c == y)
    def _():
        for m in range(4):
            r.wout[m, z1] = r.acc[m // 2, m % 2, 96:224, 0:D].astype(BF)

    xf = s + 2 - 4 * x
    got(r.nall.at[xf], r.x_r.at[1])
    send(r.nall.at[xf], r.nall.at[xf], r.x_s.at[2], r.x_r.at[2], core)
    for src, slot, ss, rs in att_sets:
        ag_z0(slot, ss, rs)
    for src, slot, ss, rs in att_sets:
        ag_z1(slot, ss, rs)
    tok_own(r.cota, 0)
    for src, slot, ss, rs in att_sets[:2]:
        ag_fin(slot, rs)

    def w_own(m):
        ag_own(w_slot(m), w_ss(m), w_rs(m))

        @pl.when(c == y)
        def _():
            v = r.wout.at[m, z1]
            send(v, v, r.o_s.at[m, 0], r.o_r.at[m, z1], z1p)
            send(v, v, r.o_s.at[m, 1], r.o_r.at[m, z1], yp)

    def w_relay(m):
        ag_z0(w_slot(m), w_ss(m), w_rs(m))

    def w_relay_far(m):
        ag_z1(w_slot(m), w_ss(m), w_rs(m))

        @pl.when(c == y)
        def _():
            v = r.wout.at[m, 1 - z1]
            got(v, r.o_r.at[m, 1 - z1])
            send(v, v, r.o_s.at[m, 2], r.o_r.at[m, 1 - z1], yp)

    def w_fin(m):
        ag_fin(w_slot(m), w_rs(m))

        @pl.when(c != y)
        def _():
            got(r.wout.at[m, 0], r.o_r.at[m, 0])
            got(r.wout.at[m, 1], r.o_r.at[m, 1])

        for n in range(1, 7):
            sent(r.win.at[m, z, y], r.w_s.at[m, n])

        @pl.when(c == y)
        def _():
            for k in range(3):
                sent(r.wout.at[m, 0], r.o_s.at[m, k])

    for m in range(4):
        w_own(m)

    rows = jnp.zeros((8, D), F32)
    for k in range(8):
        row_i = lax.broadcasted_iota(jnp.int32, (128, D), 0)
        col_i = lax.broadcasted_iota(jnp.int32, (128, D), 1)
        place = jnp.where((col_i == row_i + 96 * k) & (row_i < 96), 1.0, 0.0).astype(BF)
        rows = rows + nn(r.misc[k // 2, k % 2].astype(BF), place)
    r.mrow[...] = rows
    row8 = lax.broadcasted_iota(jnp.int32, (8, D), 0)
    r.rpad[...] = jnp.zeros((128, D), BF)
    r.rpad[0:16, :] = jnp.concatenate(
        [jnp.where(row8 < 3, rows, 0.0), jnp.zeros((8, D), F32)], axis=0
    ).astype(BF)

    got(r.nall.at[s + 1 - 2 * c], r.x_r.at[0])
    got(r.nall.at[3 - s], r.x_r.at[2])
    for k in range(3):
        sent(r.x_in, r.x_s.at[k])
    wq = r.wq[...].reshape(D, QKV_PAD)
    lane128 = lax.broadcasted_iota(jnp.int32, (TOK, 128), 1)

    def project(t, carry):
        xv = r.nall[t].astype(F32)
        r1 = lax.rsqrt(jnp.mean(xv * xv, axis=-1, keepdims=True) + EPSILON)
        nb = (xv * r1 * r.mrow[3:4, :]).astype(BF)
        r.nall[t] = nb
        pr = nn(nb, r.wq[...].reshape(D, QKV_PAD))
        at = pl.ds(pl.multiple_of(t * TOK, TOK), TOK)
        cosv = r.cos_in[at, :]
        sinv = r.sin_in[at, :]
        for h in range(3):
            g = pr[:, 128 * h : 128 * h + 128]
            g = (g * cosv + swap_halves(g) * sinv).astype(BF).astype(F32)
            g = jnp.where(lane128 < 64, g * 0.125, g)
            r.kq[h, at, :] = pltpu.roll(g, 64, 1).astype(BF)
        r.val[0, at, :] = pr[:, 384:512].astype(BF)
        r.val[1, at, :] = pr[:, 512:640].astype(BF)
        return carry

    lax.fori_loop(0, 4, project, 0)

    for m in range(4):
        w_relay(m)
    tok_relay(r.cota, 0)

    for i in range(3, -1, -1):
        n = (i + 1) * TOK
        base = i * (i + 1) // 2

        def heads(h, carry, i=i, n=n, base=base):
            q = pltpu.roll(r.kq[h, i * TOK : i * TOK + TOK, :].astype(F32), 64, 1)
            q = jnp.where(lane128 < 64, q, 0.0)
            sc = nt(q.astype(BF), r.kq[h, 0:n, :])
            top = jnp.max(sc, axis=-1, keepdims=True)
            e = jnp.exp(sc - top)
            pb = (e * (1.0 / jnp.sum(e, axis=-1, keepdims=True))).astype(BF)
            for j in range(i + 1):
                r.prob[h, base + j] = pb[:, j * TOK : j * TOK + TOK]
            r.acc[h, 0, :, 0:128] = nn(pb, r.val[lax.div(h, 2), 0:n, :])
            return carry

        lax.fori_loop(0, 3, heads, 0)
        r.att[i, :, 0:128] = jnp.where(lane128 < 64, r.acc[0, 0, :, 0:128], r.acc[1, 0, :, 0:128]).astype(BF)
        r.att[i, :, 128:256] = r.acc[2, 0, :, 0:128].astype(BF)

        @pl.when(s != i)
        def _(i=i):
            send(r.att.at[i], r.arow.at[s], r.a_s.at[i], r.a_r.at[s], (b, i))

        @pl.when(s == i)
        def _(i=i):
            r.arow[i] = r.att[i]

        if i == 3:
            ag_fin(o_slot, o_rs)
            send(r.ow.at[:, :, c], r.ow.at[:, :, c], r.ow_s.at[0], r.ow_r.at[0], core)
        if i == 2:
            w_relay_far(0)
        if i == 0:
            w_relay_far(1)

    got(r.ow.at[:, :, oc], r.ow_r.at[0])
    sent(r.ow.at[:, :, c], r.ow_s.at[0])
    for src, slot, ss, rs in att_sets:
        ag_sent(src, slot, ss)
    for i in range(4):

        @pl.when(s != i)
        def _(i=i):
            got(r.arow.at[i], r.a_r.at[i])
            sent(r.att.at[i], r.a_s.at[i])

    ow = r.ow[...].reshape(D, D)
    mid = r.x_in[...].astype(F32)
    for i in range(4):
        mid = mid + nn(r.arow[i][:, 0:192], ow[192 * i : 192 * i + 192, :])
    r.mid[...] = mid
    r2 = lax.rsqrt(jnp.mean(mid * mid, axis=-1, keepdims=True) + EPSILON)
    nb = (mid * r2 * r.mrow[4:5, :]).astype(BF)
    r.nown[...] = nb
    r.nta[jme, c, :, 0:D] = nb
    r.nta[jme, c, :, D : D + 128] = r.sel_in[...]
    tok_own(r.nta, 1)
    tok_fin(r.cota, 0)
    tok_relay(r.nta, 1)
    tok_fin(r.nta, 1)

    def gates(sel, nv):
        lg = nt(nv, r.rpad[...])
        lg = jnp.where(lane128 < 3, lg, -1e30)
        e = jnp.exp(lg - jnp.max(lg, axis=-1, keepdims=True))
        return e / jnp.sum(e, axis=-1, keepdims=True)

    def route(g, carry):
        j = lax.div(g, 2)
        k = lax.rem(g, 2)
        sel = r.nta[j, k, :, D : D + 128].astype(F32)
        pv = gates(sel, r.nta[j, k, :, 0:D])
        r.gate[g] = jnp.where(lane128 < 3, pv * sel, sel)
        r.acc[j, k] = jnp.zeros((TOK, D + 128), F32)
        return carry

    lax.fori_loop(0, 8, route, 0)
    r.pown[...] = gates(None, r.nown[...])

    def rs_first(m):
        send(r.win.at[m, :, oy], r.ry_in.at[m], r.rs_s.at[m, 0], r.rs_r.at[m, 0], yp)

        @pl.when(c != y)
        def _():
            send(r.gout.at[m], r.ry_out.at[m], r.rs_s.at[m, 1], r.rs_r.at[m, 1], yp)

    def rs_y(m):
        got(r.ry_in.at[m], r.rs_r.at[m, 0])
        for zz in range(4):
            r.win[m, zz, y] = (r.win[m, zz, y].astype(F32) + r.ry_in[m, zz].astype(F32)).astype(BF)
        send(
            r.win.at[m, pl.ds(2 - 2 * z1, 2), y], r.rz_in.at[m], r.rs_s.at[m, 2], r.rs_r.at[m, 2], z1p
        )

        @pl.when(c == y)
        def _():
            got(r.ry_out.at[m], r.rs_r.at[m, 1])
            for k in range(2):
                r.gout[m, k] = (r.gout[m, k].astype(F32) + r.ry_out[m, k].astype(F32)).astype(BF)
            send(r.gout.at[m, 1 - z1], r.rz_out.at[m], r.rs_s.at[m, 3], r.rs_r.at[m, 3], z1p)

    def rs_z(m):
        got(r.rz_in.at[m], r.rs_r.at[m, 2])
        for k in range(2):
            zz = 2 * z1 + k
            r.win[m, zz, y] = (r.win[m, zz, y].astype(F32) + r.rz_in[m, k].astype(F32)).astype(BF)
        send(r.win.at[m, zf, y], r.g_in.at[m, s, z0], r.rs_s.at[m, 4], r.rs_r.at[m, 4], z0p)
        pltpu.make_async_copy(r.win.at[m, z, y], r.g_in.at[m, s, z0], r.loc.at[m, 0]).start()

        @pl.when(c == y)
        def _():
            got(r.rz_out.at[m], r.rs_r.at[m, 3])
            v = (r.gout[m, z1].astype(F32) + r.rz_out[m].astype(F32)).astype(BF)
            r.gout[m, z1] = v
            g = r.gout.at[m, z1]
            pltpu.make_async_copy(g, r.g_out.at[m, x], r.loc.at[m, 1]).start()
            send(g, r.g_out.at[m, x], r.rs_s.at[m, 5], r.rs_r.at[m, 5], xp)
            send(g, r.g_out.at[m, x], r.rs_s.at[m, 6], r.rs_r.at[m, 6], core)

    def rs_join(m):
        got(r.g_in.at[m, s, 1 - z0], r.rs_r.at[m, 4])
        pltpu.make_async_copy(r.win.at[m, z, y], r.g_in.at[m, s, z0], r.loc.at[m, 0]).wait()
        g = r.g_in.at[m, s]
        send(g, g, r.rs_s.at[m, 7], r.rs_r.at[m, 7], xp)
        send(g, g, r.rs_s.at[m, 8], r.rs_r.at[m, 8], core)

    def rs_spread(m):
        g = r.g_in.at[m, xf]
        got(g, r.rs_r.at[m, 7])
        send(g, g, r.rs_s.at[m, 9], r.rs_r.at[m, 9], core)

        @pl.when(c == y)
        def _():
            v = r.g_out.at[m, 1 - x]
            got(v, r.rs_r.at[m, 5])
            send(v, v, r.rs_s.at[m, 10], r.rs_r.at[m, 10], core)

    def rs_end(m):
        got(r.g_in.at[m, s + 1 - 2 * c], r.rs_r.at[m, 8])
        got(r.g_in.at[m, 3 - s], r.rs_r.at[m, 9])
        sent(r.ry_in.at[m], r.rs_s.at[m, 0])
        sent(r.rz_in.at[m], r.rs_s.at[m, 2])
        sent(r.win.at[m, zf, y], r.rs_s.at[m, 4])
        for k in (7, 8, 9):
            sent(r.g_in.at[m, s], r.rs_s.at[m, k])

        @pl.when(c != y)
        def _():
            sent(r.gout.at[m], r.rs_s.at[m, 1])
            got(r.g_out.at[m, x], r.rs_r.at[m, 6])
            got(r.g_out.at[m, 1 - x], r.rs_r.at[m, 10])

        @pl.when(c == y)
        def _():
            g = r.gout.at[m, z1]
            pltpu.make_async_copy(g, r.g_out.at[m, x], r.loc.at[m, 1]).wait()
            for k in (3, 5, 6, 10):
                sent(g, r.rs_s.at[m, k])

    def feed(m, carry):
        @pl.when(m < 2)
        def _():
            w_relay_far(m + 2)

        w_fin(m)

        def tokens(g, inner):
            j = lax.div(g, 2)
            k = lax.rem(g, 2)
            w = r.win[m].reshape(D, 512)
            wo = r.wout[m].reshape(256, D)
            gu = nn(r.nta[j, k, :, 0:D], w)
            zv = gu[:, 0:256]
            uv = gu[:, 256:512]
            sg = 1.0 / (1.0 + jnp.exp(-zv))
            sw = zv * sg
            act = (sw * uv).astype(BF).astype(F32)
            dr = nt(r.cota[j, k], wo)
            gv = jnp.sum(jnp.where(lane128 == m, r.gate[g], 0.0), axis=-1, keepdims=True)
            gg = jnp.sum(act * dr, axis=-1, keepdims=True)
            r.ga[g, :, pl.ds(pl.multiple_of(m * 256, 256), 256)] = (act * gv).astype(BF)
            d = dr * gv
            dg = jnp.concatenate([d * uv * (sg * (1.0 + zv * (1.0 - sg))), d * sw], axis=1).astype(BF)
            r.dg[g] = dg
            r.acc[j, k, :, 0:D] += nt(dg, w)
            r.acc[j, k, :, D : D + 128] += jnp.where(lane128 == m, gg, 0.0)
            return inner

        lax.fori_loop(0, 8, tokens, 0)
        nta = r.nta[:, :, :, 0:D].reshape(2048, D)
        r.win[m] = tn(nta, r.dg[...].reshape(2048, 512)).astype(BF).reshape(4, 2, 96, 512)
        gam = r.ga[:, :, pl.ds(pl.multiple_of(m * 256, 256), 256)].reshape(2048, 256)
        r.gout[m] = tn(gam, r.cota[...].reshape(2048, D)).astype(BF).reshape(2, 128, D)
        rs_first(m)

        @pl.when(m >= 1)
        def _():
            rs_y(m - 1)

        @pl.when(m >= 2)
        def _():
            rs_z(m - 2)

        return carry

    for m in range(4):
        sent(r.dg.at[m, pl.ds(0, 96)], r.w_s.at[m, 0])
    lax.fori_loop(0, 4, feed, 0)

    def pack(g, carry):
        j = lax.div(g, 2)
        k = lax.rem(g, 2)
        r.nta[j, k, :, 0:D] = r.acc[j, k, :, 0:D].astype(BF)
        v = r.acc[j, k, :, D : D + 128]
        hi = v.astype(BF).astype(F32)
        r.nta[j, k, :, D : D + 128] = (hi + pltpu.roll(v - hi, 64, 1)).astype(BF)
        return carry

    lax.fori_loop(0, 8, pack, 0)
    sum_first(r.nta, r.ng_c, 0)
    sum_core(r.nta, r.ng_c, r.ng_p, 0)

    def mix(g, carry):
        j = lax.div(g, 2)
        k = lax.rem(g, 2)
        r.cota[j, k] = nn(r.ga[g], r.wout[...].reshape(1024, D)).astype(BF)
        return carry

    lax.fori_loop(0, 4, mix, 0)
    sum_relay(r.nta, r.ng_p, 0)
    lax.fori_loop(4, 8, mix, 0)
    rs_y(3)
    ngs = sum_fin(r.nta, r.ng_c, r.ng_p, 0)
    sum_first(r.cota, r.out_c, 1)

    upstream = r.cot_in[...].astype(F32)
    mid = r.mid[...]
    r2 = lax.rsqrt(jnp.mean(mid * mid, axis=-1, keepdims=True) + EPSILON)
    gg = ngs[:, D : D + 128]
    gg = gg + pltpu.roll(gg, 64, 1)
    pv = r.pown[...]
    pg = jnp.where(lane128 < 3, gg * r.sel_in[...].astype(F32), 0.0)
    lg = (pv * (pg - jnp.sum(pv * pg, axis=-1, keepdims=True))).astype(BF)
    rgrad = tn(lg, r.nown[...])
    ng = ngs[:, 0:D] + nn(lg, r.rpad[...])
    gain2 = r.mrow[4:5, :]
    fgain = jnp.sum(ng * mid * r2, axis=0, keepdims=True)
    sc = ng * gain2
    mg = upstream + r2 * sc - mid * (r2 * r2 * r2) * jnp.mean(sc * mid, axis=-1, keepdims=True)
    r.igrad[...] = mg
    r.small[...] = jnp.where(row8 < 3, rgrad[0:8, :], 0.0) + jnp.where(row8 == 4, fgain, 0.0)
    ml = mg.astype(BF)
    ow = r.ow[...].reshape(D, D)
    r.att[:, :, 128:256] = jnp.zeros((4, TOK, 128), BF)
    for i in range(4):
        da = nt(ml, ow[192 * i : 192 * i + 192, :]).astype(BF)
        r.att[i, :, 0:192] = da

        @pl.when(s != i)
        def _(i=i):
            send(r.att.at[i], r.dat.at[s], r.d_s.at[i], r.d_r.at[s], (b, i))

        @pl.when(s == i)
        def _(i=i):
            r.dat[i] = r.att[i]

    for i in range(4):
        og = tn(r.arow[i][:, 0:192], ml).astype(BF)
        og = og.reshape(2, 2, 48, D)
        for k in range(2):
            r.og[k, i] = og[:, :, :, 384 * k : 384 * k + 384]
    send(r.og.at[oc], r.og_c, r.og_s.at[0], r.og_r.at[0], core)
    sum_core(r.cota, r.out_c, r.out_p, 1)
    for i in range(4):

        @pl.when(s != i)
        def _(i=i):
            got(r.dat.at[i], r.d_r.at[i])
            sent(r.att.at[i], r.d_s.at[i])

    rs_z(2)

    for i in range(4):
        r.acc[i, 0, :, 0:QKV_PAD] = jnp.zeros((TOK, QKV_PAD), F32)
    for i in range(3, -1, -1):
        base = i * (i + 1) // 2

        def heads_back(h, carry, i=i, base=base):
            hv = lax.div(h, 2)
            here = lax.div(lane128, 64) == lax.rem(h, 2)
            vat = pl.ds(pl.multiple_of(hv * 128, 128), 128)
            cat = pl.ds(pl.multiple_of(384 + hv * 128, 128), 128)
            hat = pl.ds(pl.multiple_of(h * 128, 128), 128)
            da = jnp.where(here, r.dat[i, :, vat].astype(F32), 0.0).astype(BF)
            kqi = r.kq[h, i * TOK : i * TOK + TOK, :].astype(F32)
            qi = jnp.where(lane128 >= 64, kqi, 0.0).astype(BF)
            pf = [r.prob[h, base + j] for j in range(i + 1)]
            dp = [nt(da, r.val[hv, j * TOK : j * TOK + TOK, :]) for j in range(i + 1)]
            cen = jnp.zeros((TOK, 1), F32)
            for j in range(i + 1):
                cen = cen + jnp.sum(pf[j].astype(F32) * dp[j], axis=-1, keepdims=True)
            dq = jnp.zeros((TOK, 128), F32)
            for j in range(i + 1):
                ds = (pf[j].astype(F32) * (dp[j] - cen)).astype(BF)
                dq = dq + nn(ds, r.kq[h, j * TOK : j * TOK + TOK, :])
                r.acc[j, 0, :, hat] += tn(ds, qi)
                r.acc[j, 0, :, cat] += tn(pf[j], da)
            r.acc[i, 0, :, hat] += jnp.where(lane128 < 64, dq * 0.125, 0.0)
            return carry

        lax.fori_loop(0, 3, heads_back, 0)
        cosv = r.cos_in[i * TOK : i * TOK + TOK, :]
        sinv = r.sin_in[i * TOK : i * TOK + TOK, :]
        for h in range(3):
            g = r.acc[i, 0, :, 128 * h : 128 * h + 128].astype(BF).astype(F32)
            r.nta[i, 0, :, 128 * h : 128 * h + 128] = (g * cosv - swap_halves(g) * sinv).astype(BF)
        r.nta[i, 0, :, 384:640] = r.acc[i, 0, :, 384:640].astype(BF)
        r.ng1[i // 2, i % 2] = nt(r.nta[i, 0, :, 0:QKV_PAD], r.wq[...].reshape(D, QKV_PAD)).astype(BF)
        if i == 3:
            rs_z(3)
            got(r.og_c, r.og_r.at[0])
            for k in range(4):
                r.og[c, k] = (r.og[c, k].astype(F32) + r.og_c[k].astype(F32)).astype(BF)
            send(r.og.at[c, :, :, 1 - x], r.og_x, r.og_s.at[1], r.og_r.at[1], xp)
            sum_relay(r.cota, r.out_p, 1)
        if i == 2:
            rs_join(0)
            rs_join(1)
            got(r.og_x, r.og_r.at[1])
            for k in range(4):
                r.og[c, k, :, x] = (r.og[c, k, :, x].astype(F32) + r.og_x[k].astype(F32)).astype(BF)
            send(r.og.at[c, :, oy, x], r.og_y, r.og_s.at[2], r.og_r.at[2], yp)
            tot = sum_fin(r.cota, r.out_c, r.out_p, 1)
            r.out[...] = (r.mid[...] + tot).astype(BF)
        if i == 1:
            rs_join(2)
            rs_spread(0)
            got(r.og_y, r.og_r.at[2])
            for k in range(4):
                r.og[c, k, y, x] = (r.og[c, k, y, x].astype(F32) + r.og_y[k].astype(F32)).astype(BF)
            send(r.og.at[c, pl.ds(2 - 2 * z1, 2), y, x], r.og_z, r.og_s.at[3], r.og_r.at[3], z1p)

    ng1_c = r.ng_c.at[pl.ds(0, 2), :, pl.ds(0, D)]
    ng1_x = r.ng_p.at[0, :, pl.ds(0, D)]
    send(r.ng1.at[:, oc], ng1_c, r.n_s.at[0], r.n_r.at[0], core)
    wg = tn(r.nall[...].reshape(1024, D), r.nta[:, 0, :, 0:QKV_PAD].reshape(1024, QKV_PAD))
    r.wq[...] = wg.astype(BF).reshape(4, 2, 96, QKV_PAD)
    send(r.wq.at[:, oy], r.q_y, r.q_s.at[0], r.q_r.at[0], yp)
    got(ng1_c, r.n_r.at[0])
    for k in range(2):
        r.ng1[k, c] = (r.ng1[k, c].astype(F32) + r.ng_c[k, :, 0:D].astype(F32)).astype(BF)
    send(r.ng1.at[1 - x, c], ng1_x, r.n_s.at[1], r.n_r.at[1], xp)
    rs_join(3)
    for k in range(1, 3):
        rs_spread(k)
    got(r.og_z, r.og_r.at[3])
    for k in range(2):
        v = r.og[c, 2 * z1 + k, y, x].astype(F32) + r.og_z[k].astype(F32)
        r.og[c, 2 * z1 + k, y, x] = v.astype(BF)
    send(r.og.at[c, zf, y, x], r.og_w, r.og_s.at[4], r.og_r.at[4], z0p)

    got(ng1_x, r.n_r.at[1])
    sent(r.ng1.at[:, oc], r.n_s.at[0])
    sent(r.ng1.at[1 - x, c], r.n_s.at[1])
    ng = r.ng1[x, c].astype(F32) + r.ng_p[0, :, 0:D].astype(F32)
    xv = r.x_in[...].astype(F32)
    r1 = lax.rsqrt(jnp.mean(xv * xv, axis=-1, keepdims=True) + EPSILON)
    gain1 = r.mrow[3:4, :]
    again = jnp.sum(ng * xv * r1, axis=0, keepdims=True)
    sc = ng * gain1
    r.igrad[...] = (
        r.igrad[...] + r1 * sc - xv * (r1 * r1 * r1) * jnp.mean(sc * xv, axis=-1, keepdims=True)
    )
    r.small[...] += jnp.where(row8 == 3, again, 0.0)

    def pair_sum(k, dev):
        r.small_o[k] = r.small[...]
        send(r.small_o.at[k], r.small_i.at[k], r.sm_s.at[k], r.sm_r.at[k], dev)

    def pair_add(k):
        got(r.small_i.at[k], r.sm_r.at[k])
        r.small[...] += r.small_i[k]
        sent(r.small_o.at[k], r.sm_s.at[k])

    pair_sum(0, core)
    got(r.q_y, r.q_r.at[0])
    for k in range(4):
        r.wq[k, y] = (r.wq[k, y].astype(F32) + r.q_y[k].astype(F32)).astype(BF)
    send(r.wq.at[pl.ds(2 - 2 * z1, 2), y], r.q_z, r.q_s.at[1], r.q_r.at[1], z1p)
    pair_add(0)
    pair_sum(1, xp)
    got(r.og_w, r.og_r.at[4])
    r.og[c, z, y, x] = (r.og[c, z, y, x].astype(F32) + r.og_w[...].astype(F32)).astype(BF)
    ogf = r.og.at[c, z, y, x]
    r.g_ow[s] = r.og[c, z, y, x]
    send(ogf, r.g_ow.at[s], r.og_s.at[5], r.og_r.at[5], core)
    send(ogf, r.g_ow.at[s], r.og_s.at[6], r.og_r.at[6], xp)
    pair_add(1)
    pair_sum(2, yp)
    rs_spread(3)
    got(r.q_z, r.q_r.at[1])
    for k in range(2):
        v = r.wq[2 * z1 + k, y].astype(F32) + r.q_z[k].astype(F32)
        r.wq[2 * z1 + k, y] = v.astype(BF)
    send(r.wq.at[zf, y], r.q_w, r.q_s.at[2], r.q_r.at[2], z0p)
    pair_add(2)
    pair_sum(3, z1p)
    got(r.g_ow.at[xf], r.og_r.at[6])
    send(r.g_ow.at[xf], r.g_ow.at[xf], r.og_s.at[7], r.og_r.at[7], core)
    got(r.q_w, r.q_r.at[2])
    r.wq[z, y] = (r.wq[z, y].astype(F32) + r.q_w[...].astype(F32)).astype(BF)
    r.g_q[s] = r.wq[z, y]
    send(r.wq.at[z, y], r.g_q.at[s], r.q_s.at[3], r.q_r.at[3], xp)
    send(r.wq.at[z, y], r.g_q.at[s], r.q_s.at[4], r.q_r.at[4], core)
    pair_add(3)
    pair_sum(4, z0p)
    for m in range(4):
        rs_end(m)
    got(r.g_q.at[xf], r.q_r.at[3])
    send(r.g_q.at[xf], r.g_q.at[xf], r.q_s.at[5], r.q_r.at[5], core)
    pair_add(4)
    r.g_small[...] = r.small[...]
    got(r.g_ow.at[s + 1 - 2 * c], r.og_r.at[5])
    got(r.g_ow.at[3 - s], r.og_r.at[7])
    got(r.g_q.at[s + 1 - 2 * c], r.q_r.at[4])
    got(r.g_q.at[3 - s], r.q_r.at[5])
    sent(r.og_c, r.og_s.at[0])
    sent(r.og_x, r.og_s.at[1])
    sent(r.og_y, r.og_s.at[2])
    sent(r.og_z, r.og_s.at[3])
    sent(r.og_w, r.og_s.at[4])
    for k in (5, 6, 7):
        sent(r.g_ow.at[0], r.og_s.at[k])
    sent(r.q_y, r.q_s.at[0])
    sent(r.q_z, r.q_s.at[1])
    for k in (2, 3, 4, 5):
        sent(r.q_w, r.q_s.at[k])


def vmem(shape, kind=BF):
    return pltpu.VMEM(shape, kind)


def layer_call(ins, cos_table, sin_table):
    dma = pltpu.SemaphoreType.DMA
    in_names = (
        ["x_in", "cot_in", "wq_in", "misc_in", "ow_in", "sel_in", "cos_in", "sin_in"]
        + ["e_in", "e_out", "s_in", "s_out"]
    )
    out_names = ["out", "igrad", "g_small", "g_q", "g_ow", "g_in", "g_out"]
    out_shapes = (
        ((TOK, D), BF),
        ((TOK, D), F32),
        ((8, D), F32),
        ((4, 96, QKV_PAD), BF),
        ((4, 48, 384), BF),
        ((4, 4, 2, 96, 512), BF),
        ((4, 2, 128, D), BF),
    )
    scratch = {
        "nall": vmem((4, TOK, D)),
        "wq": vmem((4, 2, 96, QKV_PAD)),
        "misc": vmem((4, 2, 8, 128), F32),
        "ow": vmem((4, 2, 2, 48, D)),
        "kq": vmem((3, 1024, 128)),
        "val": vmem((2, 1024, 128)),
        "prob": vmem((3, 10, TOK, TOK)),
        "att": vmem((4, TOK, 256)),
        "arow": vmem((4, TOK, 256)),
        "dat": vmem((4, TOK, 256)),
        "mid": vmem((TOK, D), F32),
        "nown": vmem((TOK, D)),
        "pown": vmem((TOK, 128), F32),
        "mrow": vmem((8, D), F32),
        "rpad": vmem((128, D)),
        "nta": vmem((4, 2, TOK, D + 128)),
        "cota": vmem((4, 2, TOK, D)),
        "gate": vmem((8, TOK, 128), F32),
        "win": vmem((4, 4, 2, 96, 512)),
        "wout": vmem((4, 2, 128, D)),
        "dg": vmem((8, TOK, 512)),
        "ga": vmem((8, TOK, 1024)),
        "acc": vmem((4, 2, TOK, D + 128), F32),
        "gout": vmem((4, 2, 128, D)),
        "ry_in": vmem((4, 4, 96, 512)),
        "ry_out": vmem((4, 2, 128, D)),
        "rz_in": vmem((4, 2, 96, 512)),
        "rz_out": vmem((4, 128, D)),
        "ng_c": vmem((4, TOK, D + 128)),
        "ng_p": vmem((3, TOK, D + 128)),
        "out_c": vmem((4, TOK, D)),
        "out_p": vmem((3, TOK, D)),
        "ng1": vmem((2, 2, TOK, D)),
        "og": vmem((2, 4, 2, 2, 48, 384)),
        "og_c": vmem((4, 2, 2, 48, 384)),
        "og_x": vmem((4, 2, 48, 384)),
        "og_y": vmem((4, 48, 384)),
        "og_z": vmem((2, 48, 384)),
        "og_w": vmem((48, 384)),
        "q_y": vmem((4, 96, QKV_PAD)),
        "q_z": vmem((2, 96, QKV_PAD)),
        "q_w": vmem((96, QKV_PAD)),
        "small": vmem((8, D), F32),
        "small_o": vmem((5, 8, D), F32),
        "small_i": vmem((5, 8, D), F32),
        "stage_sem": dma((4, 9)),
        "att_s": dma((3, 7)),
        "att_r": dma((3, 8)),
        "w_s": dma((4, 7)),
        "w_r": dma((4, 8)),
        "o_s": dma((4, 3)),
        "o_r": dma((4, 2)),
        "ow_s": dma((1,)),
        "ow_r": dma((1,)),
        "x_s": dma((3,)),
        "x_r": dma((3,)),
        "tok_s": dma((2, 7)),
        "tok_r": dma((2, 7)),
        "a_s": dma((4,)),
        "a_r": dma((4,)),
        "d_s": dma((4,)),
        "d_r": dma((4,)),
        "sum_s": dma((2, 4)),
        "sum_r": dma((2, 4)),
        "rs_s": dma((4, 11)),
        "rs_r": dma((4, 11)),
        "loc": dma((4, 2)),
        "og_s": dma((8,)),
        "og_r": dma((8,)),
        "q_s": dma((6,)),
        "q_r": dma((6,)),
        "n_s": dma((2,)),
        "n_r": dma((2,)),
        "sm_s": dma((5,)),
        "sm_r": dma((5,)),
    }
    names = in_names + out_names + list(scratch)
    in_vmem = pl.BlockSpec(memory_space=pltpu.VMEM)
    in_any = pl.BlockSpec(memory_space=pl.ANY)
    return pl.pallas_call(
        functools.partial(layer_kernel, names),
        out_shape=[jax.ShapeDtypeStruct(*one) for one in out_shapes],
        in_specs=[in_vmem] * 8 + [in_any] * 4,
        out_specs=[in_vmem] * 5 + [in_any] * 2,
        scratch_shapes=list(scratch.values()),
        compiler_params=pltpu.CompilerParams(
            collective_id=0, has_side_effects=True, vmem_limit_bytes=VMEM_LIMIT
        ),
        cost_estimate=pl.CostEstimate(
            flops=35_000_000_000, bytes_accessed=60_000_000, transcendentals=6_000_000
        ),
        name="layer",
    )(*ins[:6], cos_table, sin_table, *ins[6:])


def fast_device(
    inputs,
    attn_gain,
    qkv_weight,
    out_weight,
    ffn_gain,
    router_weight,
    expert_in,
    expert_out,
    shared_in,
    shared_out,
    routes,
    slot_index,
    cotangent,
):
    b = lax.axis_index("dp")
    s = lax.axis_index("seq")
    c = s % 2
    mine = lax.dynamic_slice_in_dim(qkv_weight, 3 * s, 3, axis=1).astype(BF)
    pairs = mine[:, :, 0:2].reshape(96, 384)
    values = mine[:, :, 2].reshape(96, 192)
    wq = jnp.concatenate([pairs, values, jnp.zeros((96, 64), BF)], axis=1)
    misc = jnp.concatenate(
        [router_weight.T, attn_gain[None], ffn_gain[None], jnp.zeros((3, 96), F32)], axis=0
    )
    misc = jnp.pad(misc.astype(BF).astype(F32), ((0, 0), (0, 32)))
    half = lax.dynamic_slice_in_dim(out_weight, 48 * c, 48, axis=0).astype(BF)
    lane = jnp.arange(128, dtype=jnp.int32)
    route = routes[0]
    sel = (lane == route[:, 0:1]) | (lane == route[:, 1:2]) | (lane == 3)
    sel = sel.astype(BF)
    angle = np.arange(1024, dtype=np.float32)[:, None] * (
        np.float32(10000.0) ** (-np.arange(32, dtype=np.float32) / np.float32(32))
    )
    cos_table = jnp.asarray(np.tile(np.cos(angle), (1, 4)).astype(np.float32))
    sine = np.sin(angle)
    sin_table = jnp.asarray(np.tile(np.concatenate([-sine, sine], 1), (1, 2)).astype(np.float32))
    out, igrad, small, g_q, g_ow, g_in, g_out = layer_call(
        (
            inputs[0],
            cotangent[0],
            wq,
            misc,
            half,
            sel,
            expert_in,
            expert_out,
            shared_in,
            shared_out,
        ),
        cos_table,
        sin_table,
    )
    shard = lax.dynamic_slice_in_dim(small, 96 * b, 96, axis=1)
    pairs = g_q[:, :, 0:384].reshape(4, 96, 3, 2, 64)
    values = g_q[:, :, 384:576].reshape(4, 96, 3, 1, 64)
    qkv_grad = jnp.concatenate([pairs, values], axis=3).transpose(1, 0, 2, 3, 4)
    qkv_grad = qkv_grad.reshape(96, HEADS, 3, HEAD_DIM).astype(F32)
    ow_grad = g_ow.reshape(2, 2, 48, 384).transpose(0, 2, 1, 3).reshape(96, D).astype(F32)
    g = g_in.reshape(4, 2, 2, 2, 96, 2, 2, 128).transpose(0, 4, 5, 6, 3, 2, 1, 7)
    g = g.reshape(4, 96, 2 * FF).astype(F32)
    go = g_out.reshape(4, 256, D).astype(F32)
    return (
        out[None],
        igrad[None],
        shard[3],
        qkv_grad,
        ow_grad,
        shard[4],
        shard[0:3].T,
        g[:3],
        go[:3],
        g[3],
        go[3],
    )


def solution(mesh):
    fits = mesh.shape["dp"] == 8 and mesh.shape["seq"] == 4
    return jax.shard_map(
        fast_device if fits else on_device,
        mesh=mesh,
        in_specs=(
            P("dp", "seq", None),
            P("dp"),
            P("dp", None, None, None),
            P("dp", None),
            P("dp"),
            P("dp", None),
            P(None, "dp", None),
            P(None, "dp", None),
            P("dp", None),
            P("dp", None),
            P("dp", "seq", None),
            P("dp", "seq", None),
            P("dp", "seq", None),
        ),
        out_specs=(
            P("dp", "seq", None),
            P("dp", "seq", None),
            P("dp"),
            P("dp", None, None, None),
            P("dp", None),
            P("dp"),
            P("dp", None),
            P(None, "dp", None),
            P(None, "dp", None),
            P("dp", None),
            P("dp", None),
        ),
        check_vma=False,
    )
```

```python
import functools
import types

import jax
import jax.numpy as jnp
import numpy as np
from jax import lax
from jax.experimental import pallas as pl
from jax.experimental.pallas import tpu as pltpu
from jax.sharding import PartitionSpec as P

D = 768
HEADS = 12
HEAD_DIM = 64
FF = 2048
EXPERTS = 3
TOP = 2
ATT_BLOCK = 256
CAP = 192


EPSILON = 1e-05
VMEM_LIMIT = 66_000_000


def rotary_tables(positions):
    half_dim = HEAD_DIM // 2
    frequency = 10000.0 ** (-jnp.arange(half_dim, dtype=jnp.float32) / half_dim)
    angles = positions.astype(jnp.float32)[:, None] * frequency[None, :]
    return (jnp.cos(angles), jnp.sin(angles))


def rotate(values, cos_table, sine_table):
    half_dim = values.shape[-1] // 2
    first_half = values[..., :half_dim]
    second_half = values[..., half_dim:]
    cos_heads = cos_table[:, None, :]
    sine_heads = sine_table[:, None, :]
    return jnp.concatenate(
        [
            first_half * cos_heads - second_half * sine_heads,
            second_half * cos_heads + first_half * sine_heads,
        ],
        axis=-1,
    )


def unrotate(values, cos_table, sine_table):
    half_dim = values.shape[-1] // 2
    first_half = values[..., :half_dim]
    second_half = values[..., half_dim:]
    cos_heads = cos_table[:, None, :]
    sine_heads = sine_table[:, None, :]
    return jnp.concatenate(
        [
            first_half * cos_heads + second_half * sine_heads,
            second_half * cos_heads - first_half * sine_heads,
        ],
        axis=-1,
    )


def silu_grads(gate_in, up_in, upstream):
    sigmoid = jax.nn.sigmoid(gate_in)
    swish = gate_in * sigmoid
    slope = sigmoid * (1.0 + gate_in * (1.0 - sigmoid))
    return jnp.concatenate([upstream * up_in * slope, upstream * swish], axis=-1)


def block_mask(row_start, block_rows, length):
    query_block = (row_start + jnp.arange(block_rows, dtype=jnp.int32)) // ATT_BLOCK
    key_block = jnp.arange(length, dtype=jnp.int32) // ATT_BLOCK
    return key_block[None, :] <= query_block[:, None]


def attend_heads(received):
    packed = received[:, 0]
    length = packed.shape[0]
    heads_here = packed.shape[1]
    queries = packed[..., :HEAD_DIM]
    keys_all = packed[..., HEAD_DIM : 2 * HEAD_DIM]
    values_all = packed[..., 2 * HEAD_DIM :]
    block_rows = min(512, length)
    block_count = length // block_rows
    score_scale = HEAD_DIM ** (-0.5)

    def one_block(element):
        query_rows, row_start = element
        scores = (
            jnp.einsum("qhe,khe->hqk", query_rows, keys_all, preferred_element_type=jnp.float32)
            * score_scale
        )
        scores = jnp.where(block_mask(row_start, block_rows, length)[None], scores, -1e30)
        largest = jnp.max(scores, axis=-1, keepdims=True)
        weights_exp = jnp.exp(scores - largest)
        totals = jnp.sum(weights_exp, axis=-1, keepdims=True)
        attn_probs = (weights_exp / totals).astype(jnp.bfloat16)
        mixed_rows = jnp.einsum(
            "hqk,khe->qhe", attn_probs, values_all, preferred_element_type=jnp.float32
        )
        log_total = (largest + jnp.log(totals))[..., 0]
        return (mixed_rows.astype(jnp.bfloat16), jnp.transpose(log_total))

    blocked = queries.reshape(block_count, block_rows, heads_here, HEAD_DIM)
    starts = jnp.arange(block_count, dtype=jnp.int32) * block_rows
    mixed_rows, log_total = lax.map(one_block, (blocked, starts))
    return (
        mixed_rows.reshape(length, 1, heads_here, HEAD_DIM),
        log_total.reshape(length, 1, heads_here),
        received,
    )


def attend_back(received, log_sum, grad_in):
    packed = received[:, 0]
    length = packed.shape[0]
    heads_here = packed.shape[1]
    queries = packed[..., :HEAD_DIM]
    keys_all = packed[..., HEAD_DIM : 2 * HEAD_DIM]
    values_all = packed[..., 2 * HEAD_DIM :]
    block_rows = min(512, length)
    block_count = length // block_rows
    score_scale = HEAD_DIM ** (-0.5)

    def one_block(running, element):
        key_acc, value_acc = running
        query_rows, grad_rows, log_rows, row_start = element
        scores = (
            jnp.einsum("qhe,khe->hqk", query_rows, keys_all, preferred_element_type=jnp.float32)
            * score_scale
        )
        scores = jnp.where(block_mask(row_start, block_rows, length)[None], scores, -1e30)
        attn_probs = jnp.exp(scores - jnp.transpose(log_rows)[:, :, None])
        value_acc = value_acc + jnp.einsum(
            "hqk,qhe->khe",
            attn_probs.astype(jnp.bfloat16),
            grad_rows,
            preferred_element_type=jnp.float32,
        )
        grad_probs = jnp.einsum(
            "qhe,khe->hqk", grad_rows, values_all, preferred_element_type=jnp.float32
        )
        centre = jnp.sum(attn_probs * grad_probs, axis=-1, keepdims=True)
        grad_scores = (attn_probs * (grad_probs - centre)).astype(jnp.bfloat16)
        query_grad = (
            jnp.einsum("hqk,khe->qhe", grad_scores, keys_all, preferred_element_type=jnp.float32)
            * score_scale
        )
        key_acc = key_acc + jnp.einsum(
            "hqk,qhe->khe", grad_scores, query_rows, preferred_element_type=jnp.float32
        )
        return ((key_acc, value_acc), query_grad)

    empty_acc = jnp.zeros((length, heads_here, HEAD_DIM), jnp.float32)
    blocked_query = queries.reshape(block_count, block_rows, heads_here, HEAD_DIM)
    blocked_grad = grad_in[:, 0].reshape(block_count, block_rows, heads_here, HEAD_DIM)
    blocked_log = log_sum[:, 0].reshape(block_count, block_rows, heads_here)
    starts = jnp.arange(block_count, dtype=jnp.int32) * block_rows
    (key_acc, value_acc), query_grads = lax.scan(
        one_block, (empty_acc, empty_acc), (blocked_query, blocked_grad, blocked_log, starts)
    )
    stacked = jnp.stack(
        [query_grads.reshape(length, heads_here, HEAD_DIM), key_acc * score_scale, value_acc],
        axis=2,
    )
    return stacked.astype(jnp.bfloat16).reshape(length, 1, heads_here, 3 * HEAD_DIM)


def norm_back(values, scale_rows, gain_row, upstream):
    scaled = upstream * gain_row
    gain_term = jnp.sum(upstream * values * scale_rows, axis=0)
    value_grad = scale_rows * scaled - values * scale_rows**3 * jnp.mean(
        scaled * values, axis=-1, keepdims=True
    )
    return (gain_term, value_grad)


def on_device(
    inputs,
    attn_gain,
    qkv_weight,
    out_weight,
    ffn_gain,
    router_weight,
    expert_in,
    expert_out,
    shared_in,
    shared_out,
    routes,
    slot_index,
    cotangent,
):
    tok_rows = inputs.shape[1]
    group_count = lax.axis_size("seq")
    heads_group = HEADS // group_count
    stream = inputs[0].astype(jnp.float32)
    attn_local = (
        attn_gain.astype(jnp.bfloat16),
        qkv_weight.astype(jnp.bfloat16),
        out_weight.astype(jnp.bfloat16),
    )
    attn_full = (
        lax.all_gather(attn_local[0], "dp", axis=0, tiled=True),
        lax.all_gather(attn_local[1], "dp", axis=0, tiled=True),
        lax.all_gather(attn_local[2], "dp", axis=0, tiled=True),
    )
    gain_first, qkv_full, out_full = attn_full
    positions = lax.axis_index("seq") * tok_rows + jnp.arange(tok_rows, dtype=jnp.int32)
    cos_table, sine_table = rotary_tables(positions)
    scale_one = lax.rsqrt(jnp.mean(stream * stream, axis=-1, keepdims=True) + EPSILON)
    gain_one_f = gain_first.astype(jnp.float32)
    normed = (stream * scale_one * gain_one_f).astype(jnp.bfloat16)
    projected = jnp.einsum("td,dhce->thce", normed, qkv_full, preferred_element_type=jnp.float32)
    rotated = jnp.stack(
        [
            rotate(projected[:, :, 0], cos_table, sine_table),
            rotate(projected[:, :, 1], cos_table, sine_table),
            projected[:, :, 2],
        ],
        axis=2,
    ).astype(jnp.bfloat16)
    outgoing = rotated.reshape(tok_rows, group_count, heads_group, 3 * HEAD_DIM)
    head_out, log_sum, head_qkv = attend_heads(
        lax.all_to_all(outgoing, "seq", split_axis=1, concat_axis=0, tiled=True)
    )
    attended = lax.all_to_all(head_out, "seq", split_axis=0, concat_axis=1, tiled=True).reshape(
        tok_rows, D
    )
    middle = stream + jnp.dot(attended, out_full, preferred_element_type=jnp.float32)
    ffn_local = (
        ffn_gain.astype(jnp.bfloat16),
        router_weight.astype(jnp.bfloat16),
        expert_in.astype(jnp.bfloat16),
        expert_out.astype(jnp.bfloat16),
        shared_in.astype(jnp.bfloat16),
        shared_out.astype(jnp.bfloat16),
    )
    ffn_full = (
        lax.all_gather(ffn_local[0], "dp", axis=0, tiled=True),
        lax.all_gather(ffn_local[1], "dp", axis=0, tiled=True),
        lax.all_gather(ffn_local[2], "dp", axis=1, tiled=True),
        lax.all_gather(ffn_local[3], "dp", axis=1, tiled=True),
        lax.all_gather(ffn_local[4], "dp", axis=0, tiled=True),
        lax.all_gather(ffn_local[5], "dp", axis=0, tiled=True),
    )
    gain_second, router_full, exp_in_full, exp_out_full, sh_in_full, sh_out_full = ffn_full
    scale_two = lax.rsqrt(jnp.mean(middle * middle, axis=-1, keepdims=True) + EPSILON)
    gain_two_f = gain_second.astype(jnp.float32)
    normed_two = (middle * scale_two * gain_two_f).astype(jnp.bfloat16)
    logits = jnp.dot(normed_two, router_full, preferred_element_type=jnp.float32)
    router_probs = jax.nn.softmax(logits, axis=-1)
    route_rows = routes[0]
    choice_hot = (
        route_rows[:, :, None] == jnp.arange(EXPERTS, dtype=jnp.int32)[None, None, :]
    ).astype(jnp.float32)
    gate_values = jnp.sum(choice_hot * router_probs[:, None, :], axis=-1)
    flat_slot = (route_rows * CAP + slot_index[0]).reshape(-1)
    buffer = (
        jnp.zeros((EXPERTS * CAP, D), jnp.bfloat16)
        .at[flat_slot]
        .set(jnp.repeat(normed_two, TOP, axis=0))
        .reshape(EXPERTS, CAP, D)
    )
    gate_up = jnp.einsum("ecd,edf->ecf", buffer, exp_in_full, preferred_element_type=jnp.float32)
    activated = (jax.nn.silu(gate_up[..., :FF]) * gate_up[..., FF:]).astype(jnp.bfloat16)
    expert_rows = jnp.einsum(
        "ecf,efd->ecd", activated, exp_out_full, preferred_element_type=jnp.float32
    ).reshape(EXPERTS * CAP, D)
    picked = expert_rows[flat_slot].reshape(tok_rows, TOP, D)
    mixture = jnp.sum(gate_values[:, :, None] * picked, axis=1)
    shared_gu = jnp.dot(normed_two, sh_in_full, preferred_element_type=jnp.float32)
    shared_act = (jax.nn.silu(shared_gu[:, :FF]) * shared_gu[:, FF:]).astype(jnp.bfloat16)
    result = middle + mixture + jnp.dot(shared_act, sh_out_full, preferred_element_type=jnp.float32)
    output = result.astype(jnp.bfloat16)[None]
    ffn_back = (
        lax.all_gather(ffn_local[0], "dp", axis=0, tiled=True),
        lax.all_gather(ffn_local[1], "dp", axis=0, tiled=True),
        lax.all_gather(ffn_local[2], "dp", axis=1, tiled=True),
        lax.all_gather(ffn_local[3], "dp", axis=1, tiled=True),
        lax.all_gather(ffn_local[4], "dp", axis=0, tiled=True),
        lax.all_gather(ffn_local[5], "dp", axis=0, tiled=True),
    )
    router_back, exp_in_back, exp_out_back, sh_in_back, sh_out_back = (
        ffn_back[1],
        ffn_back[2],
        ffn_back[3],
        ffn_back[4],
        ffn_back[5],
    )
    upstream = cotangent[0].astype(jnp.float32)
    grad_low = upstream.astype(jnp.bfloat16)
    shared_out_grad = jnp.einsum(
        "tf,td->fd", shared_act, grad_low, preferred_element_type=jnp.float32
    )
    shared_act_grad = jnp.einsum(
        "td,fd->tf", grad_low, sh_out_back, preferred_element_type=jnp.float32
    )
    shared_gu_grad = silu_grads(shared_gu[:, :FF], shared_gu[:, FF:], shared_act_grad).astype(
        jnp.bfloat16
    )
    shared_in_grad = jnp.einsum(
        "td,tf->df", normed_two, shared_gu_grad, preferred_element_type=jnp.float32
    )
    norm_grad_two = jnp.einsum(
        "tf,df->td", shared_gu_grad, sh_in_back, preferred_element_type=jnp.float32
    )
    slot_terms = (gate_values[:, :, None] * upstream[:, None, :]).reshape(tok_rows * TOP, D)
    slot_grad = (
        jnp.zeros((EXPERTS * CAP, D), jnp.float32)
        .at[flat_slot]
        .set(slot_terms)
        .astype(jnp.bfloat16)
        .reshape(EXPERTS, CAP, D)
    )
    expert_out_grad = jnp.einsum(
        "ecf,ecd->efd", activated, slot_grad, preferred_element_type=jnp.float32
    )
    activated_grad = jnp.einsum(
        "ecd,efd->ecf", slot_grad, exp_out_back, preferred_element_type=jnp.float32
    )
    gate_up_grad = silu_grads(gate_up[..., :FF], gate_up[..., FF:], activated_grad).astype(
        jnp.bfloat16
    )
    expert_in_grad = jnp.einsum(
        "ecd,ecf->edf", buffer, gate_up_grad, preferred_element_type=jnp.float32
    )
    buffer_grad = jnp.einsum(
        "ecf,edf->ecd", gate_up_grad, exp_in_back, preferred_element_type=jnp.float32
    ).reshape(EXPERTS * CAP, D)
    norm_grad_two = norm_grad_two + jnp.sum(
        buffer_grad[flat_slot].reshape(tok_rows, TOP, D), axis=1
    )
    gate_grad = jnp.sum(upstream[:, None, :] * picked, axis=-1)
    prob_grad = jnp.sum(choice_hot * gate_grad[:, :, None], axis=1)
    logit_grad = (
        router_probs * (prob_grad - jnp.sum(router_probs * prob_grad, axis=-1, keepdims=True))
    ).astype(jnp.bfloat16)
    router_weight_grad = jnp.einsum(
        "td,te->de", normed_two, logit_grad, preferred_element_type=jnp.float32
    )
    norm_grad_two = norm_grad_two + jnp.einsum(
        "te,de->td", logit_grad, router_back, preferred_element_type=jnp.float32
    )
    ffn_gain_term, middle_part = norm_back(middle, scale_two, gain_two_f, norm_grad_two)
    middle_grad = upstream + middle_part
    attn_back = (
        lax.all_gather(attn_local[0], "dp", axis=0, tiled=True),
        lax.all_gather(attn_local[1], "dp", axis=0, tiled=True),
        lax.all_gather(attn_local[2], "dp", axis=0, tiled=True),
    )
    qkv_back, out_back = (attn_back[1], attn_back[2])
    middle_low = middle_grad.astype(jnp.bfloat16)
    out_weight_grad = jnp.einsum(
        "tf,td->fd", attended, middle_low, preferred_element_type=jnp.float32
    )
    attended_grad = jnp.einsum(
        "td,fd->tf", middle_low, out_back, preferred_element_type=jnp.float32
    ).astype(jnp.bfloat16)
    head_grad = lax.all_to_all(
        attended_grad.reshape(tok_rows, group_count, heads_group, HEAD_DIM),
        "seq",
        split_axis=1,
        concat_axis=0,
        tiled=True,
    )
    stacked = attend_back(head_qkv, log_sum, head_grad)
    returned = (
        lax.all_to_all(stacked, "seq", split_axis=0, concat_axis=1, tiled=True)
        .reshape(tok_rows, HEADS, 3, HEAD_DIM)
        .astype(jnp.float32)
    )
    projected_grad = jnp.stack(
        [
            unrotate(returned[:, :, 0], cos_table, sine_table),
            unrotate(returned[:, :, 1], cos_table, sine_table),
            returned[:, :, 2],
        ],
        axis=2,
    ).astype(jnp.bfloat16)
    qkv_weight_grad = jnp.einsum(
        "td,thce->dhce", normed, projected_grad, preferred_element_type=jnp.float32
    )
    norm_grad = jnp.einsum(
        "thce,dhce->td", projected_grad, qkv_back, preferred_element_type=jnp.float32
    )
    attn_gain_term, input_part = norm_back(stream, scale_one, gain_one_f, norm_grad)
    input_grad = (middle_grad + input_part)[None]
    parts = (
        lax.psum_scatter(
            qkv_weight_grad.astype(jnp.bfloat16), "seq", scatter_dimension=1, tiled=True
        ).astype(jnp.float32),
        lax.psum_scatter(
            out_weight_grad.astype(jnp.bfloat16), "seq", scatter_dimension=1, tiled=True
        ).astype(jnp.float32),
        lax.psum_scatter(
            expert_in_grad.astype(jnp.bfloat16), "seq", scatter_dimension=2, tiled=True
        ).astype(jnp.float32),
        lax.psum_scatter(
            expert_out_grad.astype(jnp.bfloat16), "seq", scatter_dimension=2, tiled=True
        ).astype(jnp.float32),
        lax.psum_scatter(
            shared_in_grad.astype(jnp.bfloat16), "seq", scatter_dimension=1, tiled=True
        ).astype(jnp.float32),
        lax.psum_scatter(
            shared_out_grad.astype(jnp.bfloat16), "seq", scatter_dimension=1, tiled=True
        ).astype(jnp.float32),
    )
    owned = (
        lax.psum_scatter(attn_gain_term, "dp", scatter_dimension=0, tiled=True),
        lax.psum_scatter(ffn_gain_term, "dp", scatter_dimension=0, tiled=True),
        lax.psum_scatter(router_weight_grad, "dp", scatter_dimension=0, tiled=True),
        lax.psum_scatter(parts[0], "dp", scatter_dimension=0, tiled=True),
        lax.psum_scatter(parts[1], "dp", scatter_dimension=0, tiled=True),
        lax.psum_scatter(parts[2], "dp", scatter_dimension=1, tiled=True),
        lax.psum_scatter(parts[3], "dp", scatter_dimension=1, tiled=True),
        lax.psum_scatter(parts[4], "dp", scatter_dimension=0, tiled=True),
        lax.psum_scatter(parts[5], "dp", scatter_dimension=0, tiled=True),
    )
    small = lax.psum((owned[0], owned[1], owned[2]), "seq")
    joined = (
        lax.all_gather(owned[3].astype(jnp.bfloat16), "seq", axis=1, tiled=True).astype(
            jnp.float32
        ),
        lax.all_gather(owned[4].astype(jnp.bfloat16), "seq", axis=1, tiled=True).astype(
            jnp.float32
        ),
        lax.all_gather(owned[5].astype(jnp.bfloat16), "seq", axis=2, tiled=True).astype(
            jnp.float32
        ),
        lax.all_gather(owned[6].astype(jnp.bfloat16), "seq", axis=2, tiled=True).astype(
            jnp.float32
        ),
        lax.all_gather(owned[7].astype(jnp.bfloat16), "seq", axis=1, tiled=True).astype(
            jnp.float32
        ),
        lax.all_gather(owned[8].astype(jnp.bfloat16), "seq", axis=1, tiled=True).astype(
            jnp.float32
        ),
    )
    return (
        output,
        input_grad,
        small[0],
        joined[0],
        joined[1],
        small[1],
        small[2],
        joined[2],
        joined[3],
        joined[4],
        joined[5],
    )


MESH = pl.DeviceIdType.MESH
BF = jnp.bfloat16
F32 = jnp.float32
TOK = ATT_BLOCK
QKV_PAD = 640


def nn(a, b):
    return lax.dot_general(a, b, (((1,), (0,)), ((), ())), preferred_element_type=F32)


def nt(a, b):
    return lax.dot_general(a, b, (((1,), (1,)), ((), ())), preferred_element_type=F32)


def tn(a, b):
    return lax.dot_general(a, b, (((0,), (0,)), ((), ())), preferred_element_type=F32)


def swap_halves(v):
    lane = lax.broadcasted_iota(jnp.int32, v.shape, 1)
    return jnp.where(lax.rem(lane, 64) < 32, pltpu.roll(v, 96, 1), pltpu.roll(v, 32, 1))


def layer_kernel(names, *refs):
    r = types.SimpleNamespace(**dict(zip(names, refs)))
    b = lax.axis_index("dp")
    s = lax.axis_index("seq")
    z = lax.div(b, 2)
    y = lax.rem(b, 2)
    z1 = lax.div(b, 4)
    z0 = lax.rem(z, 2)
    x = lax.div(s, 2)
    c = lax.rem(s, 2)
    zf = z + 1 - 2 * z0
    zg = z + 2 - 4 * z1
    zh = zf + 2 - 4 * z1
    core = (b, s + 1 - 2 * c)
    xp = (b, s + 2 - 4 * x)
    diag = (b, 3 - s)
    yp = (b + 1 - 2 * y, s)
    z0p = (b + 2 - 4 * z0, s)
    z1p = (b + 4 - 8 * z1, s)
    p1 = (b + c * (2 - 4 * z0), s + (1 - c) * (2 - 4 * x))
    p2 = (b + (1 - c) * (2 - 4 * z0), s + c * (2 - 4 * x))
    jme = z0 * 2 + x
    jx = z0 * 2 + 1 - x
    jz = (1 - z0) * 2 + x
    jd = (1 - z0) * 2 + 1 - x
    jp1 = jx + c * (jz - jx)
    jp2 = jz + c * (jx - jz)
    oc = 1 - c
    oy = 1 - y

    def send(src, dst, ss, rs, dev):
        pltpu.make_async_remote_copy(
            src_ref=src, dst_ref=dst, send_sem=ss, recv_sem=rs, device_id=dev, device_id_type=MESH
        ).start()

    def sent(src, ss):
        pltpu.make_async_remote_copy(
            src_ref=src, dst_ref=src, send_sem=ss, recv_sem=ss, device_id=core, device_id_type=MESH
        ).wait_send()

    def got(dst, rs):
        pltpu.make_async_remote_copy(
            src_ref=dst, dst_ref=dst, send_sem=rs, recv_sem=rs, device_id=core, device_id_type=MESH
        ).wait_recv()

    def ag_first(src, slot, ss, rs):
        send(src, slot(z, y), ss(0), rs(b), z0p)

    def ag_own(slot, ss, rs):
        send(slot(z, y), slot(z, y), ss(1), rs(b), z1p)
        send(slot(z, y), slot(z, y), ss(2), rs(b), yp)

    def ag_z0(slot, ss, rs):
        k = 2 * zf + y
        got(slot(zf, y), rs(k))
        send(slot(zf, y), slot(zf, y), ss(3), rs(k), z1p)
        send(slot(zf, y), slot(zf, y), ss(4), rs(k), yp)

    def ag_z1(slot, ss, rs):
        for zz, n in ((zg, 5), (zh, 6)):
            k = 2 * zz + y
            got(slot(zz, y), rs(k))
            send(slot(zz, y), slot(zz, y), ss(n), rs(k), yp)

    def ag_fin(slot, rs):
        for zz in range(4):
            got(slot(zz, oy), rs(2 * zz + oy))

    def ag_sent(src, slot, ss):
        sent(src, ss(0))
        for n in range(1, 7):
            sent(slot(z, y), ss(n))

    def tok_own(slot, n):
        own = slot(jme, c)
        send(own, own, r.tok_s.at[n, 1], r.tok_r.at[n, 2], p1)
        send(own, own, r.tok_s.at[n, 2], r.tok_r.at[n, 4], p2)
        send(own, own, r.tok_s.at[n, 0], r.tok_r.at[n, 1], core)

    def tok_near(slot, n):
        v = slot(jp1, c)
        got(v, r.tok_r.at[n, 2])
        send(v, v, r.tok_s.at[n, 3], r.tok_r.at[n, 6], p2)
        send(v, v, r.tok_s.at[n, 4], r.tok_r.at[n, 5], core)
        v = slot(jp2, c)
        got(v, r.tok_r.at[n, 4])
        send(v, v, r.tok_s.at[n, 5], r.tok_r.at[n, 3], core)

    def tok_far(slot, n):
        v = slot(jd, c)
        got(v, r.tok_r.at[n, 6])
        send(v, v, r.tok_s.at[n, 6], r.tok_r.at[n, 7], core)

    def tok_fin(slot, n):
        got(slot(jme, oc), r.tok_r.at[n, 1])
        got(slot(jp1, oc), r.tok_r.at[n, 3])
        got(slot(jp2, oc), r.tok_r.at[n, 5])
        got(slot(jd, oc), r.tok_r.at[n, 7])

    def tok_sent(slot, n):
        for k in range(7):
            sent(slot(jme, c), r.tok_s.at[n, k])

    cot_slot = lambda j, k: r.cota.at[j, k]
    sel_slot = lambda j, k: r.nta.at[j, k, :, pl.ds(D, 128)]
    two_slot = lambda j, k: r.nta.at[j, k, :, pl.ds(0, D)]

    def block_at(q):
        q1 = lax.rem(q, 2)
        q2 = lax.div(q, 2)
        fx = q1 + c * (q2 - q1)
        fz = q2 + c * (q1 - q2)
        return 2 * (z0 + fz * (1 - 2 * z0)) + x + fx * (1 - 2 * x)

    def sum_first(buf, rc, n):
        send(buf.at[:, oc], rc, r.sum_s.at[n, 0], r.sum_r.at[n, 0], core)

    def sum_core(buf, rc, rp, n):
        got(rc, r.sum_r.at[n, 0])
        for j in range(4):
            v = buf[j, c].astype(F32) + rc[j].astype(F32)
            buf[j, c] = v.astype(BF)
        send(buf.at[jd, c], rp.at[0], r.sum_s.at[n, 1], r.sum_r.at[n, 1], p2)
        send(buf.at[jp2, c], rp.at[1], r.sum_s.at[n, 2], r.sum_r.at[n, 2], p2)

    def sum_relay(buf, rp, n):
        got(rp.at[0], r.sum_r.at[n, 1])
        buf[jp1, c] = (buf[jp1, c].astype(F32) + rp[0].astype(F32)).astype(BF)
        send(buf.at[jp1, c], rp.at[2], r.sum_s.at[n, 3], r.sum_r.at[n, 3], p1)

    def sum_fin(buf, rc, rp, n):
        got(rp.at[1], r.sum_r.at[n, 2])
        got(rp.at[2], r.sum_r.at[n, 3])
        total = buf[jme, c].astype(F32) + rp[1].astype(F32) + rp[2].astype(F32)
        sent(rc, r.sum_s.at[n, 0])
        for k in range(1, 4):
            sent(rp.at[0], r.sum_s.at[n, k])
        return total

    barrier = pltpu.get_barrier_semaphore()
    peers = (core, xp, diag, yp, z0p, z1p)
    for dev in peers:
        pl.semaphore_signal(barrier, inc=1, device_id=dev, device_id_type=MESH)

    def stage_copies():
        out = []
        for m in range(4):
            for zz in range(2):
                for h in range(2):
                    for k in range(2):
                        zt = z0 + zz * (1 - 2 * z0)
                        col = pl.multiple_of(
                            h * 2048 + 1024 * k + 512 * zt + 256 * c + 128 * x, 128
                        )
                        if m < 3:
                            src = r.e_in.at[m, :, pl.ds(col, 128)]
                        else:
                            src = r.s_in.at[:, pl.ds(col, 128)]
                        at = (h * 2 + k) * 128
                        q = 2 * m + zz
                        dst = r.acc.at[q // 2, q % 2, pl.ds(0, 96), pl.ds(at, 128)]
                        out.append((src, dst, r.stage_sem.at[m, zz * 4 + h * 2 + k]))
            row = pl.multiple_of(128 * x, 128)
            if m < 3:
                src = r.e_out.at[m, pl.ds(row, 128), :]
            else:
                src = r.s_out.at[pl.ds(row, 128), :]
            dst = r.acc.at[m // 2, m % 2, pl.ds(96, 128), pl.ds(0, D)]
            out.append((src, dst, r.stage_sem.at[m, 8]))
        return [pltpu.make_async_copy(*one) for one in out]

    staged = stage_copies()
    for one in staged:
        one.start()

    q_slot = lambda zz, yy: r.wq.at[zz, yy]
    q_ss = lambda n: r.att_s.at[0, n]
    q_rs = lambda n: r.att_r.at[0, n]
    o_slot = lambda zz, yy: r.ow.at[zz, yy, c]
    o_ss = lambda n: r.att_s.at[1, n]
    o_rs = lambda n: r.att_r.at[1, n]
    m_slot = lambda zz, yy: r.misc.at[zz, yy]
    m_ss = lambda n: r.att_s.at[2, n]
    m_rs = lambda n: r.att_r.at[2, n]

    def w_slot(m):
        return lambda zz, yy: r.win.at[m, zz, yy]

    def w_ss(m):
        return lambda n: r.w_s.at[m, n]

    def w_rs(m):
        return lambda n: r.w_r.at[m, n]

    r.wq[z, y] = r.wq_in[...]
    r.misc[z, y] = r.misc_in[...]
    r.ow[z, y, c] = r.ow_in[...]
    r.nall[s] = r.x_in[...]
    r.cota[jme, c] = r.cot_in[...]
    r.nta[jme, c, :, D : D + 128] = r.sel_in[...]

    pl.semaphore_wait(barrier, len(peers))

    send(r.x_in, r.nall.at[s], r.x_s.at[0], r.x_r.at[0], core)
    send(r.x_in, r.nall.at[s], r.x_s.at[1], r.x_r.at[1], xp)
    ow_set = (r.ow_in, o_slot, o_ss, o_rs)
    att_sets = ((r.misc_in, m_slot, m_ss, m_rs), (r.wq_in, q_slot, q_ss, q_rs))
    for src, slot, ss, rs in att_sets:
        ag_first(src, slot, ss, rs)
        ag_own(slot, ss, rs)

    for one in staged:
        one.wait()
    for m in range(4):
        q = 2 * m
        r.win[m, z, y] = r.acc[q // 2, q % 2, 0:96, 0:512].astype(BF)
        q = 2 * m + 1
        r.dg[m, 0:96, :] = r.acc[q // 2, q % 2, 0:96, 0:512].astype(BF)

    @pl.when(c == y)
    def _():
        for m in range(4):
            r.wout[m, z1] = r.acc[m // 2, m % 2, 96:224, 0:D].astype(BF)

    xf = s + 2 - 4 * x
    for src, slot, ss, rs in att_sets:
        ag_z0(slot, ss, rs)
    got(r.nall.at[xf], r.x_r.at[1])
    send(r.nall.at[xf], r.nall.at[xf], r.x_s.at[2], r.x_r.at[2], core)
    for m in range(4):
        ag_first(r.dg.at[m, pl.ds(0, 96)], w_slot(m), w_ss(m), w_rs(m))
    for src, slot, ss, rs in att_sets:
        ag_z1(slot, ss, rs)
    tok_own(sel_slot, 2)
    tok_own(cot_slot, 0)
    ag_first(*ow_set)
    ag_own(*ow_set[1:])
    for src, slot, ss, rs in att_sets:
        ag_fin(slot, rs)

    def w_own(m):
        ag_own(w_slot(m), w_ss(m), w_rs(m))

        @pl.when(c == y)
        def _():
            v = r.wout.at[m, z1]
            send(v, v, r.o_s.at[m, 0], r.o_r.at[m, z1], z1p)
            send(v, v, r.o_s.at[m, 1], r.o_r.at[m, z1], yp)

    def w_relay(m):
        ag_z0(w_slot(m), w_ss(m), w_rs(m))

    def w_relay_far(m):
        ag_z1(w_slot(m), w_ss(m), w_rs(m))

        @pl.when(c == y)
        def _():
            v = r.wout.at[m, 1 - z1]
            got(v, r.o_r.at[m, 1 - z1])
            send(v, v, r.o_s.at[m, 2], r.o_r.at[m, 1 - z1], yp)

    def w_fin(m):
        ag_fin(w_slot(m), w_rs(m))

        @pl.when(c != y)
        def _():
            got(r.wout.at[m, 0], r.o_r.at[m, 0])
            got(r.wout.at[m, 1], r.o_r.at[m, 1])

        for n in range(1, 7):
            sent(r.win.at[m, z, y], r.w_s.at[m, n])

        @pl.when(c == y)
        def _():
            for k in range(3):
                sent(r.wout.at[m, 0], r.o_s.at[m, k])

    w_own(0)
    w_own(1)

    rows = jnp.zeros((8, D), F32)
    for k in range(8):
        row_i = lax.broadcasted_iota(jnp.int32, (128, D), 0)
        col_i = lax.broadcasted_iota(jnp.int32, (128, D), 1)
        place = jnp.where((col_i == row_i + 96 * k) & (row_i < 96), 1.0, 0.0).astype(BF)
        rows = rows + nn(r.misc[k // 2, k % 2].astype(BF), place)
    r.mrow[...] = rows
    row8 = lax.broadcasted_iota(jnp.int32, (8, D), 0)
    r.rpad[...] = jnp.zeros((128, D), BF)
    r.rpad[0:16, :] = jnp.concatenate(
        [jnp.where(row8 < 3, rows, 0.0), jnp.zeros((8, D), F32)], axis=0
    ).astype(BF)

    got(r.nall.at[s + 1 - 2 * c], r.x_r.at[0])
    got(r.nall.at[3 - s], r.x_r.at[2])
    for k in range(3):
        sent(r.x_in, r.x_s.at[k])
    wq = r.wq[...].reshape(D, QKV_PAD)
    lane128 = lax.broadcasted_iota(jnp.int32, (TOK, 128), 1)

    def project(t, carry):
        xv = r.nall[t].astype(F32)
        r1 = lax.rsqrt(jnp.mean(xv * xv, axis=-1, keepdims=True) + EPSILON)
        nb = (xv * r1 * r.mrow[3:4, :]).astype(BF)
        r.nall[t] = nb
        pr = nn(nb, r.wq[...].reshape(D, QKV_PAD))
        at = pl.ds(pl.multiple_of(t * TOK, TOK), TOK)
        cosv = r.cos_in[at, :]
        sinv = r.sin_in[at, :]
        for h in range(3):
            hc = 128 * h + 128 * (h // 2)
            g = pr[:, hc : hc + 128]
            g = (g * cosv + swap_halves(g) * sinv).astype(BF).astype(F32)
            g = jnp.where(lane128 < 64, g * 0.125, g)
            r.kq[h, at, :] = pltpu.roll(g, 64, 1).astype(BF)
        r.val[0, at, :] = pr[:, 256:384].astype(BF)
        r.val[1, at, :] = pr[:, 512:640].astype(BF)
        return carry

    lax.fori_loop(0, 4, project, 0)

    ag_z0(*ow_set[1:])
    w_own(2)
    w_own(3)
    for m in range(4):
        w_relay(m)
    ag_z1(*ow_set[1:])
    tok_near(sel_slot, 2)
    tok_near(cot_slot, 0)

    for i in range(3, -1, -1):
        n = (i + 1) * TOK
        base = i * (i + 1) // 2

        def heads(h, carry, i=i, n=n, base=base):
            q = pltpu.roll(r.kq[h, i * TOK : i * TOK + TOK, :].astype(F32), 64, 1)
            q = jnp.where(lane128 < 64, q, 0.0)
            sc = nt(q.astype(BF), r.kq[h, 0:n, :])
            top = jnp.max(sc, axis=-1, keepdims=True)
            e = jnp.exp(sc - top)
            pb = (e * (1.0 / jnp.sum(e, axis=-1, keepdims=True))).astype(BF)
            for j in range(i + 1):
                r.prob[h, base + j] = pb[:, j * TOK : j * TOK + TOK]
            r.acc[h, 0, :, 0:128] = nn(pb, r.val[lax.div(h, 2), 0:n, :])
            return carry

        lax.fori_loop(0, 3, heads, 0)
        r.att[i, :, 0:128] = jnp.where(lane128 < 64, r.acc[0, 0, :, 0:128], r.acc[1, 0, :, 0:128]).astype(BF)
        r.att[i, :, 128:256] = r.acc[2, 0, :, 0:128].astype(BF)

        @pl.when(s != i)
        def _(i=i):
            send(r.att.at[i], r.arow.at[s], r.a_s.at[i], r.a_r.at[s], (b, i))

        @pl.when(s == i)
        def _(i=i):
            r.arow[i] = r.att[i]

        if i == 1:
            ag_fin(o_slot, o_rs)
            send(r.ow.at[:, :, c], r.ow.at[:, :, c], r.ow_s.at[0], r.ow_r.at[0], core)
        if i == 2:
            w_relay_far(0)
            tok_far(sel_slot, 2)
            tok_far(cot_slot, 0)
        if i == 0:
            w_relay_far(1)

    got(r.ow.at[:, :, oc], r.ow_r.at[0])
    sent(r.ow.at[:, :, c], r.ow_s.at[0])
    for src, slot, ss, rs in att_sets + (ow_set,):
        ag_sent(src, slot, ss)
    for i in range(4):

        @pl.when(s != i)
        def _(i=i):
            got(r.arow.at[i], r.a_r.at[i])
            sent(r.att.at[i], r.a_s.at[i])

    ow = r.ow[...].reshape(D, D)
    mid = r.x_in[...].astype(F32)
    for i in range(4):
        mid = mid + nn(r.arow[i][:, 0:192], ow[192 * i : 192 * i + 192, :])
    r.mid[...] = mid
    r2 = lax.rsqrt(jnp.mean(mid * mid, axis=-1, keepdims=True) + EPSILON)
    nb = (mid * r2 * r.mrow[4:5, :]).astype(BF)
    r.nta[jme, c, :, 0:D] = nb
    tok_own(two_slot, 1)
    tok_fin(sel_slot, 2)
    tok_fin(cot_slot, 0)

    def gates(nv):
        lg = nt(nv, r.rpad[...])
        lg = jnp.where(lane128 < 3, lg, -1e30)
        e = jnp.exp(lg - jnp.max(lg, axis=-1, keepdims=True))
        return e / jnp.sum(e, axis=-1, keepdims=True)

    def route(j, k):
        sel = r.nta[j, k, :, D : D + 128].astype(F32)
        pv = gates(r.nta[j, k, :, 0:D])
        gv = jnp.where(lane128 < 3, pv * sel, jnp.where(lane128 == 3, sel, 0.0))
        r.acc[j, k, :, 0:D] = jnp.zeros((TOK, D), F32)
        r.acc[j, k, :, D : D + 128] = pltpu.roll(gv, 64, 1)

    def rs_first(m):
        send(r.win.at[m, :, oy], r.ry_in.at[m], r.rs_s.at[m, 0], r.rs_r.at[m, 0], yp)

        @pl.when(c != y)
        def _():
            send(r.gout.at[m], r.ry_out.at[m], r.rs_s.at[m, 1], r.rs_r.at[m, 1], yp)

    def out_rows(m, k):
        at = pl.ds(pl.multiple_of(128 * k, 128), 128)
        return r.gs_out.at[at] if m == 3 else r.ge_out.at[m, at]

    def rs_y(m):
        got(r.ry_in.at[m], r.rs_r.at[m, 0])
        for zz in range(4):
            r.win[m, zz, y] = (r.win[m, zz, y].astype(F32) + r.ry_in[m, zz].astype(F32)).astype(BF)
        send(
            r.win.at[m, pl.ds(2 - 2 * z1, 2), y], r.rz_in.at[m], r.rs_s.at[m, 2], r.rs_r.at[m, 2], z1p
        )

        @pl.when(c == y)
        def _():
            got(r.ry_out.at[m], r.rs_r.at[m, 1])
            for k in range(2):
                r.gout[m, k] = (r.gout[m, k].astype(F32) + r.ry_out[m, k].astype(F32)).astype(BF)
            send(r.gout.at[m, 1 - z1], r.rz_out.at[m], r.rs_s.at[m, 3], r.rs_r.at[m, 3], z1p)

    def rs_z(m):
        got(r.rz_in.at[m], r.rs_r.at[m, 2])
        for k in range(2):
            zz = 2 * z1 + k
            r.win[m, zz, y] = (r.win[m, zz, y].astype(F32) + r.rz_in[m, k].astype(F32)).astype(BF)
        send(r.win.at[m, zf, y], r.rzz.at[m], r.rs_s.at[m, 4], r.rs_r.at[m, 4], z0p)

        @pl.when(c == y)
        def _():
            got(r.rz_out.at[m], r.rs_r.at[m, 3])
            v = (r.gout[m, z1].astype(F32) + r.rz_out[m].astype(F32)).astype(BF)
            r.gout[m, z1] = v
            g = r.gout.at[m, z1]
            pltpu.make_async_copy(g, out_rows(m, x), r.loc.at[m, 1]).start()
            send(g, out_rows(m, x), r.rs_s.at[m, 5], r.rs_r.at[m, 5], xp)
            send(g, out_rows(m, x), r.rs_s.at[m, 6], r.rs_r.at[m, 6], core)

    def part(m, sx, sc):
        return r.ga.at[2 * m + sx, pl.ds(0, 192), pl.ds(pl.multiple_of(512 * sc, 512), 512)]

    def rs_join(m):
        got(r.rzz.at[m], r.rs_r.at[m, 4])
        cols = pl.ds(pl.multiple_of(512 * c, 512), 512)
        mine = pl.ds(pl.multiple_of(96 * z0, 96), 96)
        theirs = pl.ds(pl.multiple_of(96 - 96 * z0, 96), 96)
        r.ga[2 * m + x, mine, cols] = r.win[m, z, y]
        r.ga[2 * m + x, theirs, cols] = r.rzz[m]
        g = part(m, x, c)
        send(g, g, r.rs_s.at[m, 7], r.rs_r.at[m, 7], xp)
        send(g, g, r.rs_s.at[m, 8], r.rs_r.at[m, 8], core)

    def rs_spread(m):
        g = part(m, 1 - x, c)
        got(g, r.rs_r.at[m, 7])
        send(g, g, r.rs_s.at[m, 9], r.rs_r.at[m, 9], core)

        @pl.when(c == y)
        def _():
            v = out_rows(m, 1 - x)
            got(v, r.rs_r.at[m, 5])
            send(v, v, r.rs_s.at[m, 10], r.rs_r.at[m, 10], core)

    def rs_end(m):
        got(part(m, x, oc), r.rs_r.at[m, 8])
        got(part(m, 1 - x, oc), r.rs_r.at[m, 9])
        for k in range(8):
            h, kz, zz = k // 4, k // 2 % 2, k % 2
            for q in range(4):
                sc, sx = q // 2, q % 2
                at = 512 * sc + 128 * (2 * h + kz)
                v = r.ga[2 * m + sx, 96 * zz : 96 * zz + 96, at : at + 128]
                if h == 0:
                    r.ry_in[m, k, :, 128 * q : 128 * q + 128] = v
                else:
                    row = 96 * (k % 2)
                    r.dg[2 * m + kz, row : row + 96, 128 * q : 128 * q + 128] = v
            src = r.ry_in.at[m, k] if h == 0 else r.dg.at[2 * m + kz, pl.ds(96 * (k % 2), 96)]
            dst = r.gs_in if m == 3 else r.ge_in.at[m]
            pltpu.make_async_copy(src, dst.at[:, pl.ds(512 * k, 512)], r.fin.at[m, k]).start()
        sent(r.ry_in.at[m], r.rs_s.at[m, 0])
        sent(r.rz_in.at[m], r.rs_s.at[m, 2])
        sent(r.win.at[m, zf, y], r.rs_s.at[m, 4])
        for k in (7, 8, 9):
            sent(part(m, x, c), r.rs_s.at[m, k])

        @pl.when(c != y)
        def _():
            sent(r.gout.at[m], r.rs_s.at[m, 1])
            got(out_rows(m, x), r.rs_r.at[m, 6])
            got(out_rows(m, 1 - x), r.rs_r.at[m, 10])

        @pl.when(c == y)
        def _():
            g = r.gout.at[m, z1]
            pltpu.make_async_copy(g, out_rows(m, x), r.loc.at[m, 1]).wait()
            for k in (3, 5, 6, 10):
                sent(g, r.rs_s.at[m, k])

    def rs_done(m):
        for k in range(8):
            dst = r.gs_in if m == 3 else r.ge_in.at[m]
            piece = dst.at[:, pl.ds(512 * k, 512)]
            pltpu.make_async_copy(piece, piece, r.fin.at[m, k]).wait()

    def tokens(m, j, k):
        g = 2 * j + k
        w = r.win[m].reshape(D, 512)
        wo = r.wout[m].reshape(256, D)
        gu = nn(r.nta[j, k, :, 0:D], w)
        zv = gu[:, 0:256]
        uv = gu[:, 256:512]
        sg = 1.0 / (1.0 + jnp.exp(-zv))
        sw = zv * sg
        act = (sw * uv).astype(BF).astype(F32)
        dr = nt(r.cota[j, k], wo)
        side = r.acc[j, k, :, D : D + 128]
        gv = jnp.sum(jnp.where(lane128 == m + 64, side, 0.0), axis=-1, keepdims=True)
        gg = jnp.sum(act * dr, axis=-1, keepdims=True)
        r.ga[g, :, pl.ds(pl.multiple_of(m * 256, 256), 256)] = (act * gv).astype(BF)
        d = dr * gv
        dg = jnp.concatenate([d * uv * (sg * (1.0 + zv * (1.0 - sg))), d * sw], axis=1).astype(BF)
        r.dg[g] = dg
        r.acc[j, k, :, 0:D] += nt(dg, w)
        r.acc[j, k, :, D : D + 128] = side + jnp.where(lane128 == m, gg, 0.0)

    def weight_grads(m):
        nta = r.nta[:, :, :, 0:D].reshape(2048, D)
        r.win[m] = tn(nta, r.dg[...].reshape(2048, 512)).astype(BF).reshape(4, 2, 96, 512)
        gam = r.ga[:, :, pl.ds(pl.multiple_of(m * 256, 256), 256)].reshape(2048, 256)
        r.gout[m] = tn(gam, r.cota[...].reshape(2048, D)).astype(BF).reshape(2, 128, D)
        rs_first(m)

    def pack(j, k):
        r.ngb[j, k, :, 0:D] = r.acc[j, k, :, 0:D].astype(BF)
        v = jnp.where(lane128 < 64, r.acc[j, k, :, D : D + 128], 0.0)
        hi = v.astype(BF).astype(F32)
        r.ngb[j, k, :, D : D + 128] = (hi + pltpu.roll(v - hi, 64, 1)).astype(BF)

    w_fin(0)
    for m in range(4):
        sent(r.dg.at[m, pl.ds(0, 96)], r.w_s.at[m, 0])

    def arrive(p, carry):
        q = lax.div(p, 2)
        k2 = lax.rem(p, 2)
        j = block_at(q)
        k = c + k2 * (1 - 2 * c)

        @pl.when(p == 2)
        def _():
            tok_near(two_slot, 1)

        @pl.when(k2 == 1)
        def _():
            got(two_slot(j, k), r.tok_r.at[1, p])

        @pl.when(p == 4)
        def _():
            w_relay_far(2)

        @pl.when(p == 5)
        def _():
            tok_far(two_slot, 1)

        route(j, k)
        tokens(0, j, k)
        return carry

    lax.fori_loop(0, 8, arrive, 0)
    weight_grads(0)
    tok_sent(two_slot, 1)
    tok_sent(sel_slot, 2)
    tok_sent(cot_slot, 0)

    def feed(m, carry):
        @pl.when(m == 1)
        def _():
            w_relay_far(3)

        w_fin(m)

        def each(p, inner):
            k2 = lax.div(p, 4)
            k = oc + k2 * (2 * c - 1)
            j = block_at(3 - lax.rem(p, 4))
            tokens(m, j, k)

            @pl.when(m == 3)
            def _():
                pack(j, k)

            @pl.when((m == 3) & (p == 3))
            def _():
                sum_first(r.ngb, r.ng_c, 0)

            return inner

        lax.fori_loop(0, 8, each, 0)

        @pl.when(m == 2)
        def _():
            rs_y(0)

        @pl.when(m == 3)
        def _():
            sum_core(r.ngb, r.ng_c, r.ng_p, 0)
            rs_y(1)

        weight_grads(m)
        return carry

    lax.fori_loop(1, 4, feed, 0)

    def mix(g, carry):
        j = lax.div(g, 2)
        k = lax.rem(g, 2)
        r.cota[j, k] = nn(r.ga[g], r.wout[...].reshape(1024, D)).astype(BF)
        return carry

    lax.fori_loop(0, 4, mix, 0)
    sum_relay(r.ngb, r.ng_p, 0)
    lax.fori_loop(4, 8, mix, 0)
    rs_y(2)
    out_c = r.ng_c.at[:, :, pl.ds(0, D)]
    out_p = r.ng_p.at[:, :, pl.ds(0, D)]
    ngs = sum_fin(r.ngb, r.ng_c, r.ng_p, 0)
    rs_z(0)

    small_dev = (core, xp, yp, z1p, z0p)

    def small_send(k):
        r.small_o[k] = r.small[...]
        send(r.small_o.at[k], r.small_i.at[k], r.sm_s.at[k], r.sm_r.at[k], small_dev[k])

    def small_add(k):
        got(r.small_i.at[k], r.sm_r.at[k])
        r.small[...] += r.small_i[k]
        sent(r.small_o.at[k], r.sm_s.at[k])
        if k < 4:
            small_send(k + 1)

    upstream = r.cot_in[...].astype(F32)
    mid = r.mid[...]
    r2 = lax.rsqrt(jnp.mean(mid * mid, axis=-1, keepdims=True) + EPSILON)
    gg = ngs[:, D : D + 128]
    gg = gg + pltpu.roll(gg, 64, 1)
    nown = r.nta[jme, c, :, 0:D]
    pv = gates(nown)
    pg = jnp.where(lane128 < 3, gg * r.sel_in[...].astype(F32), 0.0)
    lg = (pv * (pg - jnp.sum(pv * pg, axis=-1, keepdims=True))).astype(BF)
    rgrad = tn(lg, nown)
    ng = ngs[:, 0:D] + nn(lg, r.rpad[...])
    gain2 = r.mrow[4:5, :]
    fgain = jnp.sum(ng * mid * r2, axis=0, keepdims=True)
    sc = ng * gain2
    mg = upstream + r2 * sc - mid * (r2 * r2 * r2) * jnp.mean(sc * mid, axis=-1, keepdims=True)
    r.igrad[...] = mg
    r.small[...] = jnp.where(row8 < 3, rgrad[0:8, :], 0.0) + jnp.where(row8 == 4, fgain, 0.0)
    ml = mg.astype(BF)
    ow = r.ow[...].reshape(D, D)
    r.att[:, :, 128:256] = jnp.zeros((4, TOK, 128), BF)
    for i in range(4):
        da = nt(ml, ow[192 * i : 192 * i + 192, :]).astype(BF)
        r.att[i, :, 0:192] = da

        @pl.when(s != i)
        def _(i=i):
            send(r.att.at[i], r.dat.at[s], r.d_s.at[i], r.d_r.at[s], (b, i))

        @pl.when(s == i)
        def _(i=i):
            r.dat[i] = r.att[i]

    small_send(0)
    for i in range(4):
        og = tn(r.arow[i][:, 0:192], ml).astype(BF)
        og = og.reshape(2, 2, 48, D)
        for k in range(2):
            r.og[k, i] = og[:, :, :, 384 * k : 384 * k + 384]
    send(r.og.at[oc], r.og_c, r.og_s.at[0], r.og_r.at[0], core)
    for i in range(4):
        r.acc[i, 0, :, 0:QKV_PAD] = jnp.zeros((TOK, QKV_PAD), F32)
        r.acc[i, 1, :, 0:D] = jnp.zeros((TOK, D), F32)
    small_add(0)
    rs_y(3)
    rs_z(1)
    for i in range(4):

        @pl.when(s != i)
        def _(i=i):
            got(r.dat.at[i], r.d_r.at[i])
            sent(r.att.at[i], r.d_s.at[i])

    sum_first(r.cota, out_c, 1)

    chunks = ((0, 128), (128, 256), (384, 256))

    def q_first(n):
        at = pl.ds(chunks[n][0], chunks[n][1])
        send(r.wq.at[:, oy, :, at], r.q_y.at[:, :, at], r.q_s.at[n, 0], r.q_r.at[n, 0], yp)

    def q_add_y(n):
        a, e = chunks[n][0], chunks[n][0] + chunks[n][1]
        at = pl.ds(a, e - a)
        got(r.q_y.at[:, :, at], r.q_r.at[n, 0])
        for k in range(4):
            v = r.wq[k, y, :, a:e].astype(F32) + r.q_y[k, :, a:e].astype(F32)
            r.wq[k, y, :, a:e] = v.astype(BF)
        send(
            r.wq.at[pl.ds(2 - 2 * z1, 2), y, :, at],
            r.q_z.at[:, :, at],
            r.q_s.at[n, 1],
            r.q_r.at[n, 1],
            z1p,
        )

    def q_add_z(n):
        a, e = chunks[n][0], chunks[n][0] + chunks[n][1]
        at = pl.ds(a, e - a)
        got(r.q_z.at[:, :, at], r.q_r.at[n, 1])
        for k in range(2):
            v = r.wq[2 * z1 + k, y, :, a:e].astype(F32) + r.q_z[k, :, a:e].astype(F32)
            r.wq[2 * z1 + k, y, :, a:e] = v.astype(BF)
        send(r.wq.at[zf, y, :, at], r.q_w.at[:, at], r.q_s.at[n, 2], r.q_r.at[n, 2], z0p)

    def head_ends(a, w):
        at = pl.ds(a, w)
        for i in range(4):
            for k in range(0, w, 128):
                g = r.acc[i, 0, :, a + k : a + k + 128].astype(BF)
                if a + k in (0, 128, 384):
                    g = g.astype(F32)
                    cosv = r.cos_in[i * TOK : i * TOK + TOK, :]
                    sinv = r.sin_in[i * TOK : i * TOK + TOK, :]
                    g = (g * cosv - swap_halves(g) * sinv).astype(BF)
                r.nta[i, 0, :, a + k : a + k + 128] = g
        wc = r.wq[:, :, :, a : a + w].reshape(D, w)
        for i in range(4):
            r.acc[i, 1, :, 0:D] += nt(r.nta[i, 0, :, a : a + w], wc)
        pg = r.nta[:, 0, :, a : a + w].reshape(1024, w)
        wg = tn(r.nall[...].reshape(1024, D), pg)
        r.wq[:, :, :, a : a + w] = wg.astype(BF).reshape(4, 2, 96, w)

    def og_core():
        got(r.og_c, r.og_r.at[0])
        for k in range(4):
            r.og[c, k] = (r.og[c, k].astype(F32) + r.og_c[k].astype(F32)).astype(BF)
        send(r.og.at[c, :, :, 1 - x], r.og_x, r.og_s.at[1], r.og_r.at[1], xp)

    def og_xp():
        got(r.og_x, r.og_r.at[1])
        for k in range(4):
            r.og[c, k, :, x] = (r.og[c, k, :, x].astype(F32) + r.og_x[k].astype(F32)).astype(BF)
        send(r.og.at[c, :, oy, x], r.og_y, r.og_s.at[2], r.og_r.at[2], yp)

    def og_yp():
        got(r.og_y, r.og_r.at[2])
        for k in range(4):
            r.og[c, k, y, x] = (r.og[c, k, y, x].astype(F32) + r.og_y[k].astype(F32)).astype(BF)
        send(r.og.at[c, pl.ds(2 - 2 * z1, 2), y, x], r.og_z, r.og_s.at[3], r.og_r.at[3], z1p)

    def og_z1p():
        got(r.og_z, r.og_r.at[3])
        for k in range(2):
            v = r.og[c, 2 * z1 + k, y, x].astype(F32) + r.og_z[k].astype(F32)
            r.og[c, 2 * z1 + k, y, x] = v.astype(BF)
        send(r.og.at[c, zf, y, x], r.og_w, r.og_s.at[4], r.og_r.at[4], z0p)

    def og_z0p():
        got(r.og_w, r.og_r.at[4])
        r.og[c, z, y, x] = (r.og[c, z, y, x].astype(F32) + r.og_w[...].astype(F32)).astype(BF)
        ogf = r.og.at[c, z, y, x]
        r.g_ow[s] = r.og[c, z, y, x]
        send(ogf, r.g_ow.at[s], r.og_s.at[6], r.og_r.at[6], xp)
        send(ogf, r.g_ow.at[s], r.og_s.at[5], r.og_r.at[5], core)

    def heads_back(h, carry):
        hv = lax.div(h, 2)
        here = lax.div(lane128, 64) == lax.rem(h, 2)
        vat = pl.ds(pl.multiple_of(hv * 128, 128), 128)
        cat = pl.ds(pl.multiple_of(256 + hv * 256, 128), 128)
        hat = pl.ds(pl.multiple_of(h * 128 + hv * 128, 128), 128)
        for i in range(3, -1, -1):
            base = i * (i + 1) // 2
            da = jnp.where(here, r.dat[i, :, vat].astype(F32), 0.0).astype(BF)
            kqi = r.kq[h, i * TOK : i * TOK + TOK, :].astype(F32)
            qi = jnp.where(lane128 >= 64, kqi, 0.0).astype(BF)
            pf = [r.prob[h, base + j] for j in range(i + 1)]
            dp = [nt(da, r.val[hv, j * TOK : j * TOK + TOK, :]) for j in range(i + 1)]
            cen = jnp.zeros((TOK, 1), F32)
            for j in range(i + 1):
                cen = cen + jnp.sum(pf[j].astype(F32) * dp[j], axis=-1, keepdims=True)
            dq = jnp.zeros((TOK, 128), F32)
            for j in range(i + 1):
                ds = (pf[j].astype(F32) * (dp[j] - cen)).astype(BF)
                dq = dq + nn(ds, r.kq[h, j * TOK : j * TOK + TOK, :])
                r.acc[j, 0, :, hat] += tn(ds, qi)
                r.acc[j, 0, :, cat] += tn(pf[j], da)
            r.acc[i, 0, :, hat] += jnp.where(lane128 < 64, dq * 0.125, 0.0)

        @pl.when(h == 0)
        def _():
            head_ends(*chunks[0])
            q_first(0)
            og_core()
            rs_join(0)
            sum_core(r.cota, out_c, out_p, 1)
            rs_z(2)
            small_add(1)

        @pl.when(h == 1)
        def _():
            head_ends(*chunks[1])
            q_first(1)
            og_xp()
            sum_relay(r.cota, out_p, 1)
            q_add_y(0)
            rs_join(1)
            rs_spread(0)
            small_add(2)

        @pl.when(h == 2)
        def _():
            head_ends(*chunks[2])
            q_first(2)

        return carry

    lax.fori_loop(0, 3, heads_back, 0)

    n_slot = lambda i: r.nta.at[i, 1, :, pl.ds(0, D)]
    for i in range(4):
        r.nta[i, 1, :, 0:D] = r.acc[i, 1, :, 0:D].astype(BF)
    for k in range(2):
        send(n_slot(2 * k + oc), r.n_c.at[k], r.n_s.at[k], r.n_r.at[k], core)
    og_yp()
    q_add_y(1)
    for k in range(2):
        got(r.n_c.at[k], r.n_r.at[k])
        v = r.nta[2 * k + c, 1, :, 0:D].astype(F32) + r.n_c[k].astype(F32)
        r.nta[2 * k + c, 1, :, 0:D] = v.astype(BF)
    send(n_slot(2 - 2 * x + c), r.n_x, r.n_s.at[2], r.n_r.at[2], xp)
    q_add_z(0)
    rs_z(3)
    rs_join(2)
    rs_spread(1)
    rs_end(0)
    small_add(3)
    q_add_y(2)
    og_z1p()
    q_add_z(1)
    rs_join(3)
    rs_spread(2)
    tot = sum_fin(r.cota, out_c, out_p, 1)
    r.out[...] = (r.mid[...] + tot).astype(BF)
    rs_end(1)
    small_add(4)
    r.g_small[...] = r.small[...]
    og_z0p()

    got(r.n_x, r.n_r.at[2])
    for k in range(3):
        sent(r.n_x, r.n_s.at[k])
    ng = r.nta[s, 1, :, 0:D].astype(F32) + r.n_x[...].astype(F32)
    xv = r.x_in[...].astype(F32)
    r1 = lax.rsqrt(jnp.mean(xv * xv, axis=-1, keepdims=True) + EPSILON)
    sc = ng * r.mrow[3:4, :]
    r.igrad[...] = (
        r.igrad[...] + r1 * sc - xv * (r1 * r1 * r1) * jnp.mean(sc * xv, axis=-1, keepdims=True)
    )
    q_add_z(2)
    rs_spread(3)
    rs_end(2)
    got(r.g_ow.at[xf], r.og_r.at[6])
    send(r.g_ow.at[xf], r.g_ow.at[xf], r.og_s.at[7], r.og_r.at[7], core)

    for n in range(3):
        got(r.q_w.at[:, pl.ds(*chunks[n])], r.q_r.at[n, 2])
    qf = r.wq[z, y].astype(F32) + r.q_w[...].astype(F32)
    qf = jnp.concatenate([qf, jnp.zeros((32, QKV_PAD), F32)], axis=0)
    qt = jnp.transpose(qf).astype(BF)
    for k, at in enumerate((0, 64, 256, 128, 192, 320, 384, 448, 512)):
        r.g_q[s, 64 * k : 64 * k + 64, :] = qt[at : at + 64, :]
    g = r.g_q.at[s]
    send(g, g, r.qg_s.at[0], r.qg_r.at[0], xp)
    send(g, g, r.qg_s.at[1], r.qg_r.at[1], core)
    rs_end(3)
    got(r.g_q.at[xf], r.qg_r.at[0])
    send(r.g_q.at[xf], r.g_q.at[xf], r.qg_s.at[2], r.qg_r.at[2], core)
    got(r.g_ow.at[s + 1 - 2 * c], r.og_r.at[5])
    got(r.g_ow.at[3 - s], r.og_r.at[7])
    for n in range(3):
        at = pl.ds(*chunks[n])
        sent(r.q_y.at[:, :, at], r.q_s.at[n, 0])
        sent(r.q_z.at[:, :, at], r.q_s.at[n, 1])
        sent(r.q_w.at[:, at], r.q_s.at[n, 2])
    sent(r.og_c, r.og_s.at[0])
    sent(r.og_x, r.og_s.at[1])
    sent(r.og_y, r.og_s.at[2])
    sent(r.og_z, r.og_s.at[3])
    sent(r.og_w, r.og_s.at[4])
    for k in (5, 6, 7):
        sent(r.g_ow.at[0], r.og_s.at[k])
    for m in range(4):
        rs_done(m)
    got(r.g_q.at[s + 1 - 2 * c], r.qg_r.at[1])
    got(r.g_q.at[3 - s], r.qg_r.at[2])
    for k in range(3):
        sent(g, r.qg_s.at[k])


def vmem(shape, kind=BF):
    return pltpu.VMEM(shape, kind)


def layer_call(ins, cos_table, sin_table):
    dma = pltpu.SemaphoreType.DMA
    in_names = (
        ["x_in", "cot_in", "wq_in", "misc_in", "ow_in", "sel_in", "cos_in", "sin_in"]
        + ["e_in", "e_out", "s_in", "s_out"]
    )
    out_names = ["out", "igrad", "g_small", "g_q", "g_ow"]
    out_names += ["ge_in", "gs_in", "ge_out", "gs_out"]
    out_shapes = (
        ((TOK, D), BF),
        ((TOK, D), F32),
        ((8, D), F32),
        ((4, 576, 128), BF),
        ((4, 48, 384), BF),
        ((3, 96, 4096), BF),
        ((96, 4096), BF),
        ((3, 256, D), BF),
        ((256, D), BF),
    )
    scratch = {
        "nall": vmem((4, TOK, D)),
        "wq": vmem((4, 2, 96, QKV_PAD)),
        "misc": vmem((4, 2, 8, 128), F32),
        "ow": vmem((4, 2, 2, 48, D)),
        "kq": vmem((3, 1024, 128)),
        "val": vmem((2, 1024, 128)),
        "prob": vmem((3, 10, TOK, TOK)),
        "att": vmem((4, TOK, 256)),
        "arow": vmem((4, TOK, 256)),
        "dat": vmem((4, TOK, 256)),
        "mid": vmem((TOK, D), F32),
        "mrow": vmem((8, D), F32),
        "rpad": vmem((128, D)),
        "nta": vmem((4, 2, TOK, D + 128)),
        "cota": vmem((4, 2, TOK, D)),
        "win": vmem((4, 4, 2, 96, 512)),
        "wout": vmem((4, 2, 128, D)),
        "dg": vmem((8, TOK, 512)),
        "ga": vmem((8, TOK, 1024)),
        "acc": vmem((4, 2, TOK, D + 128), F32),
        "gout": vmem((4, 2, 128, D)),
        "ry_in": vmem((4, 4, 96, 512)),
        "ry_out": vmem((4, 2, 128, D)),
        "rzz": vmem((4, 96, 512)),
        "rz_in": vmem((4, 2, 96, 512)),
        "rz_out": vmem((4, 128, D)),
        "ng_c": vmem((4, TOK, D + 128)),
        "ng_p": vmem((3, TOK, D + 128)),
        "ngb": vmem((4, 2, TOK, D + 128)),
        "n_c": vmem((2, TOK, D)),
        "n_x": vmem((TOK, D)),
        "og": vmem((2, 4, 2, 2, 48, 384)),
        "og_c": vmem((4, 2, 2, 48, 384)),
        "og_x": vmem((4, 2, 48, 384)),
        "og_y": vmem((4, 48, 384)),
        "og_z": vmem((2, 48, 384)),
        "og_w": vmem((48, 384)),
        "q_y": vmem((4, 96, QKV_PAD)),
        "q_z": vmem((2, 96, QKV_PAD)),
        "q_w": vmem((96, QKV_PAD)),
        "small": vmem((8, D), F32),
        "small_o": vmem((5, 8, D), F32),
        "small_i": vmem((5, 8, D), F32),
        "stage_sem": dma((4, 9)),
        "att_s": dma((3, 7)),
        "att_r": dma((3, 8)),
        "w_s": dma((4, 7)),
        "w_r": dma((4, 8)),
        "o_s": dma((4, 3)),
        "o_r": dma((4, 2)),
        "ow_s": dma((1,)),
        "ow_r": dma((1,)),
        "x_s": dma((3,)),
        "x_r": dma((3,)),
        "tok_s": dma((3, 7)),
        "tok_r": dma((3, 8)),
        "a_s": dma((4,)),
        "a_r": dma((4,)),
        "d_s": dma((4,)),
        "d_r": dma((4,)),
        "sum_s": dma((2, 4)),
        "sum_r": dma((2, 4)),
        "rs_s": dma((4, 11)),
        "rs_r": dma((4, 11)),
        "loc": dma((4, 2)),
        "og_s": dma((8,)),
        "og_r": dma((8,)),
        "q_s": dma((3, 3)),
        "q_r": dma((3, 3)),
        "qg_s": dma((3,)),
        "qg_r": dma((3,)),
        "fin": dma((4, 8)),
        "n_s": dma((3,)),
        "n_r": dma((3,)),
        "sm_s": dma((5,)),
        "sm_r": dma((5,)),
    }
    names = in_names + out_names + list(scratch)
    in_vmem = pl.BlockSpec(memory_space=pltpu.VMEM)
    in_any = pl.BlockSpec(memory_space=pl.ANY)
    return pl.pallas_call(
        functools.partial(layer_kernel, names),
        out_shape=[jax.ShapeDtypeStruct(*one) for one in out_shapes],
        in_specs=[in_vmem] * 8 + [in_any] * 4,
        out_specs=[in_vmem] * 5 + [in_any] * 4,
        scratch_shapes=list(scratch.values()),
        compiler_params=pltpu.CompilerParams(
            collective_id=0, has_side_effects=True, vmem_limit_bytes=VMEM_LIMIT
        ),
        cost_estimate=pl.CostEstimate(
            flops=35_000_000_000, bytes_accessed=60_000_000, transcendentals=6_000_000
        ),
        name="layer",
    )(*ins[:6], cos_table, sin_table, *ins[6:])


def fast_device(
    inputs,
    attn_gain,
    qkv_weight,
    out_weight,
    ffn_gain,
    router_weight,
    expert_in,
    expert_out,
    shared_in,
    shared_out,
    routes,
    slot_index,
    cotangent,
):
    b = lax.axis_index("dp")
    s = lax.axis_index("seq")
    c = s % 2
    mine = lax.dynamic_slice_in_dim(qkv_weight, 3 * s, 3, axis=1).astype(BF)
    pairs = mine[:, :, 0:2].reshape(96, 3, 128)
    values = mine[:, :, 2].reshape(96, 192)
    wq = jnp.concatenate(
        [
            pairs[:, 0],
            pairs[:, 1],
            values[:, 0:128],
            pairs[:, 2],
            values[:, 128:192],
            jnp.zeros((96, 64), BF),
        ],
        axis=1,
    )
    misc = jnp.concatenate(
        [router_weight.T, attn_gain[None], ffn_gain[None], jnp.zeros((3, 96), F32)], axis=0
    )
    misc = jnp.pad(misc.astype(BF).astype(F32), ((0, 0), (0, 32)))
    half = lax.dynamic_slice_in_dim(out_weight, 48 * c, 48, axis=0).astype(BF)
    lane = jnp.arange(128, dtype=jnp.int32)
    route = routes[0]
    sel = (lane == route[:, 0:1]) | (lane == route[:, 1:2]) | (lane == 3)
    sel = sel.astype(BF)
    angle = np.arange(1024, dtype=np.float32)[:, None] * (
        np.float32(10000.0) ** (-np.arange(32, dtype=np.float32) / np.float32(32))
    )
    cos_table = jnp.asarray(np.tile(np.cos(angle), (1, 4)).astype(np.float32))
    sine = np.sin(angle)
    sin_table = jnp.asarray(np.tile(np.concatenate([-sine, sine], 1), (1, 2)).astype(np.float32))
    out, igrad, small, g_q, g_ow, ge_in, gs_in, ge_out, gs_out = layer_call(
        (
            inputs[0],
            cotangent[0],
            wq,
            misc,
            half,
            sel,
            expert_in,
            expert_out,
            shared_in,
            shared_out,
        ),
        cos_table,
        sin_table,
    )
    shard = lax.dynamic_slice_in_dim(small, 96 * b, 96, axis=1)
    qkv_grad = g_q.reshape(HEADS, 3, HEAD_DIM, 128)[..., 0:96].transpose(3, 0, 1, 2).astype(F32)
    gain_grad = jnp.sum(qkv_weight.astype(BF).astype(F32) * qkv_grad, axis=(1, 2, 3))
    gain_grad = gain_grad / attn_gain.astype(BF).astype(F32)
    ow_grad = g_ow.reshape(2, 2, 48, 384).transpose(0, 2, 1, 3).reshape(96, D).astype(F32)
    return (
        out[None],
        igrad[None],
        gain_grad,
        qkv_grad,
        ow_grad,
        shard[4],
        shard[0:3].T,
        ge_in.astype(F32),
        ge_out.astype(F32),
        gs_in.astype(F32),
        gs_out.astype(F32),
    )


def solution(mesh):
    fits = mesh.shape["dp"] == 8 and mesh.shape["seq"] == 4
    return jax.shard_map(
        fast_device if fits else on_device,
        mesh=mesh,
        in_specs=(
            P("dp", "seq", None),
            P("dp"),
            P("dp", None, None, None),
            P("dp", None),
            P("dp"),
            P("dp", None),
            P(None, "dp", None),
            P(None, "dp", None),
            P("dp", None),
            P("dp", None),
            P("dp", "seq", None),
            P("dp", "seq", None),
            P("dp", "seq", None),
        ),
        out_specs=(
            P("dp", "seq", None),
            P("dp", "seq", None),
            P("dp"),
            P("dp", None, None, None),
            P("dp", None),
            P("dp"),
            P("dp", None),
            P(None, "dp", None),
            P(None, "dp", None),
            P("dp", None),
            P("dp", None),
        ),
        check_vma=False,
    )
```

```python
import functools
import types

import jax
import jax.numpy as jnp
import numpy as np
from jax import lax
from jax.experimental import pallas as pl
from jax.experimental.pallas import tpu as pltpu
from jax.sharding import PartitionSpec as P

D = 768
HEADS = 12
HEAD_DIM = 64
FF = 2048
EXPERTS = 3
TOP = 2
ATT_BLOCK = 256
CAP = 192


EPSILON = 1e-05
VMEM_LIMIT = 66_000_000


def rotary_tables(positions):
    half_dim = HEAD_DIM // 2
    frequency = 10000.0 ** (-jnp.arange(half_dim, dtype=jnp.float32) / half_dim)
    angles = positions.astype(jnp.float32)[:, None] * frequency[None, :]
    return (jnp.cos(angles), jnp.sin(angles))


def rotate(values, cos_table, sine_table):
    half_dim = values.shape[-1] // 2
    first_half = values[..., :half_dim]
    second_half = values[..., half_dim:]
    cos_heads = cos_table[:, None, :]
    sine_heads = sine_table[:, None, :]
    return jnp.concatenate(
        [
            first_half * cos_heads - second_half * sine_heads,
            second_half * cos_heads + first_half * sine_heads,
        ],
        axis=-1,
    )


def unrotate(values, cos_table, sine_table):
    half_dim = values.shape[-1] // 2
    first_half = values[..., :half_dim]
    second_half = values[..., half_dim:]
    cos_heads = cos_table[:, None, :]
    sine_heads = sine_table[:, None, :]
    return jnp.concatenate(
        [
            first_half * cos_heads + second_half * sine_heads,
            second_half * cos_heads - first_half * sine_heads,
        ],
        axis=-1,
    )


def silu_grads(gate_in, up_in, upstream):
    sigmoid = jax.nn.sigmoid(gate_in)
    swish = gate_in * sigmoid
    slope = sigmoid * (1.0 + gate_in * (1.0 - sigmoid))
    return jnp.concatenate([upstream * up_in * slope, upstream * swish], axis=-1)


def block_mask(row_start, block_rows, length):
    query_block = (row_start + jnp.arange(block_rows, dtype=jnp.int32)) // ATT_BLOCK
    key_block = jnp.arange(length, dtype=jnp.int32) // ATT_BLOCK
    return key_block[None, :] <= query_block[:, None]


def attend_heads(received):
    packed = received[:, 0]
    length = packed.shape[0]
    heads_here = packed.shape[1]
    queries = packed[..., :HEAD_DIM]
    keys_all = packed[..., HEAD_DIM : 2 * HEAD_DIM]
    values_all = packed[..., 2 * HEAD_DIM :]
    block_rows = min(512, length)
    block_count = length // block_rows
    score_scale = HEAD_DIM ** (-0.5)

    def one_block(element):
        query_rows, row_start = element
        scores = (
            jnp.einsum("qhe,khe->hqk", query_rows, keys_all, preferred_element_type=jnp.float32)
            * score_scale
        )
        scores = jnp.where(block_mask(row_start, block_rows, length)[None], scores, -1e30)
        largest = jnp.max(scores, axis=-1, keepdims=True)
        weights_exp = jnp.exp(scores - largest)
        totals = jnp.sum(weights_exp, axis=-1, keepdims=True)
        attn_probs = (weights_exp / totals).astype(jnp.bfloat16)
        mixed_rows = jnp.einsum(
            "hqk,khe->qhe", attn_probs, values_all, preferred_element_type=jnp.float32
        )
        log_total = (largest + jnp.log(totals))[..., 0]
        return (mixed_rows.astype(jnp.bfloat16), jnp.transpose(log_total))

    blocked = queries.reshape(block_count, block_rows, heads_here, HEAD_DIM)
    starts = jnp.arange(block_count, dtype=jnp.int32) * block_rows
    mixed_rows, log_total = lax.map(one_block, (blocked, starts))
    return (
        mixed_rows.reshape(length, 1, heads_here, HEAD_DIM),
        log_total.reshape(length, 1, heads_here),
        received,
    )


def attend_back(received, log_sum, grad_in):
    packed = received[:, 0]
    length = packed.shape[0]
    heads_here = packed.shape[1]
    queries = packed[..., :HEAD_DIM]
    keys_all = packed[..., HEAD_DIM : 2 * HEAD_DIM]
    values_all = packed[..., 2 * HEAD_DIM :]
    block_rows = min(512, length)
    block_count = length // block_rows
    score_scale = HEAD_DIM ** (-0.5)

    def one_block(running, element):
        key_acc, value_acc = running
        query_rows, grad_rows, log_rows, row_start = element
        scores = (
            jnp.einsum("qhe,khe->hqk", query_rows, keys_all, preferred_element_type=jnp.float32)
            * score_scale
        )
        scores = jnp.where(block_mask(row_start, block_rows, length)[None], scores, -1e30)
        attn_probs = jnp.exp(scores - jnp.transpose(log_rows)[:, :, None])
        value_acc = value_acc + jnp.einsum(
            "hqk,qhe->khe",
            attn_probs.astype(jnp.bfloat16),
            grad_rows,
            preferred_element_type=jnp.float32,
        )
        grad_probs = jnp.einsum(
            "qhe,khe->hqk", grad_rows, values_all, preferred_element_type=jnp.float32
        )
        centre = jnp.sum(attn_probs * grad_probs, axis=-1, keepdims=True)
        grad_scores = (attn_probs * (grad_probs - centre)).astype(jnp.bfloat16)
        query_grad = (
            jnp.einsum("hqk,khe->qhe", grad_scores, keys_all, preferred_element_type=jnp.float32)
            * score_scale
        )
        key_acc = key_acc + jnp.einsum(
            "hqk,qhe->khe", grad_scores, query_rows, preferred_element_type=jnp.float32
        )
        return ((key_acc, value_acc), query_grad)

    empty_acc = jnp.zeros((length, heads_here, HEAD_DIM), jnp.float32)
    blocked_query = queries.reshape(block_count, block_rows, heads_here, HEAD_DIM)
    blocked_grad = grad_in[:, 0].reshape(block_count, block_rows, heads_here, HEAD_DIM)
    blocked_log = log_sum[:, 0].reshape(block_count, block_rows, heads_here)
    starts = jnp.arange(block_count, dtype=jnp.int32) * block_rows
    (key_acc, value_acc), query_grads = lax.scan(
        one_block, (empty_acc, empty_acc), (blocked_query, blocked_grad, blocked_log, starts)
    )
    stacked = jnp.stack(
        [query_grads.reshape(length, heads_here, HEAD_DIM), key_acc * score_scale, value_acc],
        axis=2,
    )
    return stacked.astype(jnp.bfloat16).reshape(length, 1, heads_here, 3 * HEAD_DIM)


def norm_back(values, scale_rows, gain_row, upstream):
    scaled = upstream * gain_row
    gain_term = jnp.sum(upstream * values * scale_rows, axis=0)
    value_grad = scale_rows * scaled - values * scale_rows**3 * jnp.mean(
        scaled * values, axis=-1, keepdims=True
    )
    return (gain_term, value_grad)


def on_device(
    inputs,
    attn_gain,
    qkv_weight,
    out_weight,
    ffn_gain,
    router_weight,
    expert_in,
    expert_out,
    shared_in,
    shared_out,
    routes,
    slot_index,
    cotangent,
):
    tok_rows = inputs.shape[1]
    group_count = lax.axis_size("seq")
    heads_group = HEADS // group_count
    stream = inputs[0].astype(jnp.float32)
    attn_local = (
        attn_gain.astype(jnp.bfloat16),
        qkv_weight.astype(jnp.bfloat16),
        out_weight.astype(jnp.bfloat16),
    )
    attn_full = (
        lax.all_gather(attn_local[0], "dp", axis=0, tiled=True),
        lax.all_gather(attn_local[1], "dp", axis=0, tiled=True),
        lax.all_gather(attn_local[2], "dp", axis=0, tiled=True),
    )
    gain_first, qkv_full, out_full = attn_full
    positions = lax.axis_index("seq") * tok_rows + jnp.arange(tok_rows, dtype=jnp.int32)
    cos_table, sine_table = rotary_tables(positions)
    scale_one = lax.rsqrt(jnp.mean(stream * stream, axis=-1, keepdims=True) + EPSILON)
    gain_one_f = gain_first.astype(jnp.float32)
    normed = (stream * scale_one * gain_one_f).astype(jnp.bfloat16)
    projected = jnp.einsum("td,dhce->thce", normed, qkv_full, preferred_element_type=jnp.float32)
    rotated = jnp.stack(
        [
            rotate(projected[:, :, 0], cos_table, sine_table),
            rotate(projected[:, :, 1], cos_table, sine_table),
            projected[:, :, 2],
        ],
        axis=2,
    ).astype(jnp.bfloat16)
    outgoing = rotated.reshape(tok_rows, group_count, heads_group, 3 * HEAD_DIM)
    head_out, log_sum, head_qkv = attend_heads(
        lax.all_to_all(outgoing, "seq", split_axis=1, concat_axis=0, tiled=True)
    )
    attended = lax.all_to_all(head_out, "seq", split_axis=0, concat_axis=1, tiled=True).reshape(
        tok_rows, D
    )
    middle = stream + jnp.dot(attended, out_full, preferred_element_type=jnp.float32)
    ffn_local = (
        ffn_gain.astype(jnp.bfloat16),
        router_weight.astype(jnp.bfloat16),
        expert_in.astype(jnp.bfloat16),
        expert_out.astype(jnp.bfloat16),
        shared_in.astype(jnp.bfloat16),
        shared_out.astype(jnp.bfloat16),
    )
    ffn_full = (
        lax.all_gather(ffn_local[0], "dp", axis=0, tiled=True),
        lax.all_gather(ffn_local[1], "dp", axis=0, tiled=True),
        lax.all_gather(ffn_local[2], "dp", axis=1, tiled=True),
        lax.all_gather(ffn_local[3], "dp", axis=1, tiled=True),
        lax.all_gather(ffn_local[4], "dp", axis=0, tiled=True),
        lax.all_gather(ffn_local[5], "dp", axis=0, tiled=True),
    )
    gain_second, router_full, exp_in_full, exp_out_full, sh_in_full, sh_out_full = ffn_full
    scale_two = lax.rsqrt(jnp.mean(middle * middle, axis=-1, keepdims=True) + EPSILON)
    gain_two_f = gain_second.astype(jnp.float32)
    normed_two = (middle * scale_two * gain_two_f).astype(jnp.bfloat16)
    logits = jnp.dot(normed_two, router_full, preferred_element_type=jnp.float32)
    router_probs = jax.nn.softmax(logits, axis=-1)
    route_rows = routes[0]
    choice_hot = (
        route_rows[:, :, None] == jnp.arange(EXPERTS, dtype=jnp.int32)[None, None, :]
    ).astype(jnp.float32)
    gate_values = jnp.sum(choice_hot * router_probs[:, None, :], axis=-1)
    flat_slot = (route_rows * CAP + slot_index[0]).reshape(-1)
    buffer = (
        jnp.zeros((EXPERTS * CAP, D), jnp.bfloat16)
        .at[flat_slot]
        .set(jnp.repeat(normed_two, TOP, axis=0))
        .reshape(EXPERTS, CAP, D)
    )
    gate_up = jnp.einsum("ecd,edf->ecf", buffer, exp_in_full, preferred_element_type=jnp.float32)
    activated = (jax.nn.silu(gate_up[..., :FF]) * gate_up[..., FF:]).astype(jnp.bfloat16)
    expert_rows = jnp.einsum(
        "ecf,efd->ecd", activated, exp_out_full, preferred_element_type=jnp.float32
    ).reshape(EXPERTS * CAP, D)
    picked = expert_rows[flat_slot].reshape(tok_rows, TOP, D)
    mixture = jnp.sum(gate_values[:, :, None] * picked, axis=1)
    shared_gu = jnp.dot(normed_two, sh_in_full, preferred_element_type=jnp.float32)
    shared_act = (jax.nn.silu(shared_gu[:, :FF]) * shared_gu[:, FF:]).astype(jnp.bfloat16)
    result = middle + mixture + jnp.dot(shared_act, sh_out_full, preferred_element_type=jnp.float32)
    output = result.astype(jnp.bfloat16)[None]
    ffn_back = (
        lax.all_gather(ffn_local[0], "dp", axis=0, tiled=True),
        lax.all_gather(ffn_local[1], "dp", axis=0, tiled=True),
        lax.all_gather(ffn_local[2], "dp", axis=1, tiled=True),
        lax.all_gather(ffn_local[3], "dp", axis=1, tiled=True),
        lax.all_gather(ffn_local[4], "dp", axis=0, tiled=True),
        lax.all_gather(ffn_local[5], "dp", axis=0, tiled=True),
    )
    router_back, exp_in_back, exp_out_back, sh_in_back, sh_out_back = (
        ffn_back[1],
        ffn_back[2],
        ffn_back[3],
        ffn_back[4],
        ffn_back[5],
    )
    upstream = cotangent[0].astype(jnp.float32)
    grad_low = upstream.astype(jnp.bfloat16)
    shared_out_grad = jnp.einsum(
        "tf,td->fd", shared_act, grad_low, preferred_element_type=jnp.float32
    )
    shared_act_grad = jnp.einsum(
        "td,fd->tf", grad_low, sh_out_back, preferred_element_type=jnp.float32
    )
    shared_gu_grad = silu_grads(shared_gu[:, :FF], shared_gu[:, FF:], shared_act_grad).astype(
        jnp.bfloat16
    )
    shared_in_grad = jnp.einsum(
        "td,tf->df", normed_two, shared_gu_grad, preferred_element_type=jnp.float32
    )
    norm_grad_two = jnp.einsum(
        "tf,df->td", shared_gu_grad, sh_in_back, preferred_element_type=jnp.float32
    )
    slot_terms = (gate_values[:, :, None] * upstream[:, None, :]).reshape(tok_rows * TOP, D)
    slot_grad = (
        jnp.zeros((EXPERTS * CAP, D), jnp.float32)
        .at[flat_slot]
        .set(slot_terms)
        .astype(jnp.bfloat16)
        .reshape(EXPERTS, CAP, D)
    )
    expert_out_grad = jnp.einsum(
        "ecf,ecd->efd", activated, slot_grad, preferred_element_type=jnp.float32
    )
    activated_grad = jnp.einsum(
        "ecd,efd->ecf", slot_grad, exp_out_back, preferred_element_type=jnp.float32
    )
    gate_up_grad = silu_grads(gate_up[..., :FF], gate_up[..., FF:], activated_grad).astype(
        jnp.bfloat16
    )
    expert_in_grad = jnp.einsum(
        "ecd,ecf->edf", buffer, gate_up_grad, preferred_element_type=jnp.float32
    )
    buffer_grad = jnp.einsum(
        "ecf,edf->ecd", gate_up_grad, exp_in_back, preferred_element_type=jnp.float32
    ).reshape(EXPERTS * CAP, D)
    norm_grad_two = norm_grad_two + jnp.sum(
        buffer_grad[flat_slot].reshape(tok_rows, TOP, D), axis=1
    )
    gate_grad = jnp.sum(upstream[:, None, :] * picked, axis=-1)
    prob_grad = jnp.sum(choice_hot * gate_grad[:, :, None], axis=1)
    logit_grad = (
        router_probs * (prob_grad - jnp.sum(router_probs * prob_grad, axis=-1, keepdims=True))
    ).astype(jnp.bfloat16)
    router_weight_grad = jnp.einsum(
        "td,te->de", normed_two, logit_grad, preferred_element_type=jnp.float32
    )
    norm_grad_two = norm_grad_two + jnp.einsum(
        "te,de->td", logit_grad, router_back, preferred_element_type=jnp.float32
    )
    ffn_gain_term, middle_part = norm_back(middle, scale_two, gain_two_f, norm_grad_two)
    middle_grad = upstream + middle_part
    attn_back = (
        lax.all_gather(attn_local[0], "dp", axis=0, tiled=True),
        lax.all_gather(attn_local[1], "dp", axis=0, tiled=True),
        lax.all_gather(attn_local[2], "dp", axis=0, tiled=True),
    )
    qkv_back, out_back = (attn_back[1], attn_back[2])
    middle_low = middle_grad.astype(jnp.bfloat16)
    out_weight_grad = jnp.einsum(
        "tf,td->fd", attended, middle_low, preferred_element_type=jnp.float32
    )
    attended_grad = jnp.einsum(
        "td,fd->tf", middle_low, out_back, preferred_element_type=jnp.float32
    ).astype(jnp.bfloat16)
    head_grad = lax.all_to_all(
        attended_grad.reshape(tok_rows, group_count, heads_group, HEAD_DIM),
        "seq",
        split_axis=1,
        concat_axis=0,
        tiled=True,
    )
    stacked = attend_back(head_qkv, log_sum, head_grad)
    returned = (
        lax.all_to_all(stacked, "seq", split_axis=0, concat_axis=1, tiled=True)
        .reshape(tok_rows, HEADS, 3, HEAD_DIM)
        .astype(jnp.float32)
    )
    projected_grad = jnp.stack(
        [
            unrotate(returned[:, :, 0], cos_table, sine_table),
            unrotate(returned[:, :, 1], cos_table, sine_table),
            returned[:, :, 2],
        ],
        axis=2,
    ).astype(jnp.bfloat16)
    qkv_weight_grad = jnp.einsum(
        "td,thce->dhce", normed, projected_grad, preferred_element_type=jnp.float32
    )
    norm_grad = jnp.einsum(
        "thce,dhce->td", projected_grad, qkv_back, preferred_element_type=jnp.float32
    )
    attn_gain_term, input_part = norm_back(stream, scale_one, gain_one_f, norm_grad)
    input_grad = (middle_grad + input_part)[None]
    parts = (
        lax.psum_scatter(
            qkv_weight_grad.astype(jnp.bfloat16), "seq", scatter_dimension=1, tiled=True
        ).astype(jnp.float32),
        lax.psum_scatter(
            out_weight_grad.astype(jnp.bfloat16), "seq", scatter_dimension=1, tiled=True
        ).astype(jnp.float32),
        lax.psum_scatter(
            expert_in_grad.astype(jnp.bfloat16), "seq", scatter_dimension=2, tiled=True
        ).astype(jnp.float32),
        lax.psum_scatter(
            expert_out_grad.astype(jnp.bfloat16), "seq", scatter_dimension=2, tiled=True
        ).astype(jnp.float32),
        lax.psum_scatter(
            shared_in_grad.astype(jnp.bfloat16), "seq", scatter_dimension=1, tiled=True
        ).astype(jnp.float32),
        lax.psum_scatter(
            shared_out_grad.astype(jnp.bfloat16), "seq", scatter_dimension=1, tiled=True
        ).astype(jnp.float32),
    )
    owned = (
        lax.psum_scatter(attn_gain_term, "dp", scatter_dimension=0, tiled=True),
        lax.psum_scatter(ffn_gain_term, "dp", scatter_dimension=0, tiled=True),
        lax.psum_scatter(router_weight_grad, "dp", scatter_dimension=0, tiled=True),
        lax.psum_scatter(parts[0], "dp", scatter_dimension=0, tiled=True),
        lax.psum_scatter(parts[1], "dp", scatter_dimension=0, tiled=True),
        lax.psum_scatter(parts[2], "dp", scatter_dimension=1, tiled=True),
        lax.psum_scatter(parts[3], "dp", scatter_dimension=1, tiled=True),
        lax.psum_scatter(parts[4], "dp", scatter_dimension=0, tiled=True),
        lax.psum_scatter(parts[5], "dp", scatter_dimension=0, tiled=True),
    )
    small = lax.psum((owned[0], owned[1], owned[2]), "seq")
    joined = (
        lax.all_gather(owned[3].astype(jnp.bfloat16), "seq", axis=1, tiled=True).astype(
            jnp.float32
        ),
        lax.all_gather(owned[4].astype(jnp.bfloat16), "seq", axis=1, tiled=True).astype(
            jnp.float32
        ),
        lax.all_gather(owned[5].astype(jnp.bfloat16), "seq", axis=2, tiled=True).astype(
            jnp.float32
        ),
        lax.all_gather(owned[6].astype(jnp.bfloat16), "seq", axis=2, tiled=True).astype(
            jnp.float32
        ),
        lax.all_gather(owned[7].astype(jnp.bfloat16), "seq", axis=1, tiled=True).astype(
            jnp.float32
        ),
        lax.all_gather(owned[8].astype(jnp.bfloat16), "seq", axis=1, tiled=True).astype(
            jnp.float32
        ),
    )
    return (
        output,
        input_grad,
        small[0],
        joined[0],
        joined[1],
        small[1],
        small[2],
        joined[2],
        joined[3],
        joined[4],
        joined[5],
    )


MESH = pl.DeviceIdType.MESH
BF = jnp.bfloat16
F32 = jnp.float32
TOK = ATT_BLOCK
QKV_PAD = 640
FAR3 = 5
RSY0 = 5


def nn(a, b):
    return lax.dot_general(a, b, (((1,), (0,)), ((), ())), preferred_element_type=F32)


def nt(a, b):
    return lax.dot_general(a, b, (((1,), (1,)), ((), ())), preferred_element_type=F32)


def tn(a, b):
    return lax.dot_general(a, b, (((0,), (0,)), ((), ())), preferred_element_type=F32)


def swap_halves(v):
    lane = lax.broadcasted_iota(jnp.int32, v.shape, 1)
    return jnp.where(lax.rem(lane, 64) < 32, pltpu.roll(v, 96, 1), pltpu.roll(v, 32, 1))


def layer_kernel(names, *refs):
    r = types.SimpleNamespace(**dict(zip(names, refs)))
    b = lax.axis_index("dp")
    s = lax.axis_index("seq")
    z = lax.div(b, 2)
    y = lax.rem(b, 2)
    z1 = lax.div(b, 4)
    z0 = lax.rem(z, 2)
    x = lax.div(s, 2)
    c = lax.rem(s, 2)
    zf = z + 1 - 2 * z0
    zg = z + 2 - 4 * z1
    zh = zf + 2 - 4 * z1
    core = (b, s + 1 - 2 * c)
    xp = (b, s + 2 - 4 * x)
    diag = (b, 3 - s)
    yp = (b + 1 - 2 * y, s)
    z0p = (b + 2 - 4 * z0, s)
    z1p = (b + 4 - 8 * z1, s)
    inner = lax.div(z + 1, 2) == 1
    zip_ = (b + 6 - 4 * z, s)
    p1 = (b + c * (2 - 4 * z0), s + (1 - c) * (2 - 4 * x))
    p2 = (b + (1 - c) * (2 - 4 * z0), s + c * (2 - 4 * x))
    jme = z0 * 2 + x
    jx = z0 * 2 + 1 - x
    jz = (1 - z0) * 2 + x
    jd = (1 - z0) * 2 + 1 - x
    jp1 = jx + c * (jz - jx)
    jp2 = jz + c * (jx - jz)
    oc = 1 - c
    oy = 1 - y

    def send(src, dst, ss, rs, dev):
        pltpu.make_async_remote_copy(
            src_ref=src, dst_ref=dst, send_sem=ss, recv_sem=rs, device_id=dev, device_id_type=MESH
        ).start()

    def sent(src, ss):
        pltpu.make_async_remote_copy(
            src_ref=src, dst_ref=src, send_sem=ss, recv_sem=ss, device_id=core, device_id_type=MESH
        ).wait_send()

    def got(dst, rs):
        pltpu.make_async_remote_copy(
            src_ref=dst, dst_ref=dst, send_sem=rs, recv_sem=rs, device_id=core, device_id_type=MESH
        ).wait_recv()

    def ag_first(src, slot, ss, rs):
        send(src, slot(z, y), ss(0), rs(b), z0p)

        @pl.when(inner)
        def _():
            send(src, slot(z, y), ss(7), rs(b), zip_)

    def ag_own(slot, ss, rs):
        send(slot(z, y), slot(z, y), ss(1), rs(b), z1p)
        send(slot(z, y), slot(z, y), ss(2), rs(b), yp)

    def ag_z0(slot, ss, rs):
        k = 2 * zf + y
        got(slot(zf, y), rs(k))

        @pl.when(inner)
        def _():
            send(slot(zf, y), slot(zf, y), ss(3), rs(k), z1p)

        send(slot(zf, y), slot(zf, y), ss(4), rs(k), yp)

    def ag_z1(slot, ss, rs):
        for zz, n in ((zg, 5), (zh, 6)):
            k = 2 * zz + y
            got(slot(zz, y), rs(k))
            send(slot(zz, y), slot(zz, y), ss(n), rs(k), yp)

    def ag_fin(slot, rs):
        for zz in range(4):
            got(slot(zz, oy), rs(2 * zz + oy))

    def ag_sent(src, slot, ss):
        sent(src, ss(0))
        for n in (1, 2, 4, 5, 6):
            sent(slot(z, y), ss(n))

        @pl.when(inner)
        def _():
            sent(slot(z, y), ss(3))
            sent(src, ss(7))

    def tok_own(slot, n):
        own = slot(jme, c)
        send(own, own, r.tok_s.at[n, 1], r.tok_r.at[n, 2], p1)
        send(own, own, r.tok_s.at[n, 2], r.tok_r.at[n, 4], p2)
        send(own, own, r.tok_s.at[n, 0], r.tok_r.at[n, 1], core)

    def tok_near(slot, n):
        v = slot(jp1, c)
        got(v, r.tok_r.at[n, 2])
        send(v, v, r.tok_s.at[n, 3], r.tok_r.at[n, 6], p2)
        send(v, v, r.tok_s.at[n, 4], r.tok_r.at[n, 5], core)
        v = slot(jp2, c)
        got(v, r.tok_r.at[n, 4])
        send(v, v, r.tok_s.at[n, 5], r.tok_r.at[n, 3], core)

    def tok_far(slot, n):
        v = slot(jd, c)
        got(v, r.tok_r.at[n, 6])
        send(v, v, r.tok_s.at[n, 6], r.tok_r.at[n, 7], core)

    def tok_fin(slot, n):
        got(slot(jme, oc), r.tok_r.at[n, 1])
        got(slot(jp1, oc), r.tok_r.at[n, 3])
        got(slot(jp2, oc), r.tok_r.at[n, 5])
        got(slot(jd, oc), r.tok_r.at[n, 7])

    def tok_sent(slot, n):
        for k in range(7):
            sent(slot(jme, c), r.tok_s.at[n, k])

    cot_slot = lambda j, k: r.cota.at[j, k]
    sel_slot = lambda j, k: r.nta.at[j, k, :, pl.ds(D, 128)]
    two_slot = lambda j, k: r.nta.at[j, k, :, pl.ds(0, D)]

    def block_at(q):
        q1 = lax.rem(q, 2)
        q2 = lax.div(q, 2)
        fx = q1 + c * (q2 - q1)
        fz = q2 + c * (q1 - q2)
        return 2 * (z0 + fz * (1 - 2 * z0)) + x + fx * (1 - 2 * x)

    def sum_first(buf, rc, n):
        send(buf.at[:, oc], rc, r.sum_s.at[n, 0], r.sum_r.at[n, 0], core)

    def sum_core(buf, rc, rp, n):
        got(rc, r.sum_r.at[n, 0])
        for j in range(4):
            v = buf[j, c].astype(F32) + rc[j].astype(F32)
            buf[j, c] = v.astype(BF)
        send(buf.at[jd, c], rp.at[0], r.sum_s.at[n, 1], r.sum_r.at[n, 1], p2)
        send(buf.at[jp2, c], rp.at[1], r.sum_s.at[n, 2], r.sum_r.at[n, 2], p2)

    def sum_relay(buf, rp, n):
        got(rp.at[0], r.sum_r.at[n, 1])
        buf[jp1, c] = (buf[jp1, c].astype(F32) + rp[0].astype(F32)).astype(BF)
        send(buf.at[jp1, c], rp.at[2], r.sum_s.at[n, 3], r.sum_r.at[n, 3], p1)

    def sum_fin(buf, rc, rp, n):
        got(rp.at[1], r.sum_r.at[n, 2])
        got(rp.at[2], r.sum_r.at[n, 3])
        total = buf[jme, c].astype(F32) + rp[1].astype(F32) + rp[2].astype(F32)
        sent(rc, r.sum_s.at[n, 0])
        for k in range(1, 4):
            sent(rp.at[0], r.sum_s.at[n, k])
        return total

    barrier = pltpu.get_barrier_semaphore()
    peers = (core, xp, diag, yp, z0p, z1p, zip_)
    for dev in peers:
        pl.semaphore_signal(barrier, inc=1, device_id=dev, device_id_type=MESH)

    def stage_copies():
        out = []
        for m in range(4):
            for zz in range(2):
                for h in range(2):
                    for k in range(2):
                        zt = z0 + zz * (1 - 2 * z0)
                        col = pl.multiple_of(
                            h * 2048 + 1024 * k + 512 * zt + 256 * c + 128 * x, 128
                        )
                        if m < 3:
                            src = r.e_in.at[m, :, pl.ds(col, 128)]
                        else:
                            src = r.s_in.at[:, pl.ds(col, 128)]
                        at = (h * 2 + k) * 128
                        q = 2 * m + zz
                        dst = r.acc.at[q // 2, q % 2, pl.ds(0, 96), pl.ds(at, 128)]
                        out.append((src, dst, r.stage_sem.at[m, zz * 4 + h * 2 + k]))
            row = pl.multiple_of(128 * x, 128)
            if m < 3:
                src = r.e_out.at[m, pl.ds(row, 128), :]
            else:
                src = r.s_out.at[pl.ds(row, 128), :]
            dst = r.acc.at[m // 2, m % 2, pl.ds(96, 128), pl.ds(0, D)]
            out.append((src, dst, r.stage_sem.at[m, 8]))
        return [pltpu.make_async_copy(*one) for one in out]

    staged = stage_copies()
    for one in staged:
        one.start()

    q_slot = lambda zz, yy: r.wq.at[zz, yy]
    q_ss = lambda n: r.att_s.at[0, n]
    q_rs = lambda n: r.att_r.at[0, n]
    o_slot = lambda zz, yy: r.ow.at[zz, yy, c]
    o_ss = lambda n: r.att_s.at[1, n]
    o_rs = lambda n: r.att_r.at[1, n]
    m_slot = lambda zz, yy: r.misc.at[zz, yy]
    m_ss = lambda n: r.att_s.at[2, n]
    m_rs = lambda n: r.att_r.at[2, n]

    def w_slot(m):
        return lambda zz, yy: r.win.at[m, zz, yy]

    def w_ss(m):
        return lambda n: r.w_s.at[m, n]

    def w_rs(m):
        return lambda n: r.w_r.at[m, n]

    r.wq[z, y] = r.wq_in[...]
    r.misc[z, y] = r.misc_in[...]
    r.ow[z, y, c] = r.ow_in[...]
    r.nall[s] = r.x_in[...]
    r.cota[jme, c] = r.cot_in[...]
    r.nta[jme, c, :, D : D + 128] = r.sel_in[...]

    pl.semaphore_wait(barrier, len(peers))

    send(r.x_in, r.nall.at[s], r.x_s.at[0], r.x_r.at[0], core)
    send(r.x_in, r.nall.at[s], r.x_s.at[1], r.x_r.at[1], xp)
    ow_set = (r.ow_in, o_slot, o_ss, o_rs)
    att_sets = ((r.misc_in, m_slot, m_ss, m_rs), (r.wq_in, q_slot, q_ss, q_rs))
    for src, slot, ss, rs in att_sets:
        ag_first(src, slot, ss, rs)
        ag_own(slot, ss, rs)

    for one in staged:
        one.wait()
    for m in range(4):
        q = 2 * m
        r.win[m, z, y] = r.acc[q // 2, q % 2, 0:96, 0:512].astype(BF)
        q = 2 * m + 1
        r.dg[m, 0:96, :] = r.acc[q // 2, q % 2, 0:96, 0:512].astype(BF)

    @pl.when(c == y)
    def _():
        for m in range(4):
            r.wout[m, z1] = r.acc[m // 2, m % 2, 96:224, 0:D].astype(BF)

    xf = s + 2 - 4 * x
    for src, slot, ss, rs in att_sets:
        ag_z0(slot, ss, rs)
    got(r.nall.at[xf], r.x_r.at[1])
    send(r.nall.at[xf], r.nall.at[xf], r.x_s.at[2], r.x_r.at[2], core)
    def w_first(m):
        ag_first(r.dg.at[m, pl.ds(0, 96)], w_slot(m), w_ss(m), w_rs(m))

    def w_own(m):
        ag_own(w_slot(m), w_ss(m), w_rs(m))

        @pl.when(c == y)
        def _():
            v = r.wout.at[m, z1]
            send(v, v, r.o_s.at[m, 0], r.o_r.at[m, z1], z1p)
            send(v, v, r.o_s.at[m, 1], r.o_r.at[m, z1], yp)

    def w_relay(m):
        ag_z0(w_slot(m), w_ss(m), w_rs(m))

    def w_relay_far(m):
        ag_z1(w_slot(m), w_ss(m), w_rs(m))

        @pl.when(c == y)
        def _():
            v = r.wout.at[m, 1 - z1]
            got(v, r.o_r.at[m, 1 - z1])
            send(v, v, r.o_s.at[m, 2], r.o_r.at[m, 1 - z1], yp)

    def w_fin(m):
        ag_fin(w_slot(m), w_rs(m))

        @pl.when(c != y)
        def _():
            got(r.wout.at[m, 0], r.o_r.at[m, 0])
            got(r.wout.at[m, 1], r.o_r.at[m, 1])

        for n in (1, 2, 4, 5, 6):
            sent(r.win.at[m, z, y], r.w_s.at[m, n])

        @pl.when(inner)
        def _():
            sent(r.win.at[m, z, y], r.w_s.at[m, 3])

        @pl.when(c == y)
        def _():
            for k in range(3):
                sent(r.wout.at[m, 0], r.o_s.at[m, k])

    w_first(0)
    for src, slot, ss, rs in att_sets:
        ag_z1(slot, ss, rs)
    ag_first(*ow_set)
    ag_own(*ow_set[1:])
    tok_own(sel_slot, 2)
    tok_own(cot_slot, 0)
    w_first(1)
    for src, slot, ss, rs in att_sets:
        ag_fin(slot, rs)

    w_own(0)
    w_relay(0)

    rows = jnp.zeros((8, D), F32)
    for k in range(8):
        row_i = lax.broadcasted_iota(jnp.int32, (128, D), 0)
        col_i = lax.broadcasted_iota(jnp.int32, (128, D), 1)
        place = jnp.where((col_i == row_i + 96 * k) & (row_i < 96), 1.0, 0.0).astype(BF)
        rows = rows + nn(r.misc[k // 2, k % 2].astype(BF), place)
    r.mrow[...] = rows
    row8 = lax.broadcasted_iota(jnp.int32, (8, D), 0)
    r.rpad[...] = jnp.zeros((128, D), BF)
    r.rpad[0:16, :] = jnp.concatenate(
        [jnp.where(row8 < 3, rows, 0.0), jnp.zeros((8, D), F32)], axis=0
    ).astype(BF)

    got(r.nall.at[s + 1 - 2 * c], r.x_r.at[0])
    got(r.nall.at[3 - s], r.x_r.at[2])
    for k in range(3):
        sent(r.x_in, r.x_s.at[k])
    wq = r.wq[...].reshape(D, QKV_PAD)
    lane128 = lax.broadcasted_iota(jnp.int32, (TOK, 128), 1)

    def project(t, carry):
        xv = r.nall[t].astype(F32)
        r1 = lax.rsqrt(jnp.mean(xv * xv, axis=-1, keepdims=True) + EPSILON)
        nb = (xv * r1 * r.mrow[3:4, :]).astype(BF)
        r.nall[t] = nb
        pr = nn(nb, r.wq[...].reshape(D, QKV_PAD))
        at = pl.ds(pl.multiple_of(t * TOK, TOK), TOK)
        cosv = r.cos_in[at, :]
        sinv = r.sin_in[at, :]
        for h in range(3):
            hc = 128 * h + 128 * (h // 2)
            g = pr[:, hc : hc + 128]
            g = (g * cosv + swap_halves(g) * sinv).astype(BF).astype(F32)
            g = jnp.where(lane128 < 64, g * 0.125, g)
            r.kq[h, at, :] = pltpu.roll(g, 64, 1).astype(BF)
        r.val[0, at, :] = pr[:, 256:384].astype(BF)
        r.val[1, at, :] = pr[:, 512:640].astype(BF)
        return carry

    lax.fori_loop(0, 4, project, 0)

    ag_z0(*ow_set[1:])
    w_own(1)
    w_relay(1)
    w_first(2)
    ag_z1(*ow_set[1:])
    tok_near(sel_slot, 2)
    tok_near(cot_slot, 0)

    for i in range(3, -1, -1):
        n = (i + 1) * TOK
        base = i * (i + 1) // 2

        def heads(h, carry, i=i, n=n, base=base):
            q = pltpu.roll(r.kq[h, i * TOK : i * TOK + TOK, :].astype(F32), 64, 1)
            q = jnp.where(lane128 < 64, q, 0.0)
            sc = nt(q.astype(BF), r.kq[h, 0:n, :])
            top = jnp.max(sc, axis=-1, keepdims=True)
            e = jnp.exp(sc - top)
            pb = (e * (1.0 / jnp.sum(e, axis=-1, keepdims=True))).astype(BF)
            for j in range(i + 1):
                r.prob[h, base + j] = pb[:, j * TOK : j * TOK + TOK]
            r.acc[h, 0, :, 0:128] = nn(pb, r.val[lax.div(h, 2), 0:n, :])
            return carry

        lax.fori_loop(0, 3, heads, 0)
        r.att[i, :, 0:128] = jnp.where(lane128 < 64, r.acc[0, 0, :, 0:128], r.acc[1, 0, :, 0:128]).astype(BF)
        r.att[i, :, 128:256] = r.acc[2, 0, :, 0:128].astype(BF)

        @pl.when(s != i)
        def _(i=i):
            send(r.att.at[i], r.arow.at[s], r.a_s.at[i], r.a_r.at[s], (b, i))

        @pl.when(s == i)
        def _(i=i):
            r.arow[i] = r.att[i]

        if i == 1:
            ag_fin(o_slot, o_rs)
            send(r.ow.at[:, :, c], r.ow.at[:, :, c], r.ow_s.at[0], r.ow_r.at[0], core)
        if i == 2:
            w_relay_far(0)
            tok_far(sel_slot, 2)
            tok_far(cot_slot, 0)
            w_first(3)
        if i == 0:
            w_relay_far(1)

    got(r.ow.at[:, :, oc], r.ow_r.at[0])
    sent(r.ow.at[:, :, c], r.ow_s.at[0])
    for src, slot, ss, rs in att_sets + (ow_set,):
        ag_sent(src, slot, ss)
    for i in range(4):

        @pl.when(s != i)
        def _(i=i):
            got(r.arow.at[i], r.a_r.at[i])
            sent(r.att.at[i], r.a_s.at[i])

    ow = r.ow[...].reshape(D, D)
    mid = r.x_in[...].astype(F32)
    for i in range(4):
        mid = mid + nn(r.arow[i][:, 0:192], ow[192 * i : 192 * i + 192, :])
    r.mid[...] = mid
    r2 = lax.rsqrt(jnp.mean(mid * mid, axis=-1, keepdims=True) + EPSILON)
    nb = (mid * r2 * r.mrow[4:5, :]).astype(BF)
    r.nta[jme, c, :, 0:D] = nb
    tok_own(two_slot, 1)
    tok_fin(sel_slot, 2)
    tok_fin(cot_slot, 0)

    def gates(nv):
        lg = nt(nv, r.rpad[...])
        lg = jnp.where(lane128 < 3, lg, -1e30)
        e = jnp.exp(lg - jnp.max(lg, axis=-1, keepdims=True))
        return e / jnp.sum(e, axis=-1, keepdims=True)

    def route(j, k):
        sel = r.nta[j, k, :, D : D + 128].astype(F32)
        pv = gates(r.nta[j, k, :, 0:D])
        gv = jnp.where(lane128 < 3, pv * sel, jnp.where(lane128 == 3, sel, 0.0))
        r.acc[j, k, :, 0:D] = jnp.zeros((TOK, D), F32)
        r.acc[j, k, :, D : D + 128] = pltpu.roll(gv, 64, 1)

    def rs_first(m):
        send(r.win.at[m, :, oy], r.ry_in.at[m], r.rs_s.at[m, 0], r.rs_r.at[m, 0], yp)

        @pl.when(c != y)
        def _():
            send(r.gout.at[m], r.ry_out.at[m], r.rs_s.at[m, 1], r.rs_r.at[m, 1], yp)

    def out_rows(m, k):
        at = pl.ds(pl.multiple_of(128 * k, 128), 128)
        return r.gs_out.at[at] if m == 3 else r.ge_out.at[m, at]

    def rs_y(m):
        got(r.ry_in.at[m], r.rs_r.at[m, 0])
        for zz in range(4):
            r.win[m, zz, y] = (r.win[m, zz, y].astype(F32) + r.ry_in[m, zz].astype(F32)).astype(BF)
        send(
            r.win.at[m, pl.ds(2 - 2 * z1, 2), y], r.rz_in.at[m], r.rs_s.at[m, 2], r.rs_r.at[m, 2], z1p
        )

        @pl.when(c == y)
        def _():
            got(r.ry_out.at[m], r.rs_r.at[m, 1])
            for k in range(2):
                r.gout[m, k] = (r.gout[m, k].astype(F32) + r.ry_out[m, k].astype(F32)).astype(BF)
            send(r.gout.at[m, 1 - z1], r.rz_out.at[m], r.rs_s.at[m, 3], r.rs_r.at[m, 3], z1p)

    def rs_z(m):
        got(r.rz_in.at[m], r.rs_r.at[m, 2])
        for k in range(2):
            zz = 2 * z1 + k
            r.win[m, zz, y] = (r.win[m, zz, y].astype(F32) + r.rz_in[m, k].astype(F32)).astype(BF)
        send(r.win.at[m, zf, y], r.rzz.at[m], r.rs_s.at[m, 4], r.rs_r.at[m, 4], z0p)

        @pl.when(c == y)
        def _():
            got(r.rz_out.at[m], r.rs_r.at[m, 3])
            v = (r.gout[m, z1].astype(F32) + r.rz_out[m].astype(F32)).astype(BF)
            r.gout[m, z1] = v
            g = r.gout.at[m, z1]
            pltpu.make_async_copy(g, out_rows(m, x), r.loc.at[m, 1]).start()
            send(g, out_rows(m, x), r.rs_s.at[m, 5], r.rs_r.at[m, 5], xp)
            send(g, out_rows(m, x), r.rs_s.at[m, 6], r.rs_r.at[m, 6], core)

    def part(m, sx, sc):
        return r.ga.at[2 * m + sx, pl.ds(0, 192), pl.ds(pl.multiple_of(512 * sc, 512), 512)]

    def rs_join(m):
        got(r.rzz.at[m], r.rs_r.at[m, 4])
        cols = pl.ds(pl.multiple_of(512 * c, 512), 512)
        mine = pl.ds(pl.multiple_of(96 * z0, 96), 96)
        theirs = pl.ds(pl.multiple_of(96 - 96 * z0, 96), 96)
        r.ga[2 * m + x, mine, cols] = r.win[m, z, y]
        r.ga[2 * m + x, theirs, cols] = r.rzz[m]
        g = part(m, x, c)
        send(g, g, r.rs_s.at[m, 7], r.rs_r.at[m, 7], xp)
        send(g, g, r.rs_s.at[m, 8], r.rs_r.at[m, 8], core)

    def rs_spread(m):
        g = part(m, 1 - x, c)
        got(g, r.rs_r.at[m, 7])
        send(g, g, r.rs_s.at[m, 9], r.rs_r.at[m, 9], core)

        @pl.when(c == y)
        def _():
            v = out_rows(m, 1 - x)
            got(v, r.rs_r.at[m, 5])
            send(v, v, r.rs_s.at[m, 10], r.rs_r.at[m, 10], core)

    def rs_end(m):
        got(part(m, x, oc), r.rs_r.at[m, 8])
        got(part(m, 1 - x, oc), r.rs_r.at[m, 9])
        for k in range(8):
            h, kz, zz = k // 4, k // 2 % 2, k % 2
            for q in range(4):
                sc, sx = q // 2, q % 2
                at = 512 * sc + 128 * (2 * h + kz)
                v = r.ga[2 * m + sx, 96 * zz : 96 * zz + 96, at : at + 128]
                if h == 0:
                    r.ry_in[m, k, :, 128 * q : 128 * q + 128] = v
                else:
                    row = 96 * (k % 2)
                    r.dg[2 * m + kz, row : row + 96, 128 * q : 128 * q + 128] = v
            src = r.ry_in.at[m, k] if h == 0 else r.dg.at[2 * m + kz, pl.ds(96 * (k % 2), 96)]
            dst = r.gs_in if m == 3 else r.ge_in.at[m]
            pltpu.make_async_copy(src, dst.at[:, pl.ds(512 * k, 512)], r.fin.at[m, k]).start()
        sent(r.ry_in.at[m], r.rs_s.at[m, 0])
        sent(r.rz_in.at[m], r.rs_s.at[m, 2])
        sent(r.win.at[m, zf, y], r.rs_s.at[m, 4])
        for k in (7, 8, 9):
            sent(part(m, x, c), r.rs_s.at[m, k])

        @pl.when(c != y)
        def _():
            sent(r.gout.at[m], r.rs_s.at[m, 1])
            got(out_rows(m, x), r.rs_r.at[m, 6])
            got(out_rows(m, 1 - x), r.rs_r.at[m, 10])

        @pl.when(c == y)
        def _():
            g = r.gout.at[m, z1]
            pltpu.make_async_copy(g, out_rows(m, x), r.loc.at[m, 1]).wait()
            for k in (3, 5, 6, 10):
                sent(g, r.rs_s.at[m, k])

    def rs_done(m):
        for k in range(8):
            dst = r.gs_in if m == 3 else r.ge_in.at[m]
            piece = dst.at[:, pl.ds(512 * k, 512)]
            pltpu.make_async_copy(piece, piece, r.fin.at[m, k]).wait()

    def tokens(m, j, k):
        g = 2 * j + k
        w = r.win[m].reshape(D, 512)
        wo = r.wout[m].reshape(256, D)
        gu = nn(r.nta[j, k, :, 0:D], w)
        zv = gu[:, 0:256]
        uv = gu[:, 256:512]
        sg = 1.0 / (1.0 + jnp.exp(-zv))
        sw = zv * sg
        act = (sw * uv).astype(BF).astype(F32)
        dr = nt(r.cota[j, k], wo)
        side = r.acc[j, k, :, D : D + 128]
        gv = jnp.sum(jnp.where(lane128 == m + 64, side, 0.0), axis=-1, keepdims=True)
        gg = jnp.sum(act * dr, axis=-1, keepdims=True)
        r.ga[g, :, pl.ds(pl.multiple_of(m * 256, 256), 256)] = (act * gv).astype(BF)
        d = dr * gv
        dg = jnp.concatenate([d * uv * (sg * (1.0 + zv * (1.0 - sg))), d * sw], axis=1).astype(BF)
        r.dg[g] = dg
        r.acc[j, k, :, 0:D] += nt(dg, w)
        r.acc[j, k, :, D : D + 128] = side + jnp.where(lane128 == m, gg, 0.0)

    def weight_grads(m):
        nta = r.nta[:, :, :, 0:D].reshape(2048, D)
        r.win[m] = tn(nta, r.dg[...].reshape(2048, 512)).astype(BF).reshape(4, 2, 96, 512)
        gam = r.ga[:, :, pl.ds(pl.multiple_of(m * 256, 256), 256)].reshape(2048, 256)
        r.gout[m] = tn(gam, r.cota[...].reshape(2048, D)).astype(BF).reshape(2, 128, D)
        rs_first(m)

    def pack(j, k):
        r.ngb[j, k, :, 0:D] = r.acc[j, k, :, 0:D].astype(BF)
        v = jnp.where(lane128 < 64, r.acc[j, k, :, D : D + 128], 0.0)
        hi = v.astype(BF).astype(F32)
        r.ngb[j, k, :, D : D + 128] = (hi + pltpu.roll(v - hi, 64, 1)).astype(BF)

    w_fin(0)
    for m in range(4):
        sent(r.dg.at[m, pl.ds(0, 96)], r.w_s.at[m, 0])

        @pl.when(inner)
        def _(m=m):
            sent(r.dg.at[m, pl.ds(0, 96)], r.w_s.at[m, 7])


    def arrive(p, carry):
        q = lax.div(p, 2)
        k2 = lax.rem(p, 2)
        j = block_at(q)
        k = c + k2 * (1 - 2 * c)

        @pl.when(p == 2)
        def _():
            tok_near(two_slot, 1)
            w_own(2)
            w_relay(2)
            w_own(3)
            w_relay(3)

        @pl.when(k2 == 1)
        def _():
            got(two_slot(j, k), r.tok_r.at[1, p])

        @pl.when(p == 5)
        def _():
            tok_far(two_slot, 1)

        route(j, k)
        tokens(0, j, k)
        return carry

    lax.fori_loop(0, 8, arrive, 0)
    w_relay_far(2)
    weight_grads(0)
    tok_sent(two_slot, 1)
    tok_sent(sel_slot, 2)
    tok_sent(cot_slot, 0)

    def feed(m, carry):
        w_fin(m)

        def each(p, inner):
            k2 = lax.div(p, 4)
            k = oc + k2 * (2 * c - 1)
            j = block_at(3 - lax.rem(p, 4))
            tokens(m, j, k)

            @pl.when((m == 1) & (p == FAR3))
            def _():
                w_relay_far(3)

            @pl.when((m == 2) & (p == RSY0))
            def _():
                rs_y(0)

            @pl.when(m == 3)
            def _():
                pack(j, k)

            @pl.when((m == 3) & (p == 3))
            def _():
                sum_first(r.ngb, r.ng_c, 0)

            return inner

        lax.fori_loop(0, 8, each, 0)

        @pl.when(m == 3)
        def _():
            sum_core(r.ngb, r.ng_c, r.ng_p, 0)

        weight_grads(m)
        return carry

    lax.fori_loop(1, 4, feed, 0)

    def mix(g, carry):
        j = lax.div(g, 2)
        k = lax.rem(g, 2)
        r.cota[j, k] = nn(r.ga[g], r.wout[...].reshape(1024, D)).astype(BF)
        return carry

    lax.fori_loop(0, 4, mix, 0)
    sum_relay(r.ngb, r.ng_p, 0)
    rs_y(1)
    rs_z(0)
    lax.fori_loop(4, 8, mix, 0)
    rs_y(2)
    out_c = r.ng_c.at[:, :, pl.ds(0, D)]
    out_p = r.ng_p.at[:, :, pl.ds(0, D)]
    ngs = sum_fin(r.ngb, r.ng_c, r.ng_p, 0)
    rs_z(1)

    small_dev = (core, xp, yp, z1p, z0p)

    def small_send(k):
        r.small_o[k] = r.small[...]
        send(r.small_o.at[k], r.small_i.at[k], r.sm_s.at[k], r.sm_r.at[k], small_dev[k])

    def small_add(k):
        got(r.small_i.at[k], r.sm_r.at[k])
        r.small[...] += r.small_i[k]
        sent(r.small_o.at[k], r.sm_s.at[k])
        if k < 4:
            small_send(k + 1)

    upstream = r.cot_in[...].astype(F32)
    mid = r.mid[...]
    r2 = lax.rsqrt(jnp.mean(mid * mid, axis=-1, keepdims=True) + EPSILON)
    gg = ngs[:, D : D + 128]
    gg = gg + pltpu.roll(gg, 64, 1)
    nown = r.nta[jme, c, :, 0:D]
    pv = gates(nown)
    pg = jnp.where(lane128 < 3, gg * r.sel_in[...].astype(F32), 0.0)
    lg = (pv * (pg - jnp.sum(pv * pg, axis=-1, keepdims=True))).astype(BF)
    rgrad = tn(lg, nown)
    ng = ngs[:, 0:D] + nn(lg, r.rpad[...])
    gain2 = r.mrow[4:5, :]
    fgain = jnp.sum(ng * mid * r2, axis=0, keepdims=True)
    sc = ng * gain2
    mg = upstream + r2 * sc - mid * (r2 * r2 * r2) * jnp.mean(sc * mid, axis=-1, keepdims=True)
    r.igrad[...] = mg
    r.small[...] = jnp.where(row8 < 3, rgrad[0:8, :], 0.0) + jnp.where(row8 == 4, fgain, 0.0)
    ml = mg.astype(BF)
    ow = r.ow[...].reshape(D, D)
    r.att[:, :, 128:256] = jnp.zeros((4, TOK, 128), BF)
    for i in range(4):
        da = nt(ml, ow[192 * i : 192 * i + 192, :]).astype(BF)
        r.att[i, :, 0:192] = da

        @pl.when(s != i)
        def _(i=i):
            send(r.att.at[i], r.dat.at[s], r.d_s.at[i], r.d_r.at[s], (b, i))

        @pl.when(s == i)
        def _(i=i):
            r.dat[i] = r.att[i]

    small_send(0)
    for i in range(4):
        og = tn(r.arow[i][:, 0:192], ml).astype(BF)
        og = og.reshape(2, 2, 48, D)
        for k in range(2):
            r.og[k, i] = og[:, :, :, 384 * k : 384 * k + 384]
    send(r.og.at[oc], r.og_c, r.og_s.at[0], r.og_r.at[0], core)
    for i in range(4):
        r.acc[i, 0, :, 0:QKV_PAD] = jnp.zeros((TOK, QKV_PAD), F32)
        r.acc[i, 1, :, 0:D] = jnp.zeros((TOK, D), F32)
    small_add(0)
    rs_y(3)
    for i in range(4):

        @pl.when(s != i)
        def _(i=i):
            got(r.dat.at[i], r.d_r.at[i])
            sent(r.att.at[i], r.d_s.at[i])

    rs_join(0)
    sum_first(r.cota, out_c, 1)

    chunks = ((0, 128), (128, 256), (384, 256))

    def q_first(n):
        at = pl.ds(chunks[n][0], chunks[n][1])
        send(r.wq.at[:, oy, :, at], r.q_y.at[:, :, at], r.q_s.at[n, 0], r.q_r.at[n, 0], yp)

    def q_add_y(n):
        a, e = chunks[n][0], chunks[n][0] + chunks[n][1]
        at = pl.ds(a, e - a)
        got(r.q_y.at[:, :, at], r.q_r.at[n, 0])
        for k in range(4):
            v = r.wq[k, y, :, a:e].astype(F32) + r.q_y[k, :, a:e].astype(F32)
            r.wq[k, y, :, a:e] = v.astype(BF)
        send(
            r.wq.at[pl.ds(2 - 2 * z1, 2), y, :, at],
            r.q_z.at[:, :, at],
            r.q_s.at[n, 1],
            r.q_r.at[n, 1],
            z1p,
        )

    def q_add_z(n):
        a, e = chunks[n][0], chunks[n][0] + chunks[n][1]
        at = pl.ds(a, e - a)
        got(r.q_z.at[:, :, at], r.q_r.at[n, 1])
        for k in range(2):
            v = r.wq[2 * z1 + k, y, :, a:e].astype(F32) + r.q_z[k, :, a:e].astype(F32)
            r.wq[2 * z1 + k, y, :, a:e] = v.astype(BF)
        send(r.wq.at[zf, y, :, at], r.q_w.at[:, at], r.q_s.at[n, 2], r.q_r.at[n, 2], z0p)

    def head_ends(a, w):
        at = pl.ds(a, w)
        for i in range(4):
            for k in range(0, w, 128):
                g = r.acc[i, 0, :, a + k : a + k + 128].astype(BF)
                if a + k in (0, 128, 384):
                    g = g.astype(F32)
                    cosv = r.cos_in[i * TOK : i * TOK + TOK, :]
                    sinv = r.sin_in[i * TOK : i * TOK + TOK, :]
                    g = (g * cosv - swap_halves(g) * sinv).astype(BF)
                r.nta[i, 0, :, a + k : a + k + 128] = g
        wc = r.wq[:, :, :, a : a + w].reshape(D, w)
        for i in range(4):
            r.acc[i, 1, :, 0:D] += nt(r.nta[i, 0, :, a : a + w], wc)
        pg = r.nta[:, 0, :, a : a + w].reshape(1024, w)
        wg = tn(r.nall[...].reshape(1024, D), pg)
        r.wq[:, :, :, a : a + w] = wg.astype(BF).reshape(4, 2, 96, w)

    def og_core():
        got(r.og_c, r.og_r.at[0])
        for k in range(4):
            r.og[c, k] = (r.og[c, k].astype(F32) + r.og_c[k].astype(F32)).astype(BF)
        send(r.og.at[c, :, :, 1 - x], r.og_x, r.og_s.at[1], r.og_r.at[1], xp)

    def og_xp():
        got(r.og_x, r.og_r.at[1])
        for k in range(4):
            r.og[c, k, :, x] = (r.og[c, k, :, x].astype(F32) + r.og_x[k].astype(F32)).astype(BF)
        send(r.og.at[c, :, oy, x], r.og_y, r.og_s.at[2], r.og_r.at[2], yp)

    def og_yp():
        got(r.og_y, r.og_r.at[2])
        for k in range(4):
            r.og[c, k, y, x] = (r.og[c, k, y, x].astype(F32) + r.og_y[k].astype(F32)).astype(BF)
        send(r.og.at[c, pl.ds(2 - 2 * z1, 2), y, x], r.og_z, r.og_s.at[3], r.og_r.at[3], z1p)

    def og_z1p():
        got(r.og_z, r.og_r.at[3])
        for k in range(2):
            v = r.og[c, 2 * z1 + k, y, x].astype(F32) + r.og_z[k].astype(F32)
            r.og[c, 2 * z1 + k, y, x] = v.astype(BF)
        send(r.og.at[c, zf, y, x], r.og_w, r.og_s.at[4], r.og_r.at[4], z0p)

    def og_z0p():
        got(r.og_w, r.og_r.at[4])
        r.og[c, z, y, x] = (r.og[c, z, y, x].astype(F32) + r.og_w[...].astype(F32)).astype(BF)
        ogf = r.og.at[c, z, y, x]
        r.g_ow[s] = r.og[c, z, y, x]
        send(ogf, r.g_ow.at[s], r.og_s.at[6], r.og_r.at[6], xp)
        send(ogf, r.g_ow.at[s], r.og_s.at[5], r.og_r.at[5], core)

    def heads_back(h, carry):
        hv = lax.div(h, 2)
        here = lax.div(lane128, 64) == lax.rem(h, 2)
        vat = pl.ds(pl.multiple_of(hv * 128, 128), 128)
        cat = pl.ds(pl.multiple_of(256 + hv * 256, 128), 128)
        hat = pl.ds(pl.multiple_of(h * 128 + hv * 128, 128), 128)
        for i in range(3, -1, -1):
            base = i * (i + 1) // 2
            da = jnp.where(here, r.dat[i, :, vat].astype(F32), 0.0).astype(BF)
            kqi = r.kq[h, i * TOK : i * TOK + TOK, :].astype(F32)
            qi = jnp.where(lane128 >= 64, kqi, 0.0).astype(BF)
            pf = [r.prob[h, base + j] for j in range(i + 1)]
            dp = [nt(da, r.val[hv, j * TOK : j * TOK + TOK, :]) for j in range(i + 1)]
            cen = jnp.zeros((TOK, 1), F32)
            for j in range(i + 1):
                cen = cen + jnp.sum(pf[j].astype(F32) * dp[j], axis=-1, keepdims=True)
            dq = jnp.zeros((TOK, 128), F32)
            for j in range(i + 1):
                ds = (pf[j].astype(F32) * (dp[j] - cen)).astype(BF)
                dq = dq + nn(ds, r.kq[h, j * TOK : j * TOK + TOK, :])
                r.acc[j, 0, :, hat] += tn(ds, qi)
                r.acc[j, 0, :, cat] += tn(pf[j], da)
            r.acc[i, 0, :, hat] += jnp.where(lane128 < 64, dq * 0.125, 0.0)

        @pl.when(h == 0)
        def _():
            head_ends(*chunks[0])
            q_first(0)
            og_core()
            rs_join(1)
            sum_core(r.cota, out_c, out_p, 1)
            rs_z(2)
            small_add(1)

        @pl.when(h == 1)
        def _():
            head_ends(*chunks[1])
            q_first(1)
            og_xp()
            sum_relay(r.cota, out_p, 1)
            q_add_y(0)
            rs_join(2)
            rs_spread(0)
            rs_spread(1)
            small_add(2)

        @pl.when(h == 2)
        def _():
            head_ends(*chunks[2])
            q_first(2)

        return carry

    lax.fori_loop(0, 3, heads_back, 0)

    n_slot = lambda i: r.nta.at[i, 1, :, pl.ds(0, D)]
    for i in range(4):
        r.nta[i, 1, :, 0:D] = r.acc[i, 1, :, 0:D].astype(BF)
    for k in range(2):
        send(n_slot(2 * k + oc), r.n_c.at[k], r.n_s.at[k], r.n_r.at[k], core)
    og_yp()
    q_add_y(1)
    for k in range(2):
        got(r.n_c.at[k], r.n_r.at[k])
        v = r.nta[2 * k + c, 1, :, 0:D].astype(F32) + r.n_c[k].astype(F32)
        r.nta[2 * k + c, 1, :, 0:D] = v.astype(BF)
    send(n_slot(2 - 2 * x + c), r.n_x, r.n_s.at[2], r.n_r.at[2], xp)
    q_add_z(0)
    rs_z(3)
    rs_end(0)
    small_add(3)
    q_add_y(2)
    og_z1p()
    q_add_z(1)
    rs_join(3)
    rs_spread(2)
    tot = sum_fin(r.cota, out_c, out_p, 1)
    r.out[...] = (r.mid[...] + tot).astype(BF)
    rs_end(1)
    small_add(4)
    r.g_small[...] = r.small[...]
    og_z0p()

    got(r.n_x, r.n_r.at[2])
    for k in range(3):
        sent(r.n_x, r.n_s.at[k])
    ng = r.nta[s, 1, :, 0:D].astype(F32) + r.n_x[...].astype(F32)
    xv = r.x_in[...].astype(F32)
    r1 = lax.rsqrt(jnp.mean(xv * xv, axis=-1, keepdims=True) + EPSILON)
    sc = ng * r.mrow[3:4, :]
    r.igrad[...] = (
        r.igrad[...] + r1 * sc - xv * (r1 * r1 * r1) * jnp.mean(sc * xv, axis=-1, keepdims=True)
    )
    q_add_z(2)
    rs_spread(3)
    rs_end(2)
    got(r.g_ow.at[xf], r.og_r.at[6])
    send(r.g_ow.at[xf], r.g_ow.at[xf], r.og_s.at[7], r.og_r.at[7], core)

    for n in range(3):
        got(r.q_w.at[:, pl.ds(*chunks[n])], r.q_r.at[n, 2])
    qf = r.wq[z, y].astype(F32) + r.q_w[...].astype(F32)
    qf = jnp.concatenate([qf, jnp.zeros((32, QKV_PAD), F32)], axis=0)
    qt = jnp.transpose(qf).astype(BF)
    for k, at in enumerate((0, 64, 256, 128, 192, 320, 384, 448, 512)):
        r.g_q[s, 64 * k : 64 * k + 64, :] = qt[at : at + 64, :]
    g = r.g_q.at[s]
    send(g, g, r.qg_s.at[0], r.qg_r.at[0], xp)
    send(g, g, r.qg_s.at[1], r.qg_r.at[1], core)
    rs_end(3)
    got(r.g_q.at[xf], r.qg_r.at[0])
    send(r.g_q.at[xf], r.g_q.at[xf], r.qg_s.at[2], r.qg_r.at[2], core)
    got(r.g_ow.at[s + 1 - 2 * c], r.og_r.at[5])
    got(r.g_ow.at[3 - s], r.og_r.at[7])
    for n in range(3):
        at = pl.ds(*chunks[n])
        sent(r.q_y.at[:, :, at], r.q_s.at[n, 0])
        sent(r.q_z.at[:, :, at], r.q_s.at[n, 1])
        sent(r.q_w.at[:, at], r.q_s.at[n, 2])
    sent(r.og_c, r.og_s.at[0])
    sent(r.og_x, r.og_s.at[1])
    sent(r.og_y, r.og_s.at[2])
    sent(r.og_z, r.og_s.at[3])
    sent(r.og_w, r.og_s.at[4])
    for k in (5, 6, 7):
        sent(r.g_ow.at[0], r.og_s.at[k])
    for m in range(4):
        rs_done(m)
    got(r.g_q.at[s + 1 - 2 * c], r.qg_r.at[1])
    got(r.g_q.at[3 - s], r.qg_r.at[2])
    for k in range(3):
        sent(g, r.qg_s.at[k])


def vmem(shape, kind=BF):
    return pltpu.VMEM(shape, kind)


def layer_call(ins, cos_table, sin_table):
    dma = pltpu.SemaphoreType.DMA
    in_names = (
        ["x_in", "cot_in", "wq_in", "misc_in", "ow_in", "sel_in", "cos_in", "sin_in"]
        + ["e_in", "e_out", "s_in", "s_out"]
    )
    out_names = ["out", "igrad", "g_small", "g_q", "g_ow"]
    out_names += ["ge_in", "gs_in", "ge_out", "gs_out"]
    out_shapes = (
        ((TOK, D), BF),
        ((TOK, D), F32),
        ((8, D), F32),
        ((4, 576, 128), BF),
        ((4, 48, 384), BF),
        ((3, 96, 4096), BF),
        ((96, 4096), BF),
        ((3, 256, D), BF),
        ((256, D), BF),
    )
    scratch = {
        "nall": vmem((4, TOK, D)),
        "wq": vmem((4, 2, 96, QKV_PAD)),
        "misc": vmem((4, 2, 8, 128), F32),
        "ow": vmem((4, 2, 2, 48, D)),
        "kq": vmem((3, 1024, 128)),
        "val": vmem((2, 1024, 128)),
        "prob": vmem((3, 10, TOK, TOK)),
        "att": vmem((4, TOK, 256)),
        "arow": vmem((4, TOK, 256)),
        "dat": vmem((4, TOK, 256)),
        "mid": vmem((TOK, D), F32),
        "mrow": vmem((8, D), F32),
        "rpad": vmem((128, D)),
        "nta": vmem((4, 2, TOK, D + 128)),
        "cota": vmem((4, 2, TOK, D)),
        "win": vmem((4, 4, 2, 96, 512)),
        "wout": vmem((4, 2, 128, D)),
        "dg": vmem((8, TOK, 512)),
        "ga": vmem((8, TOK, 1024)),
        "acc": vmem((4, 2, TOK, D + 128), F32),
        "gout": vmem((4, 2, 128, D)),
        "ry_in": vmem((4, 4, 96, 512)),
        "ry_out": vmem((4, 2, 128, D)),
        "rzz": vmem((4, 96, 512)),
        "rz_in": vmem((4, 2, 96, 512)),
        "rz_out": vmem((4, 128, D)),
        "ng_c": vmem((4, TOK, D + 128)),
        "ng_p": vmem((3, TOK, D + 128)),
        "ngb": vmem((4, 2, TOK, D + 128)),
        "n_c": vmem((2, TOK, D)),
        "n_x": vmem((TOK, D)),
        "og": vmem((2, 4, 2, 2, 48, 384)),
        "og_c": vmem((4, 2, 2, 48, 384)),
        "og_x": vmem((4, 2, 48, 384)),
        "og_y": vmem((4, 48, 384)),
        "og_z": vmem((2, 48, 384)),
        "og_w": vmem((48, 384)),
        "q_y": vmem((4, 96, QKV_PAD)),
        "q_z": vmem((2, 96, QKV_PAD)),
        "q_w": vmem((96, QKV_PAD)),
        "small": vmem((8, D), F32),
        "small_o": vmem((5, 8, D), F32),
        "small_i": vmem((5, 8, D), F32),
        "stage_sem": dma((4, 9)),
        "att_s": dma((3, 8)),
        "att_r": dma((3, 8)),
        "w_s": dma((4, 8)),
        "w_r": dma((4, 8)),
        "o_s": dma((4, 3)),
        "o_r": dma((4, 2)),
        "ow_s": dma((1,)),
        "ow_r": dma((1,)),
        "x_s": dma((3,)),
        "x_r": dma((3,)),
        "tok_s": dma((3, 7)),
        "tok_r": dma((3, 8)),
        "a_s": dma((4,)),
        "a_r": dma((4,)),
        "d_s": dma((4,)),
        "d_r": dma((4,)),
        "sum_s": dma((2, 4)),
        "sum_r": dma((2, 4)),
        "rs_s": dma((4, 11)),
        "rs_r": dma((4, 11)),
        "loc": dma((4, 2)),
        "og_s": dma((8,)),
        "og_r": dma((8,)),
        "q_s": dma((3, 3)),
        "q_r": dma((3, 3)),
        "qg_s": dma((3,)),
        "qg_r": dma((3,)),
        "fin": dma((4, 8)),
        "n_s": dma((3,)),
        "n_r": dma((3,)),
        "sm_s": dma((5,)),
        "sm_r": dma((5,)),
    }
    names = in_names + out_names + list(scratch)
    in_vmem = pl.BlockSpec(memory_space=pltpu.VMEM)
    in_any = pl.BlockSpec(memory_space=pl.ANY)
    return pl.pallas_call(
        functools.partial(layer_kernel, names),
        out_shape=[jax.ShapeDtypeStruct(*one) for one in out_shapes],
        in_specs=[in_vmem] * 8 + [in_any] * 4,
        out_specs=[in_vmem] * 5 + [in_any] * 4,
        scratch_shapes=list(scratch.values()),
        compiler_params=pltpu.CompilerParams(
            collective_id=0, has_side_effects=True, vmem_limit_bytes=VMEM_LIMIT
        ),
        cost_estimate=pl.CostEstimate(
            flops=35_000_000_000, bytes_accessed=60_000_000, transcendentals=6_000_000
        ),
        name="layer",
    )(*ins[:6], cos_table, sin_table, *ins[6:])


def fast_device(
    inputs,
    attn_gain,
    qkv_weight,
    out_weight,
    ffn_gain,
    router_weight,
    expert_in,
    expert_out,
    shared_in,
    shared_out,
    routes,
    slot_index,
    cotangent,
):
    b = lax.axis_index("dp")
    s = lax.axis_index("seq")
    c = s % 2
    mine = lax.dynamic_slice_in_dim(qkv_weight, 3 * s, 3, axis=1).astype(BF)
    pairs = mine[:, :, 0:2].reshape(96, 3, 128)
    values = mine[:, :, 2].reshape(96, 192)
    wq = jnp.concatenate(
        [
            pairs[:, 0],
            pairs[:, 1],
            values[:, 0:128],
            pairs[:, 2],
            values[:, 128:192],
            jnp.zeros((96, 64), BF),
        ],
        axis=1,
    )
    misc = jnp.concatenate(
        [router_weight.T, attn_gain[None], ffn_gain[None], jnp.zeros((3, 96), F32)], axis=0
    )
    misc = jnp.pad(misc.astype(BF).astype(F32), ((0, 0), (0, 32)))
    half = lax.dynamic_slice_in_dim(out_weight, 48 * c, 48, axis=0).astype(BF)
    lane = jnp.arange(128, dtype=jnp.int32)
    route = routes[0]
    sel = (lane == route[:, 0:1]) | (lane == route[:, 1:2]) | (lane == 3)
    sel = sel.astype(BF)
    angle = np.arange(1024, dtype=np.float32)[:, None] * (
        np.float32(10000.0) ** (-np.arange(32, dtype=np.float32) / np.float32(32))
    )
    cos_table = jnp.asarray(np.tile(np.cos(angle), (1, 4)).astype(np.float32))
    sine = np.sin(angle)
    sin_table = jnp.asarray(np.tile(np.concatenate([-sine, sine], 1), (1, 2)).astype(np.float32))
    out, igrad, small, g_q, g_ow, ge_in, gs_in, ge_out, gs_out = layer_call(
        (
            inputs[0],
            cotangent[0],
            wq,
            misc,
            half,
            sel,
            expert_in,
            expert_out,
            shared_in,
            shared_out,
        ),
        cos_table,
        sin_table,
    )
    shard = lax.dynamic_slice_in_dim(small, 96 * b, 96, axis=1)
    qkv_grad = g_q.reshape(HEADS, 3, HEAD_DIM, 128)[..., 0:96].transpose(3, 0, 1, 2).astype(F32)
    gain_grad = jnp.sum(qkv_weight.astype(BF).astype(F32) * qkv_grad, axis=(1, 2, 3))
    gain_grad = gain_grad / attn_gain.astype(BF).astype(F32)
    ow_grad = g_ow.reshape(2, 2, 48, 384).transpose(0, 2, 1, 3).reshape(96, D).astype(F32)
    return (
        out[None],
        igrad[None],
        gain_grad,
        qkv_grad,
        ow_grad,
        shard[4],
        shard[0:3].T,
        ge_in.astype(F32),
        ge_out.astype(F32),
        gs_in.astype(F32),
        gs_out.astype(F32),
    )


def solution(mesh):
    fits = mesh.shape["dp"] == 8 and mesh.shape["seq"] == 4
    return jax.shard_map(
        fast_device if fits else on_device,
        mesh=mesh,
        in_specs=(
            P("dp", "seq", None),
            P("dp"),
            P("dp", None, None, None),
            P("dp", None),
            P("dp"),
            P("dp", None),
            P(None, "dp", None),
            P(None, "dp", None),
            P("dp", None),
            P("dp", None),
            P("dp", "seq", None),
            P("dp", "seq", None),
            P("dp", "seq", None),
        ),
        out_specs=(
            P("dp", "seq", None),
            P("dp", "seq", None),
            P("dp"),
            P("dp", None, None, None),
            P("dp", None),
            P("dp"),
            P("dp", None),
            P(None, "dp", None),
            P(None, "dp", None),
            P("dp", None),
            P("dp", None),
        ),
        check_vma=False,
    )
```

```python
import functools
import types

import jax
import jax.numpy as jnp
import numpy as np
from jax import lax
from jax.experimental import pallas as pl
from jax.experimental.pallas import tpu as pltpu
from jax.sharding import PartitionSpec as P

D = 768
HEADS = 12
HEAD_DIM = 64
FF = 2048
EXPERTS = 3
TOP = 2
ATT_BLOCK = 256
CAP = 192


EPSILON = 1e-05
VMEM_LIMIT = 66_000_000


def rotary_tables(positions):
    half_dim = HEAD_DIM // 2
    frequency = 10000.0 ** (-jnp.arange(half_dim, dtype=jnp.float32) / half_dim)
    angles = positions.astype(jnp.float32)[:, None] * frequency[None, :]
    return (jnp.cos(angles), jnp.sin(angles))


def rotate(values, cos_table, sine_table):
    half_dim = values.shape[-1] // 2
    first_half = values[..., :half_dim]
    second_half = values[..., half_dim:]
    cos_heads = cos_table[:, None, :]
    sine_heads = sine_table[:, None, :]
    return jnp.concatenate(
        [
            first_half * cos_heads - second_half * sine_heads,
            second_half * cos_heads + first_half * sine_heads,
        ],
        axis=-1,
    )


def unrotate(values, cos_table, sine_table):
    half_dim = values.shape[-1] // 2
    first_half = values[..., :half_dim]
    second_half = values[..., half_dim:]
    cos_heads = cos_table[:, None, :]
    sine_heads = sine_table[:, None, :]
    return jnp.concatenate(
        [
            first_half * cos_heads + second_half * sine_heads,
            second_half * cos_heads - first_half * sine_heads,
        ],
        axis=-1,
    )


def silu_grads(gate_in, up_in, upstream):
    sigmoid = jax.nn.sigmoid(gate_in)
    swish = gate_in * sigmoid
    slope = sigmoid * (1.0 + gate_in * (1.0 - sigmoid))
    return jnp.concatenate([upstream * up_in * slope, upstream * swish], axis=-1)


def block_mask(row_start, block_rows, length):
    query_block = (row_start + jnp.arange(block_rows, dtype=jnp.int32)) // ATT_BLOCK
    key_block = jnp.arange(length, dtype=jnp.int32) // ATT_BLOCK
    return key_block[None, :] <= query_block[:, None]


def attend_heads(received):
    packed = received[:, 0]
    length = packed.shape[0]
    heads_here = packed.shape[1]
    queries = packed[..., :HEAD_DIM]
    keys_all = packed[..., HEAD_DIM : 2 * HEAD_DIM]
    values_all = packed[..., 2 * HEAD_DIM :]
    block_rows = min(512, length)
    block_count = length // block_rows
    score_scale = HEAD_DIM ** (-0.5)

    def one_block(element):
        query_rows, row_start = element
        scores = (
            jnp.einsum("qhe,khe->hqk", query_rows, keys_all, preferred_element_type=jnp.float32)
            * score_scale
        )
        scores = jnp.where(block_mask(row_start, block_rows, length)[None], scores, -1e30)
        largest = jnp.max(scores, axis=-1, keepdims=True)
        weights_exp = jnp.exp(scores - largest)
        totals = jnp.sum(weights_exp, axis=-1, keepdims=True)
        attn_probs = (weights_exp / totals).astype(jnp.bfloat16)
        mixed_rows = jnp.einsum(
            "hqk,khe->qhe", attn_probs, values_all, preferred_element_type=jnp.float32
        )
        log_total = (largest + jnp.log(totals))[..., 0]
        return (mixed_rows.astype(jnp.bfloat16), jnp.transpose(log_total))

    blocked = queries.reshape(block_count, block_rows, heads_here, HEAD_DIM)
    starts = jnp.arange(block_count, dtype=jnp.int32) * block_rows
    mixed_rows, log_total = lax.map(one_block, (blocked, starts))
    return (
        mixed_rows.reshape(length, 1, heads_here, HEAD_DIM),
        log_total.reshape(length, 1, heads_here),
        received,
    )


def attend_back(received, log_sum, grad_in):
    packed = received[:, 0]
    length = packed.shape[0]
    heads_here = packed.shape[1]
    queries = packed[..., :HEAD_DIM]
    keys_all = packed[..., HEAD_DIM : 2 * HEAD_DIM]
    values_all = packed[..., 2 * HEAD_DIM :]
    block_rows = min(512, length)
    block_count = length // block_rows
    score_scale = HEAD_DIM ** (-0.5)

    def one_block(running, element):
        key_acc, value_acc = running
        query_rows, grad_rows, log_rows, row_start = element
        scores = (
            jnp.einsum("qhe,khe->hqk", query_rows, keys_all, preferred_element_type=jnp.float32)
            * score_scale
        )
        scores = jnp.where(block_mask(row_start, block_rows, length)[None], scores, -1e30)
        attn_probs = jnp.exp(scores - jnp.transpose(log_rows)[:, :, None])
        value_acc = value_acc + jnp.einsum(
            "hqk,qhe->khe",
            attn_probs.astype(jnp.bfloat16),
            grad_rows,
            preferred_element_type=jnp.float32,
        )
        grad_probs = jnp.einsum(
            "qhe,khe->hqk", grad_rows, values_all, preferred_element_type=jnp.float32
        )
        centre = jnp.sum(attn_probs * grad_probs, axis=-1, keepdims=True)
        grad_scores = (attn_probs * (grad_probs - centre)).astype(jnp.bfloat16)
        query_grad = (
            jnp.einsum("hqk,khe->qhe", grad_scores, keys_all, preferred_element_type=jnp.float32)
            * score_scale
        )
        key_acc = key_acc + jnp.einsum(
            "hqk,qhe->khe", grad_scores, query_rows, preferred_element_type=jnp.float32
        )
        return ((key_acc, value_acc), query_grad)

    empty_acc = jnp.zeros((length, heads_here, HEAD_DIM), jnp.float32)
    blocked_query = queries.reshape(block_count, block_rows, heads_here, HEAD_DIM)
    blocked_grad = grad_in[:, 0].reshape(block_count, block_rows, heads_here, HEAD_DIM)
    blocked_log = log_sum[:, 0].reshape(block_count, block_rows, heads_here)
    starts = jnp.arange(block_count, dtype=jnp.int32) * block_rows
    (key_acc, value_acc), query_grads = lax.scan(
        one_block, (empty_acc, empty_acc), (blocked_query, blocked_grad, blocked_log, starts)
    )
    stacked = jnp.stack(
        [query_grads.reshape(length, heads_here, HEAD_DIM), key_acc * score_scale, value_acc],
        axis=2,
    )
    return stacked.astype(jnp.bfloat16).reshape(length, 1, heads_here, 3 * HEAD_DIM)


def norm_back(values, scale_rows, gain_row, upstream):
    scaled = upstream * gain_row
    gain_term = jnp.sum(upstream * values * scale_rows, axis=0)
    value_grad = scale_rows * scaled - values * scale_rows**3 * jnp.mean(
        scaled * values, axis=-1, keepdims=True
    )
    return (gain_term, value_grad)


def on_device(
    inputs,
    attn_gain,
    qkv_weight,
    out_weight,
    ffn_gain,
    router_weight,
    expert_in,
    expert_out,
    shared_in,
    shared_out,
    routes,
    slot_index,
    cotangent,
):
    tok_rows = inputs.shape[1]
    group_count = lax.axis_size("seq")
    heads_group = HEADS // group_count
    stream = inputs[0].astype(jnp.float32)
    attn_local = (
        attn_gain.astype(jnp.bfloat16),
        qkv_weight.astype(jnp.bfloat16),
        out_weight.astype(jnp.bfloat16),
    )
    attn_full = (
        lax.all_gather(attn_local[0], "dp", axis=0, tiled=True),
        lax.all_gather(attn_local[1], "dp", axis=0, tiled=True),
        lax.all_gather(attn_local[2], "dp", axis=0, tiled=True),
    )
    gain_first, qkv_full, out_full = attn_full
    positions = lax.axis_index("seq") * tok_rows + jnp.arange(tok_rows, dtype=jnp.int32)
    cos_table, sine_table = rotary_tables(positions)
    scale_one = lax.rsqrt(jnp.mean(stream * stream, axis=-1, keepdims=True) + EPSILON)
    gain_one_f = gain_first.astype(jnp.float32)
    normed = (stream * scale_one * gain_one_f).astype(jnp.bfloat16)
    projected = jnp.einsum("td,dhce->thce", normed, qkv_full, preferred_element_type=jnp.float32)
    rotated = jnp.stack(
        [
            rotate(projected[:, :, 0], cos_table, sine_table),
            rotate(projected[:, :, 1], cos_table, sine_table),
            projected[:, :, 2],
        ],
        axis=2,
    ).astype(jnp.bfloat16)
    outgoing = rotated.reshape(tok_rows, group_count, heads_group, 3 * HEAD_DIM)
    head_out, log_sum, head_qkv = attend_heads(
        lax.all_to_all(outgoing, "seq", split_axis=1, concat_axis=0, tiled=True)
    )
    attended = lax.all_to_all(head_out, "seq", split_axis=0, concat_axis=1, tiled=True).reshape(
        tok_rows, D
    )
    middle = stream + jnp.dot(attended, out_full, preferred_element_type=jnp.float32)
    ffn_local = (
        ffn_gain.astype(jnp.bfloat16),
        router_weight.astype(jnp.bfloat16),
        expert_in.astype(jnp.bfloat16),
        expert_out.astype(jnp.bfloat16),
        shared_in.astype(jnp.bfloat16),
        shared_out.astype(jnp.bfloat16),
    )
    ffn_full = (
        lax.all_gather(ffn_local[0], "dp", axis=0, tiled=True),
        lax.all_gather(ffn_local[1], "dp", axis=0, tiled=True),
        lax.all_gather(ffn_local[2], "dp", axis=1, tiled=True),
        lax.all_gather(ffn_local[3], "dp", axis=1, tiled=True),
        lax.all_gather(ffn_local[4], "dp", axis=0, tiled=True),
        lax.all_gather(ffn_local[5], "dp", axis=0, tiled=True),
    )
    gain_second, router_full, exp_in_full, exp_out_full, sh_in_full, sh_out_full = ffn_full
    scale_two = lax.rsqrt(jnp.mean(middle * middle, axis=-1, keepdims=True) + EPSILON)
    gain_two_f = gain_second.astype(jnp.float32)
    normed_two = (middle * scale_two * gain_two_f).astype(jnp.bfloat16)
    logits = jnp.dot(normed_two, router_full, preferred_element_type=jnp.float32)
    router_probs = jax.nn.softmax(logits, axis=-1)
    route_rows = routes[0]
    choice_hot = (
        route_rows[:, :, None] == jnp.arange(EXPERTS, dtype=jnp.int32)[None, None, :]
    ).astype(jnp.float32)
    gate_values = jnp.sum(choice_hot * router_probs[:, None, :], axis=-1)
    flat_slot = (route_rows * CAP + slot_index[0]).reshape(-1)
    buffer = (
        jnp.zeros((EXPERTS * CAP, D), jnp.bfloat16)
        .at[flat_slot]
        .set(jnp.repeat(normed_two, TOP, axis=0))
        .reshape(EXPERTS, CAP, D)
    )
    gate_up = jnp.einsum("ecd,edf->ecf", buffer, exp_in_full, preferred_element_type=jnp.float32)
    activated = (jax.nn.silu(gate_up[..., :FF]) * gate_up[..., FF:]).astype(jnp.bfloat16)
    expert_rows = jnp.einsum(
        "ecf,efd->ecd", activated, exp_out_full, preferred_element_type=jnp.float32
    ).reshape(EXPERTS * CAP, D)
    picked = expert_rows[flat_slot].reshape(tok_rows, TOP, D)
    mixture = jnp.sum(gate_values[:, :, None] * picked, axis=1)
    shared_gu = jnp.dot(normed_two, sh_in_full, preferred_element_type=jnp.float32)
    shared_act = (jax.nn.silu(shared_gu[:, :FF]) * shared_gu[:, FF:]).astype(jnp.bfloat16)
    result = middle + mixture + jnp.dot(shared_act, sh_out_full, preferred_element_type=jnp.float32)
    output = result.astype(jnp.bfloat16)[None]
    ffn_back = (
        lax.all_gather(ffn_local[0], "dp", axis=0, tiled=True),
        lax.all_gather(ffn_local[1], "dp", axis=0, tiled=True),
        lax.all_gather(ffn_local[2], "dp", axis=1, tiled=True),
        lax.all_gather(ffn_local[3], "dp", axis=1, tiled=True),
        lax.all_gather(ffn_local[4], "dp", axis=0, tiled=True),
        lax.all_gather(ffn_local[5], "dp", axis=0, tiled=True),
    )
    router_back, exp_in_back, exp_out_back, sh_in_back, sh_out_back = (
        ffn_back[1],
        ffn_back[2],
        ffn_back[3],
        ffn_back[4],
        ffn_back[5],
    )
    upstream = cotangent[0].astype(jnp.float32)
    grad_low = upstream.astype(jnp.bfloat16)
    shared_out_grad = jnp.einsum(
        "tf,td->fd", shared_act, grad_low, preferred_element_type=jnp.float32
    )
    shared_act_grad = jnp.einsum(
        "td,fd->tf", grad_low, sh_out_back, preferred_element_type=jnp.float32
    )
    shared_gu_grad = silu_grads(shared_gu[:, :FF], shared_gu[:, FF:], shared_act_grad).astype(
        jnp.bfloat16
    )
    shared_in_grad = jnp.einsum(
        "td,tf->df", normed_two, shared_gu_grad, preferred_element_type=jnp.float32
    )
    norm_grad_two = jnp.einsum(
        "tf,df->td", shared_gu_grad, sh_in_back, preferred_element_type=jnp.float32
    )
    slot_terms = (gate_values[:, :, None] * upstream[:, None, :]).reshape(tok_rows * TOP, D)
    slot_grad = (
        jnp.zeros((EXPERTS * CAP, D), jnp.float32)
        .at[flat_slot]
        .set(slot_terms)
        .astype(jnp.bfloat16)
        .reshape(EXPERTS, CAP, D)
    )
    expert_out_grad = jnp.einsum(
        "ecf,ecd->efd", activated, slot_grad, preferred_element_type=jnp.float32
    )
    activated_grad = jnp.einsum(
        "ecd,efd->ecf", slot_grad, exp_out_back, preferred_element_type=jnp.float32
    )
    gate_up_grad = silu_grads(gate_up[..., :FF], gate_up[..., FF:], activated_grad).astype(
        jnp.bfloat16
    )
    expert_in_grad = jnp.einsum(
        "ecd,ecf->edf", buffer, gate_up_grad, preferred_element_type=jnp.float32
    )
    buffer_grad = jnp.einsum(
        "ecf,edf->ecd", gate_up_grad, exp_in_back, preferred_element_type=jnp.float32
    ).reshape(EXPERTS * CAP, D)
    norm_grad_two = norm_grad_two + jnp.sum(
        buffer_grad[flat_slot].reshape(tok_rows, TOP, D), axis=1
    )
    gate_grad = jnp.sum(upstream[:, None, :] * picked, axis=-1)
    prob_grad = jnp.sum(choice_hot * gate_grad[:, :, None], axis=1)
    logit_grad = (
        router_probs * (prob_grad - jnp.sum(router_probs * prob_grad, axis=-1, keepdims=True))
    ).astype(jnp.bfloat16)
    router_weight_grad = jnp.einsum(
        "td,te->de", normed_two, logit_grad, preferred_element_type=jnp.float32
    )
    norm_grad_two = norm_grad_two + jnp.einsum(
        "te,de->td", logit_grad, router_back, preferred_element_type=jnp.float32
    )
    ffn_gain_term, middle_part = norm_back(middle, scale_two, gain_two_f, norm_grad_two)
    middle_grad = upstream + middle_part
    attn_back = (
        lax.all_gather(attn_local[0], "dp", axis=0, tiled=True),
        lax.all_gather(attn_local[1], "dp", axis=0, tiled=True),
        lax.all_gather(attn_local[2], "dp", axis=0, tiled=True),
    )
    qkv_back, out_back = (attn_back[1], attn_back[2])
    middle_low = middle_grad.astype(jnp.bfloat16)
    out_weight_grad = jnp.einsum(
        "tf,td->fd", attended, middle_low, preferred_element_type=jnp.float32
    )
    attended_grad = jnp.einsum(
        "td,fd->tf", middle_low, out_back, preferred_element_type=jnp.float32
    ).astype(jnp.bfloat16)
    head_grad = lax.all_to_all(
        attended_grad.reshape(tok_rows, group_count, heads_group, HEAD_DIM),
        "seq",
        split_axis=1,
        concat_axis=0,
        tiled=True,
    )
    stacked = attend_back(head_qkv, log_sum, head_grad)
    returned = (
        lax.all_to_all(stacked, "seq", split_axis=0, concat_axis=1, tiled=True)
        .reshape(tok_rows, HEADS, 3, HEAD_DIM)
        .astype(jnp.float32)
    )
    projected_grad = jnp.stack(
        [
            unrotate(returned[:, :, 0], cos_table, sine_table),
            unrotate(returned[:, :, 1], cos_table, sine_table),
            returned[:, :, 2],
        ],
        axis=2,
    ).astype(jnp.bfloat16)
    qkv_weight_grad = jnp.einsum(
        "td,thce->dhce", normed, projected_grad, preferred_element_type=jnp.float32
    )
    norm_grad = jnp.einsum(
        "thce,dhce->td", projected_grad, qkv_back, preferred_element_type=jnp.float32
    )
    attn_gain_term, input_part = norm_back(stream, scale_one, gain_one_f, norm_grad)
    input_grad = (middle_grad + input_part)[None]
    parts = (
        lax.psum_scatter(
            qkv_weight_grad.astype(jnp.bfloat16), "seq", scatter_dimension=1, tiled=True
        ).astype(jnp.float32),
        lax.psum_scatter(
            out_weight_grad.astype(jnp.bfloat16), "seq", scatter_dimension=1, tiled=True
        ).astype(jnp.float32),
        lax.psum_scatter(
            expert_in_grad.astype(jnp.bfloat16), "seq", scatter_dimension=2, tiled=True
        ).astype(jnp.float32),
        lax.psum_scatter(
            expert_out_grad.astype(jnp.bfloat16), "seq", scatter_dimension=2, tiled=True
        ).astype(jnp.float32),
        lax.psum_scatter(
            shared_in_grad.astype(jnp.bfloat16), "seq", scatter_dimension=1, tiled=True
        ).astype(jnp.float32),
        lax.psum_scatter(
            shared_out_grad.astype(jnp.bfloat16), "seq", scatter_dimension=1, tiled=True
        ).astype(jnp.float32),
    )
    owned = (
        lax.psum_scatter(attn_gain_term, "dp", scatter_dimension=0, tiled=True),
        lax.psum_scatter(ffn_gain_term, "dp", scatter_dimension=0, tiled=True),
        lax.psum_scatter(router_weight_grad, "dp", scatter_dimension=0, tiled=True),
        lax.psum_scatter(parts[0], "dp", scatter_dimension=0, tiled=True),
        lax.psum_scatter(parts[1], "dp", scatter_dimension=0, tiled=True),
        lax.psum_scatter(parts[2], "dp", scatter_dimension=1, tiled=True),
        lax.psum_scatter(parts[3], "dp", scatter_dimension=1, tiled=True),
        lax.psum_scatter(parts[4], "dp", scatter_dimension=0, tiled=True),
        lax.psum_scatter(parts[5], "dp", scatter_dimension=0, tiled=True),
    )
    small = lax.psum((owned[0], owned[1], owned[2]), "seq")
    joined = (
        lax.all_gather(owned[3].astype(jnp.bfloat16), "seq", axis=1, tiled=True).astype(
            jnp.float32
        ),
        lax.all_gather(owned[4].astype(jnp.bfloat16), "seq", axis=1, tiled=True).astype(
            jnp.float32
        ),
        lax.all_gather(owned[5].astype(jnp.bfloat16), "seq", axis=2, tiled=True).astype(
            jnp.float32
        ),
        lax.all_gather(owned[6].astype(jnp.bfloat16), "seq", axis=2, tiled=True).astype(
            jnp.float32
        ),
        lax.all_gather(owned[7].astype(jnp.bfloat16), "seq", axis=1, tiled=True).astype(
            jnp.float32
        ),
        lax.all_gather(owned[8].astype(jnp.bfloat16), "seq", axis=1, tiled=True).astype(
            jnp.float32
        ),
    )
    return (
        output,
        input_grad,
        small[0],
        joined[0],
        joined[1],
        small[1],
        small[2],
        joined[2],
        joined[3],
        joined[4],
        joined[5],
    )


MESH = pl.DeviceIdType.MESH
BF = jnp.bfloat16
F32 = jnp.float32
TOK = ATT_BLOCK
QKV_PAD = 640
FAR3 = 5
RSY0 = 5


def nn(a, b):
    return lax.dot_general(a, b, (((1,), (0,)), ((), ())), preferred_element_type=F32)


def nt(a, b):
    return lax.dot_general(a, b, (((1,), (1,)), ((), ())), preferred_element_type=F32)


def tn(a, b):
    return lax.dot_general(a, b, (((0,), (0,)), ((), ())), preferred_element_type=F32)


def swap_halves(v):
    lane = lax.broadcasted_iota(jnp.int32, v.shape, 1)
    return jnp.where(lax.rem(lane, 64) < 32, pltpu.roll(v, 96, 1), pltpu.roll(v, 32, 1))


def layer_kernel(names, *refs):
    r = types.SimpleNamespace(**dict(zip(names, refs)))
    b = lax.axis_index("dp")
    s = lax.axis_index("seq")
    z = lax.div(b, 2)
    y = lax.rem(b, 2)
    z1 = lax.div(b, 4)
    z0 = lax.rem(z, 2)
    x = lax.div(s, 2)
    c = lax.rem(s, 2)
    zf = z + 1 - 2 * z0
    zg = z + 2 - 4 * z1
    zh = zf + 2 - 4 * z1
    core = (b, s + 1 - 2 * c)
    xp = (b, s + 2 - 4 * x)
    diag = (b, 3 - s)
    yp = (b + 1 - 2 * y, s)
    z0p = (b + 2 - 4 * z0, s)
    z1p = (b + 4 - 8 * z1, s)
    inner = lax.div(z + 1, 2) == 1
    zip_ = (b + 6 - 4 * z, s)
    p1 = (b + c * (2 - 4 * z0), s + (1 - c) * (2 - 4 * x))
    p2 = (b + (1 - c) * (2 - 4 * z0), s + c * (2 - 4 * x))
    jme = z0 * 2 + x
    jx = z0 * 2 + 1 - x
    jz = (1 - z0) * 2 + x
    jd = (1 - z0) * 2 + 1 - x
    jp1 = jx + c * (jz - jx)
    jp2 = jz + c * (jx - jz)
    oc = 1 - c
    oy = 1 - y

    def send(src, dst, ss, rs, dev):
        pltpu.make_async_remote_copy(
            src_ref=src, dst_ref=dst, send_sem=ss, recv_sem=rs, device_id=dev, device_id_type=MESH
        ).start()

    def sent(src, ss):
        pltpu.make_async_remote_copy(
            src_ref=src, dst_ref=src, send_sem=ss, recv_sem=ss, device_id=core, device_id_type=MESH
        ).wait_send()

    def got(dst, rs):
        pltpu.make_async_remote_copy(
            src_ref=dst, dst_ref=dst, send_sem=rs, recv_sem=rs, device_id=core, device_id_type=MESH
        ).wait_recv()

    def ag_first(src, slot, ss, rs):
        send(src, slot(z, y), ss(0), rs(b), z0p)

        @pl.when(inner)
        def _():
            send(src, slot(z, y), ss(7), rs(b), zip_)

    def ag_own(slot, ss, rs):
        send(slot(z, y), slot(z, y), ss(1), rs(b), z1p)
        send(slot(z, y), slot(z, y), ss(2), rs(b), yp)

    def ag_z0(slot, ss, rs):
        k = 2 * zf + y
        got(slot(zf, y), rs(k))

        @pl.when(inner)
        def _():
            send(slot(zf, y), slot(zf, y), ss(3), rs(k), z1p)

        send(slot(zf, y), slot(zf, y), ss(4), rs(k), yp)

    def ag_z1(slot, ss, rs):
        for zz, n in ((zg, 5), (zh, 6)):
            k = 2 * zz + y
            got(slot(zz, y), rs(k))
            send(slot(zz, y), slot(zz, y), ss(n), rs(k), yp)

    def ag_fin(slot, rs):
        for zz in range(4):
            got(slot(zz, oy), rs(2 * zz + oy))

    def ag_sent(src, slot, ss):
        sent(src, ss(0))
        for n in (1, 2, 4, 5, 6):
            sent(slot(z, y), ss(n))

        @pl.when(inner)
        def _():
            sent(slot(z, y), ss(3))
            sent(src, ss(7))

    def tok_own(slot, n):
        own = slot(jme, c)
        send(own, own, r.tok_s.at[n, 1], r.tok_r.at[n, 2], p1)
        send(own, own, r.tok_s.at[n, 2], r.tok_r.at[n, 4], p2)
        send(own, own, r.tok_s.at[n, 0], r.tok_r.at[n, 1], core)

    def tok_near(slot, n):
        v = slot(jp1, c)
        got(v, r.tok_r.at[n, 2])
        send(v, v, r.tok_s.at[n, 3], r.tok_r.at[n, 6], p2)
        send(v, v, r.tok_s.at[n, 4], r.tok_r.at[n, 5], core)
        v = slot(jp2, c)
        got(v, r.tok_r.at[n, 4])
        send(v, v, r.tok_s.at[n, 5], r.tok_r.at[n, 3], core)

    def tok_far(slot, n):
        v = slot(jd, c)
        got(v, r.tok_r.at[n, 6])
        send(v, v, r.tok_s.at[n, 6], r.tok_r.at[n, 7], core)

    def tok_fin(slot, n):
        got(slot(jme, oc), r.tok_r.at[n, 1])
        got(slot(jp1, oc), r.tok_r.at[n, 3])
        got(slot(jp2, oc), r.tok_r.at[n, 5])
        got(slot(jd, oc), r.tok_r.at[n, 7])

    def tok_sent(slot, n):
        for k in range(7):
            sent(slot(jme, c), r.tok_s.at[n, k])

    cot_slot = lambda j, k: r.cota.at[j, k]
    sel_slot = lambda j, k: r.nta.at[j, k, :, pl.ds(D, 128)]
    two_slot = lambda j, k: r.nta.at[j, k, :, pl.ds(0, D)]

    def block_at(q):
        q1 = lax.rem(q, 2)
        q2 = lax.div(q, 2)
        fx = q1 + c * (q2 - q1)
        fz = q2 + c * (q1 - q2)
        return 2 * (z0 + fz * (1 - 2 * z0)) + x + fx * (1 - 2 * x)

    def sum_first(buf, rc, n):
        send(buf.at[:, oc], rc, r.sum_s.at[n, 0], r.sum_r.at[n, 0], core)

    def sum_core(buf, rc, rp, n):
        got(rc, r.sum_r.at[n, 0])
        for j in range(4):
            v = buf[j, c].astype(F32) + rc[j].astype(F32)
            buf[j, c] = v.astype(BF)
        send(buf.at[jd, c], rp.at[0], r.sum_s.at[n, 1], r.sum_r.at[n, 1], p2)
        send(buf.at[jp2, c], rp.at[1], r.sum_s.at[n, 2], r.sum_r.at[n, 2], p2)

    def sum_relay(buf, rp, n):
        got(rp.at[0], r.sum_r.at[n, 1])
        buf[jp1, c] = (buf[jp1, c].astype(F32) + rp[0].astype(F32)).astype(BF)
        send(buf.at[jp1, c], rp.at[2], r.sum_s.at[n, 3], r.sum_r.at[n, 3], p1)

    def sum_fin(buf, rc, rp, n):
        got(rp.at[1], r.sum_r.at[n, 2])
        got(rp.at[2], r.sum_r.at[n, 3])
        total = buf[jme, c].astype(F32) + rp[1].astype(F32) + rp[2].astype(F32)
        sent(rc, r.sum_s.at[n, 0])
        for k in range(1, 4):
            sent(rp.at[0], r.sum_s.at[n, k])
        return total

    barrier = pltpu.get_barrier_semaphore()
    peers = (core, xp, diag, yp, z0p, z1p, zip_)
    for dev in peers:
        pl.semaphore_signal(barrier, inc=1, device_id=dev, device_id_type=MESH)

    def stage_copies():
        out = []
        for m in range(4):
            for zz in range(2):
                for h in range(2):
                    for k in range(2):
                        zt = z0 + zz * (1 - 2 * z0)
                        col = pl.multiple_of(
                            h * 2048 + 1024 * k + 512 * zt + 256 * c + 128 * x, 128
                        )
                        if m < 3:
                            src = r.e_in.at[m, :, pl.ds(col, 128)]
                        else:
                            src = r.s_in.at[:, pl.ds(col, 128)]
                        at = (h * 2 + k) * 128
                        q = 2 * m + zz
                        dst = r.acc.at[q // 2, q % 2, pl.ds(0, 96), pl.ds(at, 128)]
                        out.append((src, dst, r.stage_sem.at[m, zz * 4 + h * 2 + k]))
            row = pl.multiple_of(128 * x, 128)
            if m < 3:
                src = r.e_out.at[m, pl.ds(row, 128), :]
            else:
                src = r.s_out.at[pl.ds(row, 128), :]
            dst = r.acc.at[m // 2, m % 2, pl.ds(96, 128), pl.ds(0, D)]
            out.append((src, dst, r.stage_sem.at[m, 8]))
        return [pltpu.make_async_copy(*one) for one in out]

    staged = stage_copies()
    for one in staged:
        one.start()

    q_slot = lambda zz, yy: r.wq.at[zz, yy]
    q_ss = lambda n: r.att_s.at[0, n]
    q_rs = lambda n: r.att_r.at[0, n]
    o_slot = lambda zz, yy: r.ow.at[zz, yy, c]
    o_ss = lambda n: r.att_s.at[1, n]
    o_rs = lambda n: r.att_r.at[1, n]
    m_slot = lambda zz, yy: r.misc.at[zz, yy]
    m_ss = lambda n: r.att_s.at[2, n]
    m_rs = lambda n: r.att_r.at[2, n]

    def w_slot(m):
        return lambda zz, yy: r.win.at[m, zz, yy]

    def w_ss(m):
        return lambda n: r.w_s.at[m, n]

    def w_rs(m):
        return lambda n: r.w_r.at[m, n]

    r.wq[z, y] = r.wq_in[...]
    r.misc[z, y] = r.misc_in[...]
    r.ow[z, y, c] = r.ow_in[...]
    r.nall[s] = r.x_in[...]
    r.cota[jme, c] = r.cot_in[...]
    r.nta[jme, c, :, D : D + 128] = r.sel_in[...]

    pl.semaphore_wait(barrier, len(peers))

    send(r.x_in, r.nall.at[s], r.x_s.at[0], r.x_r.at[0], core)
    send(r.x_in, r.nall.at[s], r.x_s.at[1], r.x_r.at[1], xp)
    ow_set = (r.ow_in, o_slot, o_ss, o_rs)
    att_sets = ((r.misc_in, m_slot, m_ss, m_rs), (r.wq_in, q_slot, q_ss, q_rs))
    for src, slot, ss, rs in att_sets:
        ag_first(src, slot, ss, rs)
        ag_own(slot, ss, rs)

    xf = s + 2 - 4 * x
    for src, slot, ss, rs in att_sets:
        ag_z0(slot, ss, rs)
    got(r.nall.at[xf], r.x_r.at[1])
    send(r.nall.at[xf], r.nall.at[xf], r.x_s.at[2], r.x_r.at[2], core)
    def w_first(m):
        ag_first(r.dg.at[m, pl.ds(0, 96)], w_slot(m), w_ss(m), w_rs(m))

    def w_own(m):
        ag_own(w_slot(m), w_ss(m), w_rs(m))

        @pl.when(c == y)
        def _():
            v = r.wout.at[m, z1]
            send(v, v, r.o_s.at[m, 0], r.o_r.at[m, z1], z1p)
            send(v, v, r.o_s.at[m, 1], r.o_r.at[m, z1], yp)

    def w_relay(m):
        ag_z0(w_slot(m), w_ss(m), w_rs(m))

    def w_relay_far(m):
        ag_z1(w_slot(m), w_ss(m), w_rs(m))

        @pl.when(c == y)
        def _():
            v = r.wout.at[m, 1 - z1]
            got(v, r.o_r.at[m, 1 - z1])
            send(v, v, r.o_s.at[m, 2], r.o_r.at[m, 1 - z1], yp)

    def w_fin(m):
        ag_fin(w_slot(m), w_rs(m))

        @pl.when(c != y)
        def _():
            got(r.wout.at[m, 0], r.o_r.at[m, 0])
            got(r.wout.at[m, 1], r.o_r.at[m, 1])

        for n in (1, 2, 4, 5, 6):
            sent(r.win.at[m, z, y], r.w_s.at[m, n])

        @pl.when(inner)
        def _():
            sent(r.win.at[m, z, y], r.w_s.at[m, 3])

        @pl.when(c == y)
        def _():
            for k in range(3):
                sent(r.wout.at[m, 0], r.o_s.at[m, k])

    for one in staged:
        one.wait()
    for m in range(4):
        q = 2 * m
        r.win[m, z, y] = r.acc[q // 2, q % 2, 0:96, 0:512].astype(BF)
        q = 2 * m + 1
        r.dg[m, 0:96, :] = r.acc[q // 2, q % 2, 0:96, 0:512].astype(BF)

    @pl.when(c == y)
    def _():
        for m in range(4):
            r.wout[m, z1] = r.acc[m // 2, m % 2, 96:224, 0:D].astype(BF)

    w_first(0)
    for src, slot, ss, rs in att_sets:
        ag_z1(slot, ss, rs)
    ag_first(*ow_set)
    ag_own(*ow_set[1:])
    tok_own(sel_slot, 2)
    tok_own(cot_slot, 0)
    w_first(1)
    for src, slot, ss, rs in att_sets:
        ag_fin(slot, rs)

    w_own(0)
    w_relay(0)

    rows = jnp.zeros((8, D), F32)
    for k in range(8):
        row_i = lax.broadcasted_iota(jnp.int32, (128, D), 0)
        col_i = lax.broadcasted_iota(jnp.int32, (128, D), 1)
        place = jnp.where((col_i == row_i + 96 * k) & (row_i < 96), 1.0, 0.0).astype(BF)
        rows = rows + nn(r.misc[k // 2, k % 2].astype(BF), place)
    r.mrow[...] = rows
    row8 = lax.broadcasted_iota(jnp.int32, (8, D), 0)
    r.rpad[...] = jnp.zeros((128, D), BF)
    r.rpad[0:16, :] = jnp.concatenate(
        [jnp.where(row8 < 3, rows, 0.0), jnp.zeros((8, D), F32)], axis=0
    ).astype(BF)

    got(r.nall.at[s + 1 - 2 * c], r.x_r.at[0])
    got(r.nall.at[3 - s], r.x_r.at[2])
    for k in range(3):
        sent(r.x_in, r.x_s.at[k])
    wq = r.wq[...].reshape(D, QKV_PAD)
    lane128 = lax.broadcasted_iota(jnp.int32, (TOK, 128), 1)

    def project(t, carry):
        xv = r.nall[t].astype(F32)
        r1 = lax.rsqrt(jnp.mean(xv * xv, axis=-1, keepdims=True) + EPSILON)
        nb = (xv * r1 * r.mrow[3:4, :]).astype(BF)
        r.nall[t] = nb
        pr = nn(nb, r.wq[...].reshape(D, QKV_PAD))
        at = pl.ds(pl.multiple_of(t * TOK, TOK), TOK)
        cosv = r.cos_in[at, :]
        sinv = r.sin_in[at, :]
        for h in range(3):
            hc = 128 * h + 128 * (h // 2)
            g = pr[:, hc : hc + 128]
            g = (g * cosv + swap_halves(g) * sinv).astype(BF).astype(F32)
            g = jnp.where(lane128 < 64, g * 0.125, g)
            r.kq[h, at, :] = pltpu.roll(g, 64, 1).astype(BF)
        r.val[0, at, :] = pr[:, 256:384].astype(BF)
        r.val[1, at, :] = pr[:, 512:640].astype(BF)
        return carry

    lax.fori_loop(0, 4, project, 0)

    ag_z0(*ow_set[1:])
    w_own(1)
    w_relay(1)
    w_first(2)
    ag_z1(*ow_set[1:])
    tok_near(sel_slot, 2)
    tok_near(cot_slot, 0)

    for i in range(3, -1, -1):
        n = (i + 1) * TOK
        base = i * (i + 1) // 2

        def heads(h, carry, i=i, n=n, base=base):
            q = pltpu.roll(r.kq[h, i * TOK : i * TOK + TOK, :].astype(F32), 64, 1)
            q = jnp.where(lane128 < 64, q, 0.0)
            sc = nt(q.astype(BF), r.kq[h, 0:n, :])
            top = jnp.max(sc, axis=-1, keepdims=True)
            e = jnp.exp(sc - top)
            pb = (e * (1.0 / jnp.sum(e, axis=-1, keepdims=True))).astype(BF)
            for j in range(i + 1):
                r.prob[h, base + j] = pb[:, j * TOK : j * TOK + TOK]
            r.acc[h, 0, :, 0:128] = nn(pb, r.val[lax.div(h, 2), 0:n, :])
            return carry

        lax.fori_loop(0, 3, heads, 0)
        r.att[i, :, 0:128] = jnp.where(lane128 < 64, r.acc[0, 0, :, 0:128], r.acc[1, 0, :, 0:128]).astype(BF)
        r.att[i, :, 128:256] = r.acc[2, 0, :, 0:128].astype(BF)

        @pl.when(s != i)
        def _(i=i):
            send(r.att.at[i], r.arow.at[s], r.a_s.at[i], r.a_r.at[s], (b, i))

        @pl.when(s == i)
        def _(i=i):
            r.arow[i] = r.att[i]

        if i == 1:
            ag_fin(o_slot, o_rs)
            send(r.ow.at[:, :, c], r.ow.at[:, :, c], r.ow_s.at[0], r.ow_r.at[0], core)
        if i == 2:
            w_relay_far(0)
            tok_far(sel_slot, 2)
            tok_far(cot_slot, 0)
            w_first(3)
        if i == 0:
            w_relay_far(1)

    got(r.ow.at[:, :, oc], r.ow_r.at[0])
    sent(r.ow.at[:, :, c], r.ow_s.at[0])
    for src, slot, ss, rs in att_sets + (ow_set,):
        ag_sent(src, slot, ss)
    for i in range(4):

        @pl.when(s != i)
        def _(i=i):
            got(r.arow.at[i], r.a_r.at[i])
            sent(r.att.at[i], r.a_s.at[i])

    ow = r.ow[...].reshape(D, D)
    mid = r.x_in[...].astype(F32)
    for i in range(4):
        mid = mid + nn(r.arow[i][:, 0:192], ow[192 * i : 192 * i + 192, :])
    r.mid[...] = mid
    r2 = lax.rsqrt(jnp.mean(mid * mid, axis=-1, keepdims=True) + EPSILON)
    nb = (mid * r2 * r.mrow[4:5, :]).astype(BF)
    r.nta[jme, c, :, 0:D] = nb
    tok_own(two_slot, 1)
    tok_fin(sel_slot, 2)
    tok_fin(cot_slot, 0)

    def gates(nv):
        lg = nt(nv, r.rpad[...])
        lg = jnp.where(lane128 < 3, lg, -1e30)
        e = jnp.exp(lg - jnp.max(lg, axis=-1, keepdims=True))
        return e / jnp.sum(e, axis=-1, keepdims=True)

    def route(j, k):
        sel = r.nta[j, k, :, D : D + 128].astype(F32)
        pv = gates(r.nta[j, k, :, 0:D])
        gv = jnp.where(lane128 < 3, pv * sel, jnp.where(lane128 == 3, sel, 0.0))
        r.acc[j, k, :, 0:D] = jnp.zeros((TOK, D), F32)
        r.acc[j, k, :, D : D + 128] = pltpu.roll(gv, 64, 1)

    def rs_first(m):
        send(r.win.at[m, :, oy], r.ry_in.at[m], r.rs_s.at[m, 0], r.rs_r.at[m, 0], yp)

        @pl.when(c != y)
        def _():
            send(r.gout.at[m], r.ry_out.at[m], r.rs_s.at[m, 1], r.rs_r.at[m, 1], yp)

    def out_rows(m, k):
        at = pl.ds(pl.multiple_of(128 * k, 128), 128)
        return r.gs_out.at[at] if m == 3 else r.ge_out.at[m, at]

    def rs_y(m):
        got(r.ry_in.at[m], r.rs_r.at[m, 0])
        for zz in range(4):
            r.win[m, zz, y] = (r.win[m, zz, y].astype(F32) + r.ry_in[m, zz].astype(F32)).astype(BF)
        send(
            r.win.at[m, pl.ds(2 - 2 * z1, 2), y], r.rz_in.at[m], r.rs_s.at[m, 2], r.rs_r.at[m, 2], z1p
        )

        @pl.when(c == y)
        def _():
            got(r.ry_out.at[m], r.rs_r.at[m, 1])
            for k in range(2):
                r.gout[m, k] = (r.gout[m, k].astype(F32) + r.ry_out[m, k].astype(F32)).astype(BF)
            send(r.gout.at[m, 1 - z1], r.rz_out.at[m], r.rs_s.at[m, 3], r.rs_r.at[m, 3], z1p)

    def rs_z(m):
        got(r.rz_in.at[m], r.rs_r.at[m, 2])
        for k in range(2):
            zz = 2 * z1 + k
            r.win[m, zz, y] = (r.win[m, zz, y].astype(F32) + r.rz_in[m, k].astype(F32)).astype(BF)
        send(r.win.at[m, zf, y], r.rzz.at[m], r.rs_s.at[m, 4], r.rs_r.at[m, 4], z0p)

        @pl.when(c == y)
        def _():
            got(r.rz_out.at[m], r.rs_r.at[m, 3])
            v = (r.gout[m, z1].astype(F32) + r.rz_out[m].astype(F32)).astype(BF)
            r.gout[m, z1] = v
            g = r.gout.at[m, z1]
            pltpu.make_async_copy(g, out_rows(m, x), r.loc.at[m, 1]).start()
            send(g, out_rows(m, x), r.rs_s.at[m, 5], r.rs_r.at[m, 5], xp)
            send(g, out_rows(m, x), r.rs_s.at[m, 6], r.rs_r.at[m, 6], core)

    def part(m, sx, sc):
        return r.ga.at[2 * m + sx, pl.ds(0, 192), pl.ds(pl.multiple_of(512 * sc, 512), 512)]

    def rs_join(m):
        got(r.rzz.at[m], r.rs_r.at[m, 4])
        cols = pl.ds(pl.multiple_of(512 * c, 512), 512)
        mine = pl.ds(pl.multiple_of(96 * z0, 96), 96)
        theirs = pl.ds(pl.multiple_of(96 - 96 * z0, 96), 96)
        r.ga[2 * m + x, mine, cols] = r.win[m, z, y]
        r.ga[2 * m + x, theirs, cols] = r.rzz[m]
        g = part(m, x, c)
        send(g, g, r.rs_s.at[m, 7], r.rs_r.at[m, 7], xp)
        send(g, g, r.rs_s.at[m, 8], r.rs_r.at[m, 8], core)

    def rs_spread(m):
        g = part(m, 1 - x, c)
        got(g, r.rs_r.at[m, 7])
        send(g, g, r.rs_s.at[m, 9], r.rs_r.at[m, 9], core)

        @pl.when(c == y)
        def _():
            v = out_rows(m, 1 - x)
            got(v, r.rs_r.at[m, 5])
            send(v, v, r.rs_s.at[m, 10], r.rs_r.at[m, 10], core)

    def rs_end(m):
        got(part(m, x, oc), r.rs_r.at[m, 8])
        got(part(m, 1 - x, oc), r.rs_r.at[m, 9])
        for k in range(8):
            h, kz, zz = k // 4, k // 2 % 2, k % 2
            for q in range(4):
                sc, sx = q // 2, q % 2
                at = 512 * sc + 128 * (2 * h + kz)
                v = r.ga[2 * m + sx, 96 * zz : 96 * zz + 96, at : at + 128]
                if h == 0:
                    r.ry_in[m, k, :, 128 * q : 128 * q + 128] = v
                else:
                    row = 96 * (k % 2)
                    r.dg[2 * m + kz, row : row + 96, 128 * q : 128 * q + 128] = v
            src = r.ry_in.at[m, k] if h == 0 else r.dg.at[2 * m + kz, pl.ds(96 * (k % 2), 96)]
            dst = r.gs_in if m == 3 else r.ge_in.at[m]
            pltpu.make_async_copy(src, dst.at[:, pl.ds(512 * k, 512)], r.fin.at[m, k]).start()
        sent(r.ry_in.at[m], r.rs_s.at[m, 0])
        sent(r.rz_in.at[m], r.rs_s.at[m, 2])
        sent(r.win.at[m, zf, y], r.rs_s.at[m, 4])
        for k in (7, 8, 9):
            sent(part(m, x, c), r.rs_s.at[m, k])

        @pl.when(c != y)
        def _():
            sent(r.gout.at[m], r.rs_s.at[m, 1])
            got(out_rows(m, x), r.rs_r.at[m, 6])
            got(out_rows(m, 1 - x), r.rs_r.at[m, 10])

        @pl.when(c == y)
        def _():
            g = r.gout.at[m, z1]
            pltpu.make_async_copy(g, out_rows(m, x), r.loc.at[m, 1]).wait()
            for k in (3, 5, 6, 10):
                sent(g, r.rs_s.at[m, k])

    def rs_done(m):
        for k in range(8):
            dst = r.gs_in if m == 3 else r.ge_in.at[m]
            piece = dst.at[:, pl.ds(512 * k, 512)]
            pltpu.make_async_copy(piece, piece, r.fin.at[m, k]).wait()

    def tokens(m, j, k):
        g = 2 * j + k
        w = r.win[m].reshape(D, 512)
        wo = r.wout[m].reshape(256, D)
        gu = nn(r.nta[j, k, :, 0:D], w)
        zv = gu[:, 0:256]
        uv = gu[:, 256:512]
        sg = 1.0 / (1.0 + jnp.exp(-zv))
        sw = zv * sg
        act = (sw * uv).astype(BF).astype(F32)
        dr = nt(r.cota[j, k], wo)
        side = r.acc[j, k, :, D : D + 128]
        gv = jnp.sum(jnp.where(lane128 == m + 64, side, 0.0), axis=-1, keepdims=True)
        gg = jnp.sum(act * dr, axis=-1, keepdims=True)
        r.ga[g, :, pl.ds(pl.multiple_of(m * 256, 256), 256)] = (act * gv).astype(BF)
        d = dr * gv
        dg = jnp.concatenate([d * uv * (sg * (1.0 + zv * (1.0 - sg))), d * sw], axis=1).astype(BF)
        r.dg[g] = dg
        r.acc[j, k, :, 0:D] += nt(dg, w)
        r.acc[j, k, :, D : D + 128] = side + jnp.where(lane128 == m, gg, 0.0)

    def weight_grads(m):
        nta = r.nta[:, :, :, 0:D].reshape(2048, D)
        r.win[m] = tn(nta, r.dg[...].reshape(2048, 512)).astype(BF).reshape(4, 2, 96, 512)
        gam = r.ga[:, :, pl.ds(pl.multiple_of(m * 256, 256), 256)].reshape(2048, 256)
        r.gout[m] = tn(gam, r.cota[...].reshape(2048, D)).astype(BF).reshape(2, 128, D)
        rs_first(m)

    def pack(j, k):
        r.ngb[j, k, :, 0:D] = r.acc[j, k, :, 0:D].astype(BF)
        v = jnp.where(lane128 < 64, r.acc[j, k, :, D : D + 128], 0.0)
        hi = v.astype(BF).astype(F32)
        r.ngb[j, k, :, D : D + 128] = (hi + pltpu.roll(v - hi, 64, 1)).astype(BF)

    w_fin(0)
    for m in range(4):
        sent(r.dg.at[m, pl.ds(0, 96)], r.w_s.at[m, 0])

        @pl.when(inner)
        def _(m=m):
            sent(r.dg.at[m, pl.ds(0, 96)], r.w_s.at[m, 7])


    def arrive(p, carry):
        q = lax.div(p, 2)
        k2 = lax.rem(p, 2)
        j = block_at(q)
        k = c + k2 * (1 - 2 * c)

        @pl.when(p == 2)
        def _():
            tok_near(two_slot, 1)
            w_own(2)
            w_relay(2)
            w_own(3)
            w_relay(3)

        @pl.when(k2 == 1)
        def _():
            got(two_slot(j, k), r.tok_r.at[1, p])

        @pl.when(p == 5)
        def _():
            tok_far(two_slot, 1)

        route(j, k)
        tokens(0, j, k)
        return carry

    lax.fori_loop(0, 8, arrive, 0)
    w_relay_far(2)
    weight_grads(0)
    tok_sent(two_slot, 1)
    tok_sent(sel_slot, 2)
    tok_sent(cot_slot, 0)

    def feed(m, carry):
        w_fin(m)

        def each(p, inner):
            k2 = lax.div(p, 4)
            k = oc + k2 * (2 * c - 1)
            j = block_at(3 - lax.rem(p, 4))
            tokens(m, j, k)

            @pl.when((m == 1) & (p == FAR3))
            def _():
                w_relay_far(3)

            @pl.when((m == 2) & (p == RSY0))
            def _():
                rs_y(0)

            @pl.when(m == 3)
            def _():
                pack(j, k)

            @pl.when((m == 3) & (p == 3))
            def _():
                sum_first(r.ngb, r.ng_c, 0)

            return inner

        lax.fori_loop(0, 8, each, 0)

        @pl.when(m == 3)
        def _():
            sum_core(r.ngb, r.ng_c, r.ng_p, 0)

        weight_grads(m)
        return carry

    lax.fori_loop(1, 4, feed, 0)

    def mix(g, carry):
        j = lax.div(g, 2)
        k = lax.rem(g, 2)
        r.cota[j, k] = nn(r.ga[g], r.wout[...].reshape(1024, D)).astype(BF)
        return carry

    lax.fori_loop(0, 4, mix, 0)
    sum_relay(r.ngb, r.ng_p, 0)
    rs_y(1)
    rs_z(0)
    lax.fori_loop(4, 8, mix, 0)
    rs_y(2)
    out_c = r.ng_c.at[:, :, pl.ds(0, D)]
    out_p = r.ng_p.at[:, :, pl.ds(0, D)]
    ngs = sum_fin(r.ngb, r.ng_c, r.ng_p, 0)
    rs_z(1)

    small_dev = (core, xp, yp, z1p, z0p)

    def small_send(k):
        r.small_o[k] = r.small[...]
        send(r.small_o.at[k], r.small_i.at[k], r.sm_s.at[k], r.sm_r.at[k], small_dev[k])

    def small_add(k):
        got(r.small_i.at[k], r.sm_r.at[k])
        r.small[...] += r.small_i[k]
        sent(r.small_o.at[k], r.sm_s.at[k])
        if k < 4:
            small_send(k + 1)

    upstream = r.cot_in[...].astype(F32)
    mid = r.mid[...]
    r2 = lax.rsqrt(jnp.mean(mid * mid, axis=-1, keepdims=True) + EPSILON)
    gg = ngs[:, D : D + 128]
    gg = gg + pltpu.roll(gg, 64, 1)
    nown = r.nta[jme, c, :, 0:D]
    pv = gates(nown)
    pg = jnp.where(lane128 < 3, gg * r.sel_in[...].astype(F32), 0.0)
    lg = (pv * (pg - jnp.sum(pv * pg, axis=-1, keepdims=True))).astype(BF)
    rgrad = tn(lg, nown)
    ng = ngs[:, 0:D] + nn(lg, r.rpad[...])
    gain2 = r.mrow[4:5, :]
    fgain = jnp.sum(ng * mid * r2, axis=0, keepdims=True)
    sc = ng * gain2
    mg = upstream + r2 * sc - mid * (r2 * r2 * r2) * jnp.mean(sc * mid, axis=-1, keepdims=True)
    r.igrad[...] = mg
    r.small[...] = jnp.where(row8 < 3, rgrad[0:8, :], 0.0) + jnp.where(row8 == 4, fgain, 0.0)
    ml = mg.astype(BF)
    ow = r.ow[...].reshape(D, D)
    r.att[:, :, 128:256] = jnp.zeros((4, TOK, 128), BF)
    for i in range(4):
        da = nt(ml, ow[192 * i : 192 * i + 192, :]).astype(BF)
        r.att[i, :, 0:192] = da

        @pl.when(s != i)
        def _(i=i):
            send(r.att.at[i], r.dat.at[s], r.d_s.at[i], r.d_r.at[s], (b, i))

        @pl.when(s == i)
        def _(i=i):
            r.dat[i] = r.att[i]

    small_send(0)
    for i in range(4):
        og = tn(r.arow[i][:, 0:192], ml).astype(BF)
        og = og.reshape(2, 2, 48, D)
        for k in range(2):
            r.og[k, i] = og[:, :, :, 384 * k : 384 * k + 384]
    send(r.og.at[oc], r.og_c, r.og_s.at[0], r.og_r.at[0], core)
    for i in range(4):
        r.acc[i, 0, :, 0:QKV_PAD] = jnp.zeros((TOK, QKV_PAD), F32)
        r.acc[i, 1, :, 0:D] = jnp.zeros((TOK, D), F32)
    small_add(0)
    rs_y(3)
    for i in range(4):

        @pl.when(s != i)
        def _(i=i):
            got(r.dat.at[i], r.d_r.at[i])
            sent(r.att.at[i], r.d_s.at[i])

    rs_join(0)
    sum_first(r.cota, out_c, 1)

    chunks = ((0, 128), (128, 256), (384, 256))

    def q_first(n):
        at = pl.ds(chunks[n][0], chunks[n][1])
        send(r.wq.at[:, oy, :, at], r.q_y.at[:, :, at], r.q_s.at[n, 0], r.q_r.at[n, 0], yp)

    def q_add_y(n):
        a, e = chunks[n][0], chunks[n][0] + chunks[n][1]
        at = pl.ds(a, e - a)
        got(r.q_y.at[:, :, at], r.q_r.at[n, 0])
        for k in range(4):
            v = r.wq[k, y, :, a:e].astype(F32) + r.q_y[k, :, a:e].astype(F32)
            r.wq[k, y, :, a:e] = v.astype(BF)
        send(
            r.wq.at[pl.ds(2 - 2 * z1, 2), y, :, at],
            r.q_z.at[:, :, at],
            r.q_s.at[n, 1],
            r.q_r.at[n, 1],
            z1p,
        )

    def q_add_z(n):
        a, e = chunks[n][0], chunks[n][0] + chunks[n][1]
        at = pl.ds(a, e - a)
        got(r.q_z.at[:, :, at], r.q_r.at[n, 1])
        for k in range(2):
            v = r.wq[2 * z1 + k, y, :, a:e].astype(F32) + r.q_z[k, :, a:e].astype(F32)
            r.wq[2 * z1 + k, y, :, a:e] = v.astype(BF)
        send(r.wq.at[zf, y, :, at], r.q_w.at[:, at], r.q_s.at[n, 2], r.q_r.at[n, 2], z0p)

    def head_ends(a, w):
        at = pl.ds(a, w)
        for i in range(4):
            for k in range(0, w, 128):
                g = r.acc[i, 0, :, a + k : a + k + 128].astype(BF)
                if a + k in (0, 128, 384):
                    g = g.astype(F32)
                    cosv = r.cos_in[i * TOK : i * TOK + TOK, :]
                    sinv = r.sin_in[i * TOK : i * TOK + TOK, :]
                    g = (g * cosv - swap_halves(g) * sinv).astype(BF)
                r.nta[i, 0, :, a + k : a + k + 128] = g
        wc = r.wq[:, :, :, a : a + w].reshape(D, w)
        for i in range(4):
            r.acc[i, 1, :, 0:D] += nt(r.nta[i, 0, :, a : a + w], wc)
        pg = r.nta[:, 0, :, a : a + w].reshape(1024, w)
        wg = tn(r.nall[...].reshape(1024, D), pg)
        r.wq[:, :, :, a : a + w] = wg.astype(BF).reshape(4, 2, 96, w)

    def og_core():
        got(r.og_c, r.og_r.at[0])
        for k in range(4):
            r.og[c, k] = (r.og[c, k].astype(F32) + r.og_c[k].astype(F32)).astype(BF)
        send(r.og.at[c, :, :, 1 - x], r.og_x, r.og_s.at[1], r.og_r.at[1], xp)

    def og_xp():
        got(r.og_x, r.og_r.at[1])
        for k in range(4):
            r.og[c, k, :, x] = (r.og[c, k, :, x].astype(F32) + r.og_x[k].astype(F32)).astype(BF)
        send(r.og.at[c, :, oy, x], r.og_y, r.og_s.at[2], r.og_r.at[2], yp)

    def og_yp():
        got(r.og_y, r.og_r.at[2])
        for k in range(4):
            r.og[c, k, y, x] = (r.og[c, k, y, x].astype(F32) + r.og_y[k].astype(F32)).astype(BF)
        send(r.og.at[c, pl.ds(2 - 2 * z1, 2), y, x], r.og_z, r.og_s.at[3], r.og_r.at[3], z1p)

    def og_z1p():
        got(r.og_z, r.og_r.at[3])
        for k in range(2):
            v = r.og[c, 2 * z1 + k, y, x].astype(F32) + r.og_z[k].astype(F32)
            r.og[c, 2 * z1 + k, y, x] = v.astype(BF)
        send(r.og.at[c, zf, y, x], r.og_w, r.og_s.at[4], r.og_r.at[4], z0p)

    def og_z0p():
        got(r.og_w, r.og_r.at[4])
        r.og[c, z, y, x] = (r.og[c, z, y, x].astype(F32) + r.og_w[...].astype(F32)).astype(BF)
        ogf = r.og.at[c, z, y, x]
        r.g_ow[s] = r.og[c, z, y, x]
        send(ogf, r.g_ow.at[s], r.og_s.at[6], r.og_r.at[6], xp)
        send(ogf, r.g_ow.at[s], r.og_s.at[5], r.og_r.at[5], core)

    def heads_back(h, carry):
        hv = lax.div(h, 2)
        here = lax.div(lane128, 64) == lax.rem(h, 2)
        vat = pl.ds(pl.multiple_of(hv * 128, 128), 128)
        cat = pl.ds(pl.multiple_of(256 + hv * 256, 128), 128)
        hat = pl.ds(pl.multiple_of(h * 128 + hv * 128, 128), 128)
        for i in range(3, -1, -1):
            base = i * (i + 1) // 2
            da = jnp.where(here, r.dat[i, :, vat].astype(F32), 0.0).astype(BF)
            kqi = r.kq[h, i * TOK : i * TOK + TOK, :].astype(F32)
            qi = jnp.where(lane128 >= 64, kqi, 0.0).astype(BF)
            pf = [r.prob[h, base + j] for j in range(i + 1)]
            dp = [nt(da, r.val[hv, j * TOK : j * TOK + TOK, :]) for j in range(i + 1)]
            cen = jnp.zeros((TOK, 1), F32)
            for j in range(i + 1):
                cen = cen + jnp.sum(pf[j].astype(F32) * dp[j], axis=-1, keepdims=True)
            dq = jnp.zeros((TOK, 128), F32)
            for j in range(i + 1):
                ds = (pf[j].astype(F32) * (dp[j] - cen)).astype(BF)
                dq = dq + nn(ds, r.kq[h, j * TOK : j * TOK + TOK, :])
                r.acc[j, 0, :, hat] += tn(ds, qi)
                r.acc[j, 0, :, cat] += tn(pf[j], da)
            r.acc[i, 0, :, hat] += jnp.where(lane128 < 64, dq * 0.125, 0.0)

        @pl.when(h == 0)
        def _():
            head_ends(*chunks[0])
            q_first(0)
            og_core()
            rs_join(1)
            sum_core(r.cota, out_c, out_p, 1)
            rs_z(2)
            small_add(1)

        @pl.when(h == 1)
        def _():
            head_ends(*chunks[1])
            q_first(1)
            og_xp()
            sum_relay(r.cota, out_p, 1)
            q_add_y(0)
            rs_join(2)
            rs_spread(0)
            rs_spread(1)
            small_add(2)

        @pl.when(h == 2)
        def _():
            head_ends(*chunks[2])
            q_first(2)

        return carry

    lax.fori_loop(0, 3, heads_back, 0)

    n_slot = lambda i: r.nta.at[i, 1, :, pl.ds(0, D)]
    for i in range(4):
        r.nta[i, 1, :, 0:D] = r.acc[i, 1, :, 0:D].astype(BF)
    for k in range(2):
        send(n_slot(2 * k + oc), r.n_c.at[k], r.n_s.at[k], r.n_r.at[k], core)
    og_yp()
    q_add_y(1)
    for k in range(2):
        got(r.n_c.at[k], r.n_r.at[k])
        v = r.nta[2 * k + c, 1, :, 0:D].astype(F32) + r.n_c[k].astype(F32)
        r.nta[2 * k + c, 1, :, 0:D] = v.astype(BF)
    send(n_slot(2 - 2 * x + c), r.n_x, r.n_s.at[2], r.n_r.at[2], xp)
    q_add_z(0)
    rs_z(3)
    rs_end(0)
    small_add(3)
    q_add_y(2)
    og_z1p()
    q_add_z(1)
    rs_join(3)
    rs_spread(2)
    tot = sum_fin(r.cota, out_c, out_p, 1)
    r.out[...] = (r.mid[...] + tot).astype(BF)
    rs_end(1)
    small_add(4)
    r.g_small[...] = r.small[...]
    og_z0p()

    got(r.n_x, r.n_r.at[2])
    for k in range(3):
        sent(r.n_x, r.n_s.at[k])
    ng = r.nta[s, 1, :, 0:D].astype(F32) + r.n_x[...].astype(F32)
    xv = r.x_in[...].astype(F32)
    r1 = lax.rsqrt(jnp.mean(xv * xv, axis=-1, keepdims=True) + EPSILON)
    sc = ng * r.mrow[3:4, :]
    r.igrad[...] = (
        r.igrad[...] + r1 * sc - xv * (r1 * r1 * r1) * jnp.mean(sc * xv, axis=-1, keepdims=True)
    )
    q_add_z(2)
    rs_spread(3)
    rs_end(2)
    got(r.g_ow.at[xf], r.og_r.at[6])
    send(r.g_ow.at[xf], r.g_ow.at[xf], r.og_s.at[7], r.og_r.at[7], core)

    for n in range(3):
        got(r.q_w.at[:, pl.ds(*chunks[n])], r.q_r.at[n, 2])
    qf = r.wq[z, y].astype(F32) + r.q_w[...].astype(F32)
    qf = jnp.concatenate([qf, jnp.zeros((32, QKV_PAD), F32)], axis=0)
    qt = jnp.transpose(qf).astype(BF)
    for k, at in enumerate((0, 64, 256, 128, 192, 320, 384, 448, 512)):
        r.g_q[s, 64 * k : 64 * k + 64, :] = qt[at : at + 64, :]
    g = r.g_q.at[s]
    send(g, g, r.qg_s.at[0], r.qg_r.at[0], xp)
    send(g, g, r.qg_s.at[1], r.qg_r.at[1], core)
    rs_end(3)
    got(r.g_q.at[xf], r.qg_r.at[0])
    send(r.g_q.at[xf], r.g_q.at[xf], r.qg_s.at[2], r.qg_r.at[2], core)
    got(r.g_ow.at[s + 1 - 2 * c], r.og_r.at[5])
    got(r.g_ow.at[3 - s], r.og_r.at[7])
    for n in range(3):
        at = pl.ds(*chunks[n])
        sent(r.q_y.at[:, :, at], r.q_s.at[n, 0])
        sent(r.q_z.at[:, :, at], r.q_s.at[n, 1])
        sent(r.q_w.at[:, at], r.q_s.at[n, 2])
    sent(r.og_c, r.og_s.at[0])
    sent(r.og_x, r.og_s.at[1])
    sent(r.og_y, r.og_s.at[2])
    sent(r.og_z, r.og_s.at[3])
    sent(r.og_w, r.og_s.at[4])
    for k in (5, 6, 7):
        sent(r.g_ow.at[0], r.og_s.at[k])
    for m in range(4):
        rs_done(m)
    got(r.g_q.at[s + 1 - 2 * c], r.qg_r.at[1])
    got(r.g_q.at[3 - s], r.qg_r.at[2])
    for k in range(3):
        sent(g, r.qg_s.at[k])


def vmem(shape, kind=BF):
    return pltpu.VMEM(shape, kind)


def layer_call(ins, cos_table, sin_table):
    dma = pltpu.SemaphoreType.DMA
    in_names = (
        ["x_in", "cot_in", "wq_in", "misc_in", "ow_in", "sel_in", "cos_in", "sin_in"]
        + ["e_in", "e_out", "s_in", "s_out"]
    )
    out_names = ["out", "igrad", "g_small", "g_q", "g_ow"]
    out_names += ["ge_in", "gs_in", "ge_out", "gs_out"]
    out_shapes = (
        ((TOK, D), BF),
        ((TOK, D), F32),
        ((8, D), F32),
        ((4, 576, 128), BF),
        ((4, 48, 384), BF),
        ((3, 96, 4096), BF),
        ((96, 4096), BF),
        ((3, 256, D), BF),
        ((256, D), BF),
    )
    scratch = {
        "nall": vmem((4, TOK, D)),
        "wq": vmem((4, 2, 96, QKV_PAD)),
        "misc": vmem((4, 2, 8, 128), F32),
        "ow": vmem((4, 2, 2, 48, D)),
        "kq": vmem((3, 1024, 128)),
        "val": vmem((2, 1024, 128)),
        "prob": vmem((3, 10, TOK, TOK)),
        "att": vmem((4, TOK, 256)),
        "arow": vmem((4, TOK, 256)),
        "dat": vmem((4, TOK, 256)),
        "mid": vmem((TOK, D), F32),
        "mrow": vmem((8, D), F32),
        "rpad": vmem((128, D)),
        "nta": vmem((4, 2, TOK, D + 128)),
        "cota": vmem((4, 2, TOK, D)),
        "win": vmem((4, 4, 2, 96, 512)),
        "wout": vmem((4, 2, 128, D)),
        "dg": vmem((8, TOK, 512)),
        "ga": vmem((8, TOK, 1024)),
        "acc": vmem((4, 2, TOK, D + 128), F32),
        "gout": vmem((4, 2, 128, D)),
        "ry_in": vmem((4, 4, 96, 512)),
        "ry_out": vmem((4, 2, 128, D)),
        "rzz": vmem((4, 96, 512)),
        "rz_in": vmem((4, 2, 96, 512)),
        "rz_out": vmem((4, 128, D)),
        "ng_c": vmem((4, TOK, D + 128)),
        "ng_p": vmem((3, TOK, D + 128)),
        "ngb": vmem((4, 2, TOK, D + 128)),
        "n_c": vmem((2, TOK, D)),
        "n_x": vmem((TOK, D)),
        "og": vmem((2, 4, 2, 2, 48, 384)),
        "og_c": vmem((4, 2, 2, 48, 384)),
        "og_x": vmem((4, 2, 48, 384)),
        "og_y": vmem((4, 48, 384)),
        "og_z": vmem((2, 48, 384)),
        "og_w": vmem((48, 384)),
        "q_y": vmem((4, 96, QKV_PAD)),
        "q_z": vmem((2, 96, QKV_PAD)),
        "q_w": vmem((96, QKV_PAD)),
        "small": vmem((8, D), F32),
        "small_o": vmem((5, 8, D), F32),
        "small_i": vmem((5, 8, D), F32),
        "stage_sem": dma((4, 9)),
        "att_s": dma((3, 8)),
        "att_r": dma((3, 8)),
        "w_s": dma((4, 8)),
        "w_r": dma((4, 8)),
        "o_s": dma((4, 3)),
        "o_r": dma((4, 2)),
        "ow_s": dma((1,)),
        "ow_r": dma((1,)),
        "x_s": dma((3,)),
        "x_r": dma((3,)),
        "tok_s": dma((3, 7)),
        "tok_r": dma((3, 8)),
        "a_s": dma((4,)),
        "a_r": dma((4,)),
        "d_s": dma((4,)),
        "d_r": dma((4,)),
        "sum_s": dma((2, 4)),
        "sum_r": dma((2, 4)),
        "rs_s": dma((4, 11)),
        "rs_r": dma((4, 11)),
        "loc": dma((4, 2)),
        "og_s": dma((8,)),
        "og_r": dma((8,)),
        "q_s": dma((3, 3)),
        "q_r": dma((3, 3)),
        "qg_s": dma((3,)),
        "qg_r": dma((3,)),
        "fin": dma((4, 8)),
        "n_s": dma((3,)),
        "n_r": dma((3,)),
        "sm_s": dma((5,)),
        "sm_r": dma((5,)),
    }
    names = in_names + out_names + list(scratch)
    in_vmem = pl.BlockSpec(memory_space=pltpu.VMEM)
    in_any = pl.BlockSpec(memory_space=pl.ANY)
    return pl.pallas_call(
        functools.partial(layer_kernel, names),
        out_shape=[jax.ShapeDtypeStruct(*one) for one in out_shapes],
        in_specs=[in_vmem] * 8 + [in_any] * 4,
        out_specs=[in_vmem] * 5 + [in_any] * 4,
        scratch_shapes=list(scratch.values()),
        compiler_params=pltpu.CompilerParams(
            collective_id=0, has_side_effects=True, vmem_limit_bytes=VMEM_LIMIT
        ),
        cost_estimate=pl.CostEstimate(
            flops=35_000_000_000, bytes_accessed=60_000_000, transcendentals=6_000_000
        ),
        name="layer",
    )(*ins[:6], cos_table, sin_table, *ins[6:])


def fast_device(
    inputs,
    attn_gain,
    qkv_weight,
    out_weight,
    ffn_gain,
    router_weight,
    expert_in,
    expert_out,
    shared_in,
    shared_out,
    routes,
    slot_index,
    cotangent,
):
    b = lax.axis_index("dp")
    s = lax.axis_index("seq")
    c = s % 2
    mine = lax.dynamic_slice_in_dim(qkv_weight, 3 * s, 3, axis=1).astype(BF)
    pairs = mine[:, :, 0:2].reshape(96, 3, 128)
    values = mine[:, :, 2].reshape(96, 192)
    wq = jnp.concatenate(
        [
            pairs[:, 0],
            pairs[:, 1],
            values[:, 0:128],
            pairs[:, 2],
            values[:, 128:192],
            jnp.zeros((96, 64), BF),
        ],
        axis=1,
    )
    misc = jnp.concatenate(
        [router_weight.T, attn_gain[None], ffn_gain[None], jnp.zeros((3, 96), F32)], axis=0
    )
    misc = jnp.pad(misc.astype(BF).astype(F32), ((0, 0), (0, 32)))
    half = lax.dynamic_slice_in_dim(out_weight, 48 * c, 48, axis=0).astype(BF)
    lane = jnp.arange(128, dtype=jnp.int32)
    route = routes[0]
    sel = (lane == route[:, 0:1]) | (lane == route[:, 1:2]) | (lane == 3)
    sel = sel.astype(BF)
    angle = np.arange(1024, dtype=np.float32)[:, None] * (
        np.float32(10000.0) ** (-np.arange(32, dtype=np.float32) / np.float32(32))
    )
    cos_table = jnp.asarray(np.tile(np.cos(angle), (1, 4)).astype(np.float32))
    sine = np.sin(angle)
    sin_table = jnp.asarray(np.tile(np.concatenate([-sine, sine], 1), (1, 2)).astype(np.float32))
    out, igrad, small, g_q, g_ow, ge_in, gs_in, ge_out, gs_out = layer_call(
        (
            inputs[0],
            cotangent[0],
            wq,
            misc,
            half,
            sel,
            expert_in,
            expert_out,
            shared_in,
            shared_out,
        ),
        cos_table,
        sin_table,
    )
    shard = lax.dynamic_slice_in_dim(small, 96 * b, 96, axis=1)
    qkv_grad = g_q.reshape(HEADS, 3, HEAD_DIM, 128)[..., 0:96].transpose(3, 0, 1, 2).astype(F32)
    gain_grad = jnp.sum(qkv_weight.astype(BF).astype(F32) * qkv_grad, axis=(1, 2, 3))
    gain_grad = gain_grad / attn_gain.astype(BF).astype(F32)
    ow_grad = g_ow.reshape(2, 2, 48, 384).transpose(0, 2, 1, 3).reshape(96, D).astype(F32)
    return (
        out[None],
        igrad[None],
        gain_grad,
        qkv_grad,
        ow_grad,
        shard[4],
        shard[0:3].T,
        ge_in.astype(F32),
        ge_out.astype(F32),
        gs_in.astype(F32),
        gs_out.astype(F32),
    )


def solution(mesh):
    fits = mesh.shape["dp"] == 8 and mesh.shape["seq"] == 4
    return jax.shard_map(
        fast_device if fits else on_device,
        mesh=mesh,
        in_specs=(
            P("dp", "seq", None),
            P("dp"),
            P("dp", None, None, None),
            P("dp", None),
            P("dp"),
            P("dp", None),
            P(None, "dp", None),
            P(None, "dp", None),
            P("dp", None),
            P("dp", None),
            P("dp", "seq", None),
            P("dp", "seq", None),
            P("dp", "seq", None),
        ),
        out_specs=(
            P("dp", "seq", None),
            P("dp", "seq", None),
            P("dp"),
            P("dp", None, None, None),
            P("dp", None),
            P("dp"),
            P("dp", None),
            P(None, "dp", None),
            P(None, "dp", None),
            P("dp", None),
            P("dp", None),
        ),
        check_vma=False,
    )
```
